32 devices in a mesh: ens: 2 (over x), face: 16 (over z, y, core).
Axes of the slice: x: 2, y: 2, z: 4, core: 2. Of those that a mesh axis runs over, the one named last changes fastest.
Arguments:
- tracer_adjoint: float32 [2, 50, 128, 2048], P(None, None, 'face', 'ens'), parts along dimension 3, may hold values from -6 to 6
- eta_adjoint: float32 [128, 2048], P('face', 'ens'), parts along dimension 1, may hold values from -18 to 18
- velocity_x: float32 [50, 128, 2048], P(None, 'face', 'ens'), parts along dimension 2, may hold values from -3 to 3
- velocity_y: float32 [50, 128, 2048], P(None, 'face', 'ens'), parts along dimension 2, may hold values from -3 to 3
- mixing: float32 [49, 128, 2048], P(None, 'face', 'ens'), parts along dimension 2, may hold values from 0.05 to 5
- thickness: float32 [50], replicated, may hold values from 0.5 to 4
- surface_damping: float32 [128, 1024], P('face'), may hold values from 0.01 to 0.2
- wet_levels: int32 [128, 1024], P('face'), may hold values from 0 to 50
- seam_codes: int32 [16], P('face'), may hold values from 0 to 1
Outputs:
- tracer_start_adjoint: float32 [2, 50, 128, 2048], P(None, None, 'face', 'ens'), parts along dimension 3
- surface_adjoint: float32 [128, 2048], P('face', 'ens'), parts along dimension 1
The draws below stay inside these ranges and needn't reach their ends.
There are 2 independent parts, one for each index of `ens`. The reference program is written for one: setup_inputs(seed, part) draws one part's arguments, and reference() takes and returns one part's arrays. A program takes and returns all parts, laid end to end along the dimension named above; an argument that names none is the same for every part. Nothing has to cross between parts.
All inputs are finite; a program needn't handle non-finite values.
Results may differ from the reference program's by a relative error of at most 0.00017.
Values sent between devices are 32-bit elements; how exact they have to be, the bound alone decides.
No kernel may reach another device: no remote copies, remote signals or barrier semaphores. Data moves between devices by JAX's collectives and lax.ppermute only.
A program may use at most 128 MiB of HBM per device.

```python
import math
import jax
import jax.numpy as jnp

NT = 2
K = 50
ITERS = 4
CY = 8
NX = 1024
NY = 128
N_FACE = 16


def draw_eta_adjoint(key, part):
    key = jax.random.fold_in(key, 11)
    ramp = 1.0 + 2.0 * jnp.arange(NY, dtype=jnp.float32) / (NY - 1)
    values_in = jnp.clip(jax.random.normal(key, (NY, NX), jnp.float32), -6.0, 6.0)
    return values_in * ramp[:, None]


def set_ends(drawn, own_key, least, top_value):
    shape = drawn.shape
    place = [jax.random.randint(jax.random.fold_in(own_key, axis), (), 0, shape[axis]) for axis in range(len(shape))]
    drawn = drawn.at[tuple(place)].set(least)
    longest = shape.index(max(shape))
    place[longest] = (place[longest] + 1) % shape[longest]
    return drawn.at[tuple(place)].set(top_value)


def block_levels(own_key, dims, split, smallest, top_value):
    level, own = 1.0, jax.random.fold_in(own_key, 6)
    for dim, blocks in split:
        heights = jnp.exp(jax.random.uniform(jax.random.fold_in(own, dim), (blocks,), jnp.float32, smallest / len(split), top_value / len(split)))
        level = level * jnp.repeat(heights, dims[dim] // blocks).reshape([-1 if axis == dim else 1 for axis in range(len(dims))])
    return level


def normal_values(rng, extent, deviation, bound, cuts=(), kind=jnp.bfloat16):
    factor_of = block_levels(rng, extent, cuts, -0.22, 0.18) if cuts else 1.0
    array = jax.random.normal(rng, extent, jnp.float32) * deviation * factor_of
    return jnp.minimum(jnp.maximum(array, -bound), bound).astype(kind)


def setup_inputs(seed: int = 0, part: int = 0) -> dict:
    arg_keys = jax.random.split(jax.random.key(seed), 10)
    own_keys = jax.random.split(jax.random.fold_in(arg_keys[9], part), 10)
    tracer_adjoint = normal_values(own_keys[0], (NT, K, NY, NX), 1.0, 6.0, ((2, 16),), jnp.float32)
    eta_adjoint = draw_eta_adjoint(jax.random.fold_in(jax.random.fold_in(arg_keys[9], part), 71), part)
    velocity_x = normal_values(own_keys[2], (K, NY, NX), 0.5, 3.0, ((1, 16),), jnp.float32)
    velocity_y = normal_values(own_keys[3], (K, NY, NX), 0.5, 3.0, ((1, 16),), jnp.float32)
    mixing = jnp.clip(jnp.exp(math.log(5.0) - 4.6051702 * jax.random.uniform(own_keys[4], (K - 1, NY, NX), jnp.float32) ** block_levels(own_keys[4], (K - 1, NY, NX), ((1, 16),), -0.2, 0.2)), 0.05, 5.0)
    thickness = jnp.clip(jnp.exp(jax.random.uniform(arg_keys[5], (K,), jnp.float32, math.log(0.5), math.log(4.0))), 0.5, 4.0)
    surface_damping = jnp.clip(jnp.exp(math.log(0.2) - 2.9957323 * jax.random.uniform(arg_keys[6], (NY, NX), jnp.float32) ** block_levels(arg_keys[6], (NY, NX), ((0, 16),), -0.2, 0.2)), 0.01, 0.2)
    wet_levels = set_ends(jax.random.randint(arg_keys[7], (NY, NX), 0, K + 1), jax.random.fold_in(arg_keys[7], 1), 0, K).astype(jnp.int32)
    seam_codes = set_ends(jax.random.randint(arg_keys[8], (N_FACE,), 0, 2), jax.random.fold_in(arg_keys[8], 1), 0, 1).astype(jnp.int32)
    return {"tracer_adjoint": tracer_adjoint, "eta_adjoint": eta_adjoint, "velocity_x": velocity_x, "velocity_y": velocity_y, "mixing": mixing, "thickness": thickness, "surface_damping": surface_damping, "wet_levels": wet_levels, "seam_codes": seam_codes}


diffusion = 0.1
advection = 0.5


def seam_neighbours(values_in, seam_codes):
    starts = jnp.arange(N_FACE, dtype=jnp.int32) * CY
    finals = starts + CY - 1
    southern = jnp.roll(values_in, 1, axis=-2)
    northern = jnp.roll(values_in, -1, axis=-2)
    below_rows = values_in[..., jnp.roll(finals, 1), :]
    turned_below = (jnp.roll(seam_codes, 1) == 1)[:, None]
    below_rows = jnp.where(turned_below, jnp.flip(below_rows, -1), below_rows)
    southern = southern.at[..., starts, :].set(below_rows)
    above_rows = values_in[..., jnp.roll(starts, -1), :]
    turned_above = (seam_codes == 1)[:, None]
    above_rows = jnp.where(turned_above, jnp.flip(above_rows, -1), above_rows)
    northern = northern.at[..., finals, :].set(above_rows)
    return southern, northern


def surface_apply(values_in, damping, seam_codes):
    southern, northern = seam_neighbours(values_in, seam_codes)
    return (4.0 + damping) * values_in - (southern + northern + jnp.roll(values_in, 1, -1) + jnp.roll(values_in, -1, -1))


def transposed_solve(right_side, coupling, thickness):
    ratios = []
    scaled = []
    for level in range(K):
        inward = jnp.zeros_like(coupling[0])
        if level > 0:
            inward = inward + coupling[level - 1]
        if level < K - 1:
            inward = inward + coupling[level]
        pivots = 1.0 + inward / thickness[level]
        numer_term = right_side[:, level]
        if level > 0:
            below_term = -coupling[level - 1] / thickness[level - 1]
            pivots = pivots - below_term * ratios[level - 1]
            numer_term = numer_term - below_term * scaled[level - 1]
        if level < K - 1:
            ratios.append((-coupling[level] / thickness[level + 1]) / pivots)
        scaled.append(numer_term / pivots)
    solved = [scaled[K - 1]]
    for level in range(K - 2, -1, -1):
        solved.insert(0, scaled[level] - ratios[level] * solved[0])
    return jnp.stack(solved, axis=1)


def reference(tracer_adjoint, eta_adjoint, velocity_x, velocity_y, mixing, thickness, surface_damping, wet_levels, seam_codes):
    surface = jnp.zeros_like(eta_adjoint)
    residual = eta_adjoint
    direction = eta_adjoint
    norm_now = jnp.sum(residual * residual)
    for step in range(ITERS):
        applied = surface_apply(direction, surface_damping, seam_codes)
        step_size = norm_now / jnp.sum(direction * applied)
        surface = surface + step_size * direction
        residual = residual - step_size * applied
        norm_next = jnp.sum(residual * residual)
        direction = residual + (norm_next / norm_now) * direction
        norm_now = norm_next
    wet_mask = (jnp.arange(K, dtype=jnp.int32)[:, None, None] < wet_levels[None]).astype(jnp.float32)
    coupling = mixing * wet_mask[1:]
    first_tracer = tracer_adjoint[0] + thickness[:, None, None] * wet_mask * surface[None]
    loaded = jnp.concatenate([first_tracer[None], tracer_adjoint[1:]], axis=0)
    carried = transposed_solve(loaded, coupling, thickness)
    xflux = velocity_x[None] * carried
    yflux = velocity_y[None] * carried
    southern, northern = seam_neighbours(carried, seam_codes)
    yflux_south, yflux_north = seam_neighbours(yflux, seam_codes)
    eastern = jnp.roll(carried, -1, -1)
    western = jnp.roll(carried, 1, -1)
    spread = eastern + western + northern + southern - 4.0 * carried
    moved = (jnp.roll(xflux, -1, -1) - jnp.roll(xflux, 1, -1)) * advection + (yflux_north - yflux_south) * advection
    result = wet_mask * (carried + diffusion * spread + moved)
    return result, surface
```

```python
import functools
import jax
import jax.numpy as jnp
from jax import lax
from jax.experimental import pallas as pl
from jax.experimental.pallas import tpu as pltpu
from jax.sharding import PartitionSpec as P

ITERS = 4
LANES = 128
SUBLANES = 8
diffusion = 0.1
advection = 0.5

MIDDLE = 4.1
LOSS = 1000.0

SMEM = pl.BlockSpec(memory_space=pltpu.SMEM)
VMEM = pl.BlockSpec(memory_space=pltpu.VMEM)
PARAMS = pltpu.CompilerParams(vmem_limit_bytes=56 * 2**20)


def with_halo(x, sides, width):
    for axis, dim in sides:
        count, length = (lax.axis_size(axis), x.shape[dim])
        up = [(i, (i + 1) % count) for i in range(count)]
        down = [(j, i) for i, j in up]
        last = lax.slice_in_dim(x, length - width, length, axis=dim)
        initial = lax.slice_in_dim(x, 0, width, axis=dim)
        before = lax.ppermute(last, axis, up)
        after = lax.ppermute(initial, axis, down)
        x = jnp.concatenate([before, x, after], axis=dim)
    return x


def raised(block_rows, turned):
    upper_row = block_rows[..., -1:, :]
    upper_row = jnp.where(turned, jnp.flip(upper_row, -1), upper_row)
    return jnp.concatenate([block_rows[..., :-1, :], upper_row], axis=-2)


def settled(block_rows, padded, turned):
    lower_rim = padded[..., :1, :]
    upper_rim = padded[..., -1:, :]
    upper_rim = jnp.where(turned, jnp.flip(upper_rim, -1), upper_rim)
    southern = jnp.concatenate([lower_rim, block_rows[..., :-1, :]], axis=-2)
    northern = jnp.concatenate([block_rows[..., 1:, :], upper_rim], axis=-2)
    return (southern, northern)


def surface_apply(values_in, damping, turned):
    padded = with_halo(raised(values_in, turned), (("face", 0),), 1)
    southern, northern = settled(values_in, padded, turned)
    return (4.0 + damping) * values_in - (
        southern + northern + jnp.roll(values_in, 1, -1) + jnp.roll(values_in, -1, -1)
    )


def stepwise_surface(eta_adjoint, surface_damping, turned):
    surface = jnp.zeros_like(eta_adjoint)
    residual = eta_adjoint
    direction = eta_adjoint
    norm_now = lax.psum(jnp.sum(residual * residual), "face")
    for step in range(ITERS):
        applied = surface_apply(direction, surface_damping, turned)
        step_size = norm_now / lax.psum(jnp.sum(direction * applied), "face")
        surface = surface + step_size * direction
        residual = residual - step_size * applied
        norm_next = lax.psum(jnp.sum(residual * residual), "face")
        direction = residual + norm_next / norm_now * direction
        norm_now = norm_next
    return surface


def flip_lanes(rows):
    width = rows.shape[1]
    back = LANES - 1 - lax.broadcasted_iota(jnp.int32, (SUBLANES, LANES), 1)
    tiles = []
    for start in range(width - LANES, -1, -LANES):
        tiles.append(
            jnp.take_along_axis(
                rows[:, start : start + LANES], back, axis=1, mode="promise_in_bounds"
            )
        )
    return jnp.concatenate(tiles, axis=1)


def flip_rows_in_place(ref):
    def body(i, _):
        at = pl.ds(pl.multiple_of(i * SUBLANES, SUBLANES), SUBLANES)
        ref[at, :] = flip_lanes(ref[at, :])
        return 0

    lax.fori_loop(0, ref.shape[0] // SUBLANES, body, 0)


def outer_kernel(seam, eta, damping, up, down):
    half = SUBLANES // 2
    down[:half, :] = eta[:half, :]
    down[half:, :] = damping[:half, :]
    up[:half, :] = eta[half:, :]
    up[half:, :] = damping[half:, :]

    @pl.when(seam[0] == 1)
    def _():
        up[...] = flip_lanes(up[...])


def basis_kernel(seam, eta, damping, below, above, basis, sums):
    half = SUBLANES // 2
    rows = 2 * SUBLANES
    beyond = above[...]
    beyond = jnp.where(seam[0] == 1, flip_lanes(beyond), beyond)
    width = beyond.shape[1]
    v = jnp.concatenate([below[:half, :], eta[...], beyond[:half, :]], axis=0)
    d = jnp.concatenate([below[half:, :], damping[...], beyond[half:, :]], axis=0)
    d = (d + (4.0 - MIDDLE)) * (1.0 / MIDDLE)
    vectors = [v]
    for j in range(ITERS):
        now = vectors[-1]
        near = (
            pltpu.roll(now, 1, 0)
            + pltpu.roll(now, rows - 1, 0)
            + pltpu.roll(now, 1, 1)
            + pltpu.roll(now, width - 1, 1)
        )
        image = d * now - near * (1.0 / MIDDLE)
        vectors.append(image if j == 0 else 2.0 * image - vectors[-2])
    for j in range(ITERS):
        basis[j] = vectors[j]
    row = lax.broadcasted_iota(jnp.int32, (rows, LANES), 0)
    own = (row >= half) & (row < half + SUBLANES)
    for j in range(2 * ITERS):
        product = vectors[j // 2] * vectors[j // 2 + j % 2]
        total = product[:, :LANES]
        for start in range(LANES, width, LANES):
            total = total + product[:, start : start + LANES]
        sums[j : j + 1, :] = jnp.sum(jnp.where(own, total, 0.0), axis=0, keepdims=True)


def coefficients(moments):
    def dot(a, b):
        total = None
        for i, x in enumerate(a):
            for j, y in enumerate(b):
                term = x * y * (moments[i + j] + moments[abs(i - j)])
                total = term if total is None else total + term
        return 0.5 * total

    def image(p):
        q = [MIDDLE * x for x in p] + [jnp.zeros_like(p[0])]
        for i, x in enumerate(p):
            if i == 0:
                q[1] = q[1] + MIDDLE * x
            else:
                q[i + 1] = q[i + 1] + (0.5 * MIDDLE) * x
                q[i - 1] = q[i - 1] + (0.5 * MIDDLE) * x
        return q

    def size(p):
        return functools.reduce(lambda a, b: a + b, [jnp.abs(x) for x in p])

    def plus(a, b):
        return [x + y for x, y in zip(a, b)] + list(a[len(b) :]) + list(b[len(a) :])

    norm_first = moments[0]
    p = [jnp.ones_like(norm_first)]
    r = p
    norm_now = norm_first
    s = []
    sound = norm_first > 0.0
    for step in range(ITERS):
        q = image(p)
        curve = dot(p, q)
        sound = sound & (curve * LOSS >= size(p) * size(q) * norm_first)
        rate = norm_now / curve
        s = plus(s, [rate * x for x in p])
        if step < ITERS - 1:
            r = plus(r, [-rate * x for x in q])
            norm_next = dot(r, r)
            sound = sound & (norm_next * LOSS >= size(r) * size(r) * norm_first)
            ratio = norm_next / norm_now
            p = plus(r, [ratio * x for x in p])
            norm_now = norm_next
    return s, sound


def surface_kernel(sums, basis, surface, rims, sound):
    half = SUBLANES // 2
    sets = sums.shape[0]
    total = sums[0]
    for i in range(1, sets):
        total = total + sums[i]
    total = jnp.sum(total, axis=1, keepdims=True)
    raw = [total[j : j + 1, :] for j in range(2 * ITERS)]
    moments = raw[:2]
    for j in range(2, 2 * ITERS):
        moments.append(2.0 * raw[j] - raw[j % 2])
    s, good = coefficients(moments)
    value = s[0] * basis[0]
    for j in range(1, ITERS):
        value = value + s[j] * basis[j]
    surface[...] = value[half : half + SUBLANES, :]
    rims[0:1, :] = value[half - 1 : half, :]
    rims[1:2, :] = value[half + SUBLANES : half + SUBLANES + 1, :]
    sound[...] = jnp.broadcast_to(jnp.where(good, 1, 0), sound.shape)


def column_kernel(
    seam, thickness, tracer, mixing, velocity_y, wet, solved, up, down, ratio_at
):
    levels = tracer.shape[1]
    depth = wet[...]
    zero = jnp.zeros(depth.shape, jnp.float32)

    def forward(k, carry):
        c_before, g_before, y0, y1, y2 = carry
        th = thickness[k]
        c = jnp.where(k + 1 < depth, mixing[jnp.minimum(k, levels - 2)], 0.0)
        inverse = 1.0 / (th + c + c_before * (1.0 - g_before))
        g = c * inverse
        y0 = (tracer[0, k] + c_before * y0) * inverse
        y1 = (tracer[1, k] + c_before * y1) * inverse
        y2 = (jnp.where(k < depth, th, 0.0) + c_before * y2) * inverse
        ratio_at[k] = g
        solved[0, k] = y0
        solved[1, k] = y1
        solved[2, k] = y2
        return c, g, y0, y1, y2

    lax.fori_loop(0, levels, forward, (zero,) * 5, unroll=2)

    def backward(i, carry):
        k = levels - 1 - i
        th = thickness[k]
        g = ratio_at[k]
        flow = advection * velocity_y[k]
        upward = diffusion - flow
        downward = diffusion + flow
        after = []
        for t in range(3):
            u = solved[t, k] + g * carry[t]
            x = th * u
            solved[t, k] = x
            up[pl.ds(t * levels + k, 1), :] = (x * upward)[SUBLANES - 1 :, :]
            down[pl.ds(t * levels + k, 1), :] = (x * downward)[:1, :]
            after.append(u)
        return tuple(after)

    lax.fori_loop(0, levels, backward, (zero,) * 3, unroll=2)

    @pl.when(seam[0] == 1)
    def _():
        flip_rows_in_place(up)


def transport_kernel(
    seam, solved, velocity_x, velocity_y, wet, surface, rims, below, above, result, beyond
):
    levels_here = velocity_x.shape[0]
    levels = levels_here * pl.num_programs(0)
    first = pl.program_id(0) * levels_here
    width = wet.shape[1]

    @pl.when(pl.program_id(0) == 0)
    def _():
        beyond[...] = above[...]

        @pl.when(seam[0] == 1)
        def _():
            flip_rows_in_place(beyond)

    depth = wet[...]
    s = surface[...]
    south_s = rims[0:1, :]
    north_s = rims[1:2, :]
    row = lax.broadcasted_iota(jnp.int32, depth.shape, 0)

    def level(i, _):
        k = first + i
        flow_x = advection * velocity_x[i]
        flow_y = advection * velocity_y[i]
        is_wet = k < depth
        for t in range(2):
            x = solved[t, i]
            from_south = below[pl.ds(t * levels + k, 1), :]
            from_north = beyond[pl.ds(t * levels + k, 1), :]
            if t == 0:
                x = x + s * solved[2, i]
                from_south = from_south + south_s * below[pl.ds(2 * levels + k, 1), :]
                from_north = from_north + north_s * beyond[pl.ds(2 * levels + k, 1), :]
            spread = diffusion * x
            push_x = flow_x * x
            push_y = flow_y * x
            eastern = pltpu.roll(spread + push_x, width - 1, 1)
            western = pltpu.roll(spread - push_x, 1, 1)
            northern = jnp.where(
                row == SUBLANES - 1, from_north, pltpu.roll(spread + push_y, SUBLANES - 1, 0)
            )
            southern = jnp.where(row == 0, from_south, pltpu.roll(spread - push_y, 1, 0))
            value = (1.0 - 4.0 * diffusion) * x + ((eastern + western) + (northern + southern))
            result[t, i] = jnp.where(is_wet, value, 0.0)
        return 0

    lax.fori_loop(0, levels_here, level, 0, unroll=True)


def gathered_sums(sums, axis):
    count = lax.axis_size(axis)
    if count & (count - 1):
        return lax.psum(sums, axis)[None]
    stride = 1
    parts = [sums]
    while stride < count:
        total = parts[0] if len(parts) == 1 else (parts[0] + parts[2]) + (parts[1] + parts[3])
        reach = min(4, count // stride)
        parts = [total]
        for step in range(1, reach):
            pairs = []
            for i in range(count):
                place = i // stride % reach
                pairs.append((i, i + ((place + step) % reach - place) * stride))
            parts.append(lax.ppermute(total, axis, pairs))
        stride *= reach
    return jnp.stack(parts)


def shards(
    tracer_adjoint,
    eta_adjoint,
    velocity_x,
    velocity_y,
    mixing,
    thickness,
    surface_damping,
    wet_levels,
    seam_codes,
):
    tracers, levels, rows, width = tracer_adjoint.shape
    f32 = jnp.float32
    count = lax.axis_size("face")
    upward = [(i, (i + 1) % count) for i in range(count)]
    downward = [(j, i) for i, j in upward]
    tile = jax.ShapeDtypeStruct((rows, width), f32)
    ext = jax.ShapeDtypeStruct((ITERS, 2 * rows, width), f32)
    lines = -(-3 * levels // SUBLANES) * SUBLANES
    line = jax.ShapeDtypeStruct((lines, width), f32)

    up, down = pl.pallas_call(
        outer_kernel,
        out_shape=(tile, tile),
        in_specs=[SMEM, VMEM, VMEM],
        out_specs=(VMEM, VMEM),
        name="outer_rows",
    )(seam_codes, eta_adjoint, surface_damping)
    below = lax.ppermute(up, "face", upward)
    above = lax.ppermute(down, "face", downward)

    basis, sums = pl.pallas_call(
        basis_kernel,
        out_shape=(ext, jax.ShapeDtypeStruct((SUBLANES, LANES), f32)),
        in_specs=[SMEM] + [VMEM] * 4,
        out_specs=(VMEM, VMEM),
        compiler_params=PARAMS,
        name="surface_basis",
    )(seam_codes, eta_adjoint, surface_damping, below, above)
    parts = gathered_sums(sums, "face")

    solved, up, down = pl.pallas_call(
        column_kernel,
        out_shape=(jax.ShapeDtypeStruct((3, levels, rows, width), f32), line, line),
        in_specs=[SMEM, SMEM] + [VMEM] * 4,
        out_specs=(VMEM, VMEM, VMEM),
        scratch_shapes=[pltpu.VMEM((levels, rows, width), f32)],
        compiler_params=PARAMS,
        cost_estimate=pl.CostEstimate(flops=40000000, bytes_accessed=13000000, transcendentals=0),
        name="columns",
    )(seam_codes, thickness, tracer_adjoint, mixing, velocity_y, wet_levels)
    below = lax.ppermute(up, "face", upward)
    above = lax.ppermute(down, "face", downward)

    surface, rims, sound = pl.pallas_call(
        surface_kernel,
        out_shape=(tile, tile, jax.ShapeDtypeStruct((SUBLANES, LANES), jnp.int32)),
        in_specs=[VMEM, VMEM],
        out_specs=(VMEM, VMEM, VMEM),
        compiler_params=PARAMS,
        name="surface",
    )(parts, basis)

    def transport(surface, rims, solved, below, above):
        chunk = 5 if levels % 5 == 0 else 1
        whole = pl.BlockSpec((rows, width), lambda k: (0, 0))
        many = pl.BlockSpec((lines, width), lambda k: (0, 0))
        field = pl.BlockSpec((chunk, rows, width), lambda k: (k, 0, 0))
        return pl.pallas_call(
            transport_kernel,
            out_shape=jax.ShapeDtypeStruct((tracers, levels, rows, width), f32),
            grid=(levels // chunk,),
            in_specs=[
                SMEM,
                pl.BlockSpec((3, chunk, rows, width), lambda k: (0, k, 0, 0)),
                field,
                field,
                whole,
                whole,
                whole,
                many,
                many,
            ],
            out_specs=pl.BlockSpec((tracers, chunk, rows, width), lambda k: (0, k, 0, 0)),
            scratch_shapes=[pltpu.VMEM((lines, width), f32)],
            compiler_params=PARAMS,
            name="transport",
        )(seam_codes, solved, velocity_x, velocity_y, wet_levels, surface, rims, below, above)

    def by_moments(surface, rims, solved, below, above):
        return transport(surface, rims, solved, below, above), surface

    def by_steps(surface, rims, solved, below, above):
        surface = stepwise_surface(eta_adjoint, surface_damping, seam_codes[0] == 1)
        top, bottom = surface[-1:], surface[:1]
        top = jnp.where(seam_codes[0] == 1, jnp.flip(top, -1), top)
        south = lax.ppermute(top, "face", upward)
        north = lax.ppermute(bottom, "face", downward)
        north = jnp.where(seam_codes[0] == 1, jnp.flip(north, -1), north)
        rims = jnp.concatenate([south, north, surface[2:]], axis=0)
        return transport(surface, rims, solved, below, above), surface

    return lax.cond(
        sound[0, 0] == 1, by_moments, by_steps, surface, rims, solved, below, above
    )


def solution(mesh):
    placed = (
        P(None, None, "face", "ens"),
        P("face", "ens"),
        P(None, "face", "ens"),
        P(None, "face", "ens"),
        P(None, "face", "ens"),
        P(),
        P("face", None),
        P("face", None),
        P("face"),
    )
    return jax.shard_map(
        shards,
        mesh=mesh,
        in_specs=placed,
        out_specs=(P(None, None, "face", "ens"), P("face", "ens")),
        check_vma=False,
    )
```

```python
import jax
import jax.numpy as jnp
from jax import lax
from jax.experimental import pallas as pl
from jax.experimental.pallas import tpu as pltpu
from jax.sharding import PartitionSpec as P

ITERS = 4
LANES = 128
SUBLANES = 8
diffusion = 0.1
advection = 0.5

SMEM = pl.BlockSpec(memory_space=pltpu.SMEM)
VMEM = pl.BlockSpec(memory_space=pltpu.VMEM)
PARAMS = pltpu.CompilerParams(vmem_limit_bytes=56 * 2**20)


def flip_lanes(rows):
    height, width = rows.shape
    if height > SUBLANES:
        parts = [flip_lanes(rows[i : i + SUBLANES]) for i in range(0, height, SUBLANES)]
        return jnp.concatenate(parts, axis=0)
    back = LANES - 1 - lax.broadcasted_iota(jnp.int32, (SUBLANES, LANES), 1)
    tiles = []
    for start in range(width - LANES, -1, -LANES):
        tiles.append(
            jnp.take_along_axis(
                rows[:, start : start + LANES], back, axis=1, mode="promise_in_bounds"
            )
        )
    return jnp.concatenate(tiles, axis=1)


def flip_rows_in_place(ref):
    def body(i, _):
        at = pl.ds(pl.multiple_of(i * SUBLANES, SUBLANES), SUBLANES)
        ref[at, :] = flip_lanes(ref[at, :])
        return 0

    lax.fori_loop(0, ref.shape[0] // SUBLANES, body, 0)


def pack_kernel(seam, eta, damping, packed):
    rows, width = eta.shape
    packed[:rows, :width] = eta[...]
    packed[rows:, :width] = damping[...]
    code = seam[0].astype(jnp.float32)
    packed[:, width:] = jnp.full((2 * rows, LANES), code, jnp.float32)


def surface_kernel(place, packed, surface, rims, p_at, r_at, q_at, north_at, south_at):
    blocks, double, wide = packed.shape
    rows, width = double // 2, wide - LANES
    me = place[0]
    row = lax.broadcasted_iota(jnp.int32, (rows, width), 0)
    zero = jnp.zeros((rows, width), jnp.float32)
    turned = packed[:, 0, width : width + 1] > 0.5

    def whole(value):
        return jnp.sum(value, axis=(0, 1), keepdims=True)

    def start(b, total):
        value = packed[b, :rows, :width]
        r_at[b] = value
        return total + value * value

    norm_now = whole(lax.fori_loop(0, blocks, start, zero, unroll=2))
    ratio = None
    surface[...] = zero
    rims[...] = zero
    for step in range(ITERS):
        first = r_at[:, 0, :]
        last = r_at[:, rows - 1, :]
        if step:
            first = first + ratio * p_at[:, 0, :]
            last = last + ratio * p_at[:, rows - 1, :]
        after = pltpu.roll(first, blocks - 1, 0)
        north_at[...] = jnp.where(turned, flip_lanes(after), after)
        south_at[...] = pltpu.roll(jnp.where(turned, flip_lanes(last), last), 1, 0)

        def apply(b, total):
            p = r_at[b]
            if step:
                p = p + ratio * p_at[b]
            p_at[b] = p
            northern = jnp.where(
                row == rows - 1, north_at[pl.ds(b, 1), :], pltpu.roll(p, rows - 1, 0)
            )
            southern = jnp.where(row == 0, south_at[pl.ds(b, 1), :], pltpu.roll(p, 1, 0))
            near = (southern + northern) + (pltpu.roll(p, 1, 1) + pltpu.roll(p, width - 1, 1))
            q = (4.0 + packed[b, rows:, :width]) * p - near
            q_at[b] = q
            return total + p * q

        rate = norm_now / whole(lax.fori_loop(0, blocks, apply, zero, unroll=2))
        surface[...] += rate * p_at[me]
        rims[0:1, :] += rate * south_at[pl.ds(me, 1), :]
        rims[1:2, :] += rate * north_at[pl.ds(me, 1), :]
        if step < ITERS - 1:

            def reduce(b, total):
                r = r_at[b] - rate * q_at[b]
                r_at[b] = r
                return total + r * r

            norm_next = whole(lax.fori_loop(0, blocks, reduce, zero, unroll=2))
            ratio = norm_next / norm_now
            norm_now = norm_next


def column_kernel(
    seam, thickness, tracer, mixing, velocity_y, wet, solved, up, down, ratio_at
):
    levels = tracer.shape[1]
    depth = wet[...]
    zero = jnp.zeros(depth.shape, jnp.float32)

    def forward(k, carry):
        c_before, g_before, y0, y1, y2 = carry
        th = thickness[k]
        c = jnp.where(k + 1 < depth, mixing[jnp.minimum(k, levels - 2)], 0.0)
        inverse = 1.0 / (th + c + c_before * (1.0 - g_before))
        g = c * inverse
        y0 = (tracer[0, k] + c_before * y0) * inverse
        y1 = (tracer[1, k] + c_before * y1) * inverse
        y2 = (jnp.where(k < depth, th, 0.0) + c_before * y2) * inverse
        ratio_at[k] = g
        solved[0, k] = y0
        solved[1, k] = y1
        solved[2, k] = y2
        return c, g, y0, y1, y2

    lax.fori_loop(0, levels, forward, (zero,) * 5, unroll=2)

    def backward(i, carry):
        k = levels - 1 - i
        th = thickness[k]
        g = ratio_at[k]
        flow = advection * velocity_y[k]
        upward = diffusion - flow
        downward = diffusion + flow
        after = []
        for t in range(3):
            u = solved[t, k] + g * carry[t]
            x = th * u
            solved[t, k] = x
            up[pl.ds(t * levels + k, 1), :] = (x * upward)[SUBLANES - 1 :, :]
            down[pl.ds(t * levels + k, 1), :] = (x * downward)[:1, :]
            after.append(u)
        return tuple(after)

    lax.fori_loop(0, levels, backward, (zero,) * 3, unroll=2)

    @pl.when(seam[0] == 1)
    def _():
        flip_rows_in_place(up)


def transport_kernel(
    seam, solved, velocity_x, velocity_y, wet, surface, rims, below, above, result, beyond
):
    levels_here = velocity_x.shape[0]
    levels = levels_here * pl.num_programs(0)
    first = pl.program_id(0) * levels_here
    width = wet.shape[1]

    @pl.when(pl.program_id(0) == 0)
    def _():
        beyond[...] = above[...]

        @pl.when(seam[0] == 1)
        def _():
            flip_rows_in_place(beyond)

    depth = wet[...]
    s = surface[...]
    south_s = rims[0:1, :]
    north_s = rims[1:2, :]
    row = lax.broadcasted_iota(jnp.int32, depth.shape, 0)

    def level(i, _):
        k = first + i
        flow_x = advection * velocity_x[i]
        flow_y = advection * velocity_y[i]
        is_wet = k < depth
        for t in range(2):
            x = solved[t, i]
            from_south = below[pl.ds(t * levels + k, 1), :]
            from_north = beyond[pl.ds(t * levels + k, 1), :]
            if t == 0:
                x = x + s * solved[2, i]
                from_south = from_south + south_s * below[pl.ds(2 * levels + k, 1), :]
                from_north = from_north + north_s * beyond[pl.ds(2 * levels + k, 1), :]
            spread = diffusion * x
            push_x = flow_x * x
            push_y = flow_y * x
            eastern = pltpu.roll(spread + push_x, width - 1, 1)
            western = pltpu.roll(spread - push_x, 1, 1)
            northern = jnp.where(
                row == SUBLANES - 1, from_north, pltpu.roll(spread + push_y, SUBLANES - 1, 0)
            )
            southern = jnp.where(row == 0, from_south, pltpu.roll(spread - push_y, 1, 0))
            value = (1.0 - 4.0 * diffusion) * x + ((eastern + western) + (northern + southern))
            result[t, i] = jnp.where(is_wet, value, 0.0)
        return 0

    lax.fori_loop(0, levels_here, level, 0, unroll=True)


def shards(
    tracer_adjoint,
    eta_adjoint,
    velocity_x,
    velocity_y,
    mixing,
    thickness,
    surface_damping,
    wet_levels,
    seam_codes,
):
    tracers, levels, rows, width = tracer_adjoint.shape
    f32 = jnp.float32
    count = lax.axis_size("face")
    upward = [(i, (i + 1) % count) for i in range(count)]
    downward = [(j, i) for i, j in upward]
    tile = jax.ShapeDtypeStruct((rows, width), f32)
    lines = -(-3 * levels // SUBLANES) * SUBLANES
    line = jax.ShapeDtypeStruct((lines, width), f32)

    packed = pl.pallas_call(
        pack_kernel,
        out_shape=jax.ShapeDtypeStruct((2 * rows, width + LANES), f32),
        in_specs=[SMEM, VMEM, VMEM],
        out_specs=VMEM,
        name="pack",
    )(seam_codes, eta_adjoint, surface_damping)
    packed = lax.all_gather(packed, "face")

    solved, up, down = pl.pallas_call(
        column_kernel,
        out_shape=(jax.ShapeDtypeStruct((3, levels, rows, width), f32), line, line),
        in_specs=[SMEM, SMEM] + [VMEM] * 4,
        out_specs=(VMEM, VMEM, VMEM),
        scratch_shapes=[pltpu.VMEM((levels, rows, width), f32)],
        compiler_params=PARAMS,
        cost_estimate=pl.CostEstimate(flops=40000000, bytes_accessed=13000000, transcendentals=0),
        name="columns",
    )(seam_codes, thickness, tracer_adjoint, mixing, velocity_y, wet_levels)
    below = lax.ppermute(up, "face", upward)
    above = lax.ppermute(down, "face", downward)

    fields = pltpu.VMEM((count, rows, width), f32)
    edges = pltpu.VMEM((count, width), f32)
    surface, rims = pl.pallas_call(
        surface_kernel,
        out_shape=(tile, tile),
        in_specs=[SMEM, VMEM],
        out_specs=(VMEM, VMEM),
        scratch_shapes=[fields, fields, fields, edges, edges],
        compiler_params=PARAMS,
        name="surface",
    )(lax.axis_index("face")[None], packed)

    def transport(surface, rims, solved, below, above):
        chunk = 5 if levels % 5 == 0 else 1
        whole = pl.BlockSpec((rows, width), lambda k: (0, 0))
        many = pl.BlockSpec((lines, width), lambda k: (0, 0))
        field = pl.BlockSpec((chunk, rows, width), lambda k: (k, 0, 0))
        return pl.pallas_call(
            transport_kernel,
            out_shape=jax.ShapeDtypeStruct((tracers, levels, rows, width), f32),
            grid=(levels // chunk,),
            in_specs=[
                SMEM,
                pl.BlockSpec((3, chunk, rows, width), lambda k: (0, k, 0, 0)),
                field,
                field,
                whole,
                whole,
                whole,
                many,
                many,
            ],
            out_specs=pl.BlockSpec((tracers, chunk, rows, width), lambda k: (0, k, 0, 0)),
            scratch_shapes=[pltpu.VMEM((lines, width), f32)],
            compiler_params=PARAMS,
            name="transport",
        )(seam_codes, solved, velocity_x, velocity_y, wet_levels, surface, rims, below, above)

    return transport(surface, rims, solved, below, above), surface


def solution(mesh):
    placed = (
        P(None, None, "face", "ens"),
        P("face", "ens"),
        P(None, "face", "ens"),
        P(None, "face", "ens"),
        P(None, "face", "ens"),
        P(),
        P("face", None),
        P("face", None),
        P("face"),
    )
    return jax.shard_map(
        shards,
        mesh=mesh,
        in_specs=placed,
        out_specs=(P(None, None, "face", "ens"), P("face", "ens")),
        check_vma=False,
    )
```

```python
import functools
import jax
import jax.numpy as jnp
from jax import lax
from jax.experimental import pallas as pl
from jax.experimental.pallas import tpu as pltpu
from jax.sharding import PartitionSpec as P

ITERS = 4
LANES = 128
SUBLANES = 8
diffusion = 0.1
advection = 0.5

MIDDLE = 4.1
LOSS = 1000.0

SMEM = pl.BlockSpec(memory_space=pltpu.SMEM)
VMEM = pl.BlockSpec(memory_space=pltpu.VMEM)
HBM = pl.BlockSpec(memory_space=pltpu.HBM)
PARAMS = pltpu.CompilerParams(vmem_limit_bytes=32 * 2**20)


def with_halo(x, sides, width):
    for axis, dim in sides:
        count, length = (lax.axis_size(axis), x.shape[dim])
        up = [(i, (i + 1) % count) for i in range(count)]
        down = [(j, i) for i, j in up]
        last = lax.slice_in_dim(x, length - width, length, axis=dim)
        initial = lax.slice_in_dim(x, 0, width, axis=dim)
        before = lax.ppermute(last, axis, up)
        after = lax.ppermute(initial, axis, down)
        x = jnp.concatenate([before, x, after], axis=dim)
    return x


def raised(block_rows, turned):
    upper_row = block_rows[..., -1:, :]
    upper_row = jnp.where(turned, jnp.flip(upper_row, -1), upper_row)
    return jnp.concatenate([block_rows[..., :-1, :], upper_row], axis=-2)


def settled(block_rows, padded, turned):
    lower_rim = padded[..., :1, :]
    upper_rim = padded[..., -1:, :]
    upper_rim = jnp.where(turned, jnp.flip(upper_rim, -1), upper_rim)
    southern = jnp.concatenate([lower_rim, block_rows[..., :-1, :]], axis=-2)
    northern = jnp.concatenate([block_rows[..., 1:, :], upper_rim], axis=-2)
    return (southern, northern)


def surface_apply(values_in, damping, turned):
    padded = with_halo(raised(values_in, turned), (("face", 0),), 1)
    southern, northern = settled(values_in, padded, turned)
    return (4.0 + damping) * values_in - (
        southern + northern + jnp.roll(values_in, 1, -1) + jnp.roll(values_in, -1, -1)
    )


def stepwise_surface(eta_adjoint, surface_damping, turned):
    surface = jnp.zeros_like(eta_adjoint)
    residual = eta_adjoint
    direction = eta_adjoint
    norm_now = lax.psum(jnp.sum(residual * residual), "face")
    for step in range(ITERS):
        applied = surface_apply(direction, surface_damping, turned)
        step_size = norm_now / lax.psum(jnp.sum(direction * applied), "face")
        surface = surface + step_size * direction
        residual = residual - step_size * applied
        norm_next = lax.psum(jnp.sum(residual * residual), "face")
        direction = residual + norm_next / norm_now * direction
        norm_now = norm_next
    return surface


def flip_lanes(rows):
    width = rows.shape[1]
    back = LANES - 1 - lax.broadcasted_iota(jnp.int32, (SUBLANES, LANES), 1)
    tiles = []
    for start in range(width - LANES, -1, -LANES):
        tiles.append(
            jnp.take_along_axis(
                rows[:, start : start + LANES], back, axis=1, mode="promise_in_bounds"
            )
        )
    return jnp.concatenate(tiles, axis=1)


def chunks_of(levels, size):
    return [(k, min(size, levels - k)) for k in range(0, levels, size)]


def line_of(tracer, level, levels):
    full = levels // SUBLANES
    if level < full * SUBLANES:
        return tracer * full * SUBLANES + level
    return 3 * full * SUBLANES + tracer * (levels % SUBLANES) + level - full * SUBLANES


def flip_some(rows):
    height, width = rows.shape
    if height < SUBLANES:
        rows = jnp.concatenate([rows, jnp.zeros((SUBLANES - height, width), rows.dtype)], axis=0)
    return flip_lanes(rows)[:height]


def outer_kernel(seam, eta, damping, up, down):
    half = SUBLANES // 2
    down[:half, :] = eta[:half, :]
    down[half:, :] = damping[:half, :]
    up[:half, :] = eta[half:, :]
    up[half:, :] = damping[half:, :]

    @pl.when(seam[0] == 1)
    def _():
        up[...] = flip_lanes(up[...])


def basis_kernel(seam, eta, damping, below, above, basis, sums):
    half = SUBLANES // 2
    rows = 2 * SUBLANES
    beyond = above[...]
    beyond = jnp.where(seam[0] == 1, flip_lanes(beyond), beyond)
    width = beyond.shape[1]
    v = jnp.concatenate([below[:half, :], eta[...], beyond[:half, :]], axis=0)
    d = jnp.concatenate([below[half:, :], damping[...], beyond[half:, :]], axis=0)
    d = (d + (4.0 - MIDDLE)) * (1.0 / MIDDLE)
    vectors = [v]
    for j in range(ITERS):
        now = vectors[-1]
        near = (
            pltpu.roll(now, 1, 0)
            + pltpu.roll(now, rows - 1, 0)
            + pltpu.roll(now, 1, 1)
            + pltpu.roll(now, width - 1, 1)
        )
        image = d * now - near * (1.0 / MIDDLE)
        vectors.append(image if j == 0 else 2.0 * image - vectors[-2])
    for j in range(ITERS):
        basis[j] = vectors[j]
    row = lax.broadcasted_iota(jnp.int32, (rows, LANES), 0)
    own = (row >= half) & (row < half + SUBLANES)
    parts = []
    for j in range(2 * ITERS):
        product = vectors[j // 2] * vectors[j // 2 + j % 2]
        total = product[:, :LANES]
        for start in range(LANES, width, LANES):
            total = total + product[:, start : start + LANES]
        parts.append(jnp.sum(jnp.where(own, total, 0.0), axis=0, keepdims=True))
    tile = jnp.concatenate(parts, axis=0)
    for i in range(sums.shape[0]):
        sums[i] = tile


def coefficients(moments):
    def dot(a, b):
        total = None
        for i, x in enumerate(a):
            for j, y in enumerate(b):
                term = x * y * (moments[i + j] + moments[abs(i - j)])
                total = term if total is None else total + term
        return 0.5 * total

    def image(p):
        q = [MIDDLE * x for x in p] + [jnp.zeros_like(p[0])]
        for i, x in enumerate(p):
            if i == 0:
                q[1] = q[1] + MIDDLE * x
            else:
                q[i + 1] = q[i + 1] + (0.5 * MIDDLE) * x
                q[i - 1] = q[i - 1] + (0.5 * MIDDLE) * x
        return q

    def size(p):
        return functools.reduce(lambda a, b: a + b, [jnp.abs(x) for x in p])

    def plus(a, b):
        return [x + y for x, y in zip(a, b)] + list(a[len(b) :]) + list(b[len(a) :])

    norm_first = moments[0]
    p = [jnp.ones_like(norm_first)]
    r = p
    norm_now = norm_first
    s = []
    sound = norm_first > 0.0
    for step in range(ITERS):
        q = image(p)
        curve = dot(p, q)
        sound = sound & (curve * LOSS >= size(p) * size(q) * norm_first)
        rate = norm_now / curve
        s = plus(s, [rate * x for x in p])
        if step < ITERS - 1:
            r = plus(r, [-rate * x for x in q])
            norm_next = dot(r, r)
            sound = sound & (norm_next * LOSS >= size(r) * size(r) * norm_first)
            ratio = norm_next / norm_now
            p = plus(r, [ratio * x for x in p])
            norm_now = norm_next
    return s, sound


def surface_kernel(sums, basis, surface, sound):
    half = SUBLANES // 2
    parts = [sums[i] for i in range(sums.shape[0])]
    while len(parts) > 1:
        pairs = [a + b for a, b in zip(parts[::2], parts[1::2])]
        parts = pairs + parts[len(parts) - len(parts) % 2 :]
    total = jnp.sum(parts[0], axis=1, keepdims=True)
    raw = [total[j : j + 1, :] for j in range(2 * ITERS)]
    moments = raw[:2]
    for j in range(2, 2 * ITERS):
        moments.append(2.0 * raw[j] - raw[j % 2])
    s, good = coefficients(moments)
    value = s[0] * basis[0]
    for j in range(1, ITERS):
        value = value + s[j] * basis[j]
    surface[:SUBLANES, :] = value[half : half + SUBLANES, :]
    surface[SUBLANES : SUBLANES + 1, :] = value[half - 1 : half, :]
    surface[SUBLANES + 1 : SUBLANES + 2, :] = value[half + SUBLANES : half + SUBLANES + 1, :]
    surface[SUBLANES + 2 :, :] = jnp.zeros((SUBLANES - 2, value.shape[1]), value.dtype)
    sound[0] = jnp.where(good, 1, 0)[0, 0]


CHUNK = 10


def column_kernel(
    seam, thickness, tracer, mixing, velocity_y, wet, after, solved, up, down,
    tracer_at, mixing_at, velocity_at, solved_at, ratio_at, sems, out_sems,
):
    levels = tracer.shape[1]
    chunks = chunks_of(levels, CHUNK)
    loads = []
    for i, (k, n) in enumerate(chunks):
        m = min(n, levels - 1 - k)
        loads.append((
            pltpu.make_async_copy(
                tracer.at[:, pl.ds(k, n)], tracer_at.at[:, pl.ds(k, n)], sems.at[0, i]
            ),
            pltpu.make_async_copy(
                mixing.at[pl.ds(k, m)], mixing_at.at[pl.ds(k, m)], sems.at[1, i]
            ),
        ))
    velocity_load = pltpu.make_async_copy(velocity_y, velocity_at, sems.at[2, 0])
    for pair in loads:
        pair[0].start()
        pair[1].start()
    velocity_load.start()

    depth = wet[...]
    zero = jnp.zeros(depth.shape, jnp.float32)

    def forward(k, carry):
        c_before, g_before, y0, y1, y2 = carry
        th = thickness[k]
        c = jnp.where(k + 1 < depth, mixing_at[jnp.minimum(k, levels - 2)], 0.0)
        inverse = 1.0 / (th + c + c_before * (1.0 - g_before))
        g = c * inverse
        y0 = (tracer_at[0, k] + c_before * y0) * inverse
        y1 = (tracer_at[1, k] + c_before * y1) * inverse
        y2 = (jnp.where(k < depth, th, 0.0) + c_before * y2) * inverse
        ratio_at[k] = g
        solved_at[0, k] = y0
        solved_at[1, k] = y1
        solved_at[2, k] = y2
        return c, g, y0, y1, y2

    carry = (zero,) * 5
    for i, (k, n) in enumerate(chunks):
        loads[i][0].wait()
        loads[i][1].wait()
        carry = lax.fori_loop(k, k + n, forward, carry, unroll=2)

    stores = []
    carry = (zero,) * 3
    for i, (k, n) in reversed(list(enumerate(chunks))):

        def backward(j, carry, last=k + n - 1):
            level = last - j
            th = thickness[level]
            g = ratio_at[level]
            after = []
            for t in range(3):
                u = solved_at[t, level] + g * carry[t]
                solved_at[t, level] = th * u
                after.append(u)
            return tuple(after)

        carry = lax.fori_loop(0, n, backward, carry, unroll=2)
        stores.append(
            pltpu.make_async_copy(
                solved_at.at[:, pl.ds(k, n)], solved.at[:, pl.ds(k, n)], out_sems.at[i]
            )
        )
        stores[-1].start()

    velocity_load.wait()
    turned = seam[0] == 1
    for k, n in chunks_of(levels, SUBLANES):
        flow_top = advection * velocity_at[pl.ds(k, n), SUBLANES - 1, :]
        flow_bottom = advection * velocity_at[pl.ds(k, n), 0, :]
        for t in range(3):
            line = line_of(t, k, levels)
            top = solved_at[t, pl.ds(k, n), SUBLANES - 1, :] * (diffusion - flow_top)
            up[line : line + n, :] = jnp.where(turned, flip_some(top), top)
            bottom = solved_at[t, pl.ds(k, n), 0, :] * (diffusion + flow_bottom)
            down[line : line + n, :] = bottom
    for store in stores:
        store.wait()


def transport_kernel(
    seam, solved, velocity_x, velocity_y, wet, fields, below, above, result, surface,
    solved_at, x_at, y_at, result_at, sems, out_sems,
):
    levels = velocity_x.shape[0]
    width = wet.shape[1]
    chunks = chunks_of(levels, SUBLANES)
    loads = []
    for i, (k, n) in enumerate(chunks):
        at = pl.ds(k, n)
        loads.append((
            pltpu.make_async_copy(solved.at[:, at], solved_at.at[:, at], sems.at[0, i]),
            pltpu.make_async_copy(velocity_x.at[at], x_at.at[at], sems.at[1, i]),
            pltpu.make_async_copy(velocity_y.at[at], y_at.at[at], sems.at[2, i]),
        ))
    for group in loads:
        for load in group:
            load.start()

    turned = seam[0] == 1
    depth = wet[...]
    s = fields[:SUBLANES, :]
    surface[...] = s
    south_s = fields[SUBLANES : SUBLANES + 1, :]
    north_s = fields[SUBLANES + 1 : SUBLANES + 2, :]
    depth_south = depth[:1, :]
    depth_north = depth[SUBLANES - 1 :, :]
    row = lax.broadcasted_iota(jnp.int32, depth.shape, 0)
    is_south = row == 0
    is_north = row == SUBLANES - 1

    def level(k, _):
        flow_x = advection * x_at[k]
        flow_y = advection * y_at[k]
        to_west = diffusion + flow_x
        to_east = diffusion - flow_x
        to_south = jnp.where(is_south, 0.0, diffusion + flow_y)
        to_north = jnp.where(is_north, 0.0, diffusion - flow_y)
        is_wet = k < depth
        for t in range(2):
            x = solved_at[t, k]
            if t == 0:
                x = x + s * solved_at[2, k]
            eastern = pltpu.roll(x * to_west, width - 1, 1)
            western = pltpu.roll(x * to_east, 1, 1)
            northern = pltpu.roll(x * to_south, SUBLANES - 1, 0)
            southern = pltpu.roll(x * to_north, 1, 0)
            value = (1.0 - 4.0 * diffusion) * x + ((eastern + western) + (northern + southern))
            result_at[t, k] = jnp.where(is_wet, value, 0.0)
        return 0

    stores = []
    for i, (k, n) in enumerate(chunks):
        for load in loads[i]:
            load.wait()
        lax.fori_loop(k, k + n, level, 0, unroll=2)
        index = k + lax.broadcasted_iota(jnp.int32, (n, width), 0)
        for t in range(2):
            line = line_of(t, k, levels)
            south = below[line : line + n, :]
            north = above[line : line + n, :]
            if t == 0:
                line = line_of(2, k, levels)
                south = south + south_s * below[line : line + n, :]
                beyond = above[line : line + n, :]
                north = jnp.where(turned, flip_some(north), north)
                north = north + north_s * jnp.where(turned, flip_some(beyond), beyond)
            else:
                north = jnp.where(turned, flip_some(north), north)
            at = pl.ds(k, n)
            result_at[t, at, 0, :] += jnp.where(index < depth_south, south, 0.0)
            result_at[t, at, SUBLANES - 1, :] += jnp.where(index < depth_north, north, 0.0)
        stores.append(
            pltpu.make_async_copy(
                result_at.at[:, pl.ds(k, n)], result.at[:, pl.ds(k, n)], out_sems.at[i]
            )
        )
        stores[-1].start()
    for store in stores:
        store.wait()


def shards(
    tracer_adjoint,
    eta_adjoint,
    velocity_x,
    velocity_y,
    mixing,
    thickness,
    surface_damping,
    wet_levels,
    seam_codes,
):
    tracers, levels, rows, width = tracer_adjoint.shape
    f32 = jnp.float32
    count = lax.axis_size("face")
    upward = [(i, (i + 1) % count) for i in range(count)]
    downward = [(j, i) for i, j in upward]
    tile = jax.ShapeDtypeStruct((rows, width), f32)
    ext = jax.ShapeDtypeStruct((ITERS, 2 * rows, width), f32)
    lines = -(-3 * levels // SUBLANES) * SUBLANES
    line = jax.ShapeDtypeStruct((lines, width), f32)

    up, down = pl.pallas_call(
        outer_kernel,
        out_shape=(tile, tile),
        in_specs=[SMEM, VMEM, VMEM],
        out_specs=(VMEM, VMEM),
        name="outer_rows",
    )(seam_codes, eta_adjoint, surface_damping)
    below = lax.ppermute(up, "face", upward)
    above = lax.ppermute(down, "face", downward)

    cube = pltpu.VMEM((levels, rows, width), f32)
    parts = len(chunks_of(levels, CHUNK))
    solved, up, down = pl.pallas_call(
        column_kernel,
        out_shape=(jax.ShapeDtypeStruct((3, levels, rows, width), f32), line, line),
        in_specs=[SMEM, SMEM, HBM, HBM, HBM, VMEM, HBM],
        out_specs=(HBM, VMEM, VMEM),
        scratch_shapes=[
            pltpu.VMEM((tracers, levels, rows, width), f32),
            cube,
            cube,
            pltpu.VMEM((3, levels, rows, width), f32),
            cube,
            pltpu.SemaphoreType.DMA((3, parts)),
            pltpu.SemaphoreType.DMA((parts,)),
        ],
        compiler_params=PARAMS,
        cost_estimate=pl.CostEstimate(flops=40000000, bytes_accessed=13000000, transcendentals=0),
        name="columns",
    )(
        seam_codes,
        thickness,
        *(pltpu.with_memory_space_constraint(x, pltpu.HBM) for x in (tracer_adjoint, mixing, velocity_y)),
        wet_levels,
        up,
    )

    basis, sums = pl.pallas_call(
        basis_kernel,
        out_shape=(ext, jax.ShapeDtypeStruct((count, SUBLANES, LANES), f32)),
        in_specs=[SMEM] + [VMEM] * 4,
        out_specs=(VMEM, VMEM),
        compiler_params=PARAMS,
        name="surface_basis",
    )(seam_codes, eta_adjoint, surface_damping, below, above)
    sums, up, down = lax.optimization_barrier((sums, up, down))
    sums = lax.all_to_all(sums, "face", 0, 0)
    below = lax.ppermute(up, "face", upward)
    above = lax.ppermute(down, "face", downward)

    fields, sound = pl.pallas_call(
        surface_kernel,
        out_shape=(
            jax.ShapeDtypeStruct((2 * rows, width), f32),
            jax.ShapeDtypeStruct((1,), jnp.int32),
        ),
        in_specs=[VMEM, VMEM],
        out_specs=(VMEM, SMEM),
        compiler_params=PARAMS,
        name="surface",
    )(sums, basis)

    def by_moments(fields):
        return fields

    def by_steps(fields):
        turned = seam_codes[0] == 1
        surface = stepwise_surface(eta_adjoint, surface_damping, turned)
        top, bottom = surface[-1:], surface[:1]
        top = jnp.where(turned, jnp.flip(top, -1), top)
        south = lax.ppermute(top, "face", upward)
        north = lax.ppermute(bottom, "face", downward)
        north = jnp.where(turned, jnp.flip(north, -1), north)
        return jnp.concatenate([surface, south, north, fields[rows + 2 :]], axis=0)

    fields = lax.cond(sound[0] == 1, by_moments, by_steps, fields)

    parts = len(chunks_of(levels, SUBLANES))
    return pl.pallas_call(
        transport_kernel,
        out_shape=(jax.ShapeDtypeStruct((tracers, levels, rows, width), f32), tile),
        in_specs=[SMEM, HBM, HBM, HBM] + [VMEM] * 4,
        out_specs=(HBM, VMEM),
        scratch_shapes=[
            pltpu.VMEM((3, levels, rows, width), f32),
            cube,
            cube,
            pltpu.VMEM((tracers, levels, rows, width), f32),
            pltpu.SemaphoreType.DMA((3, parts)),
            pltpu.SemaphoreType.DMA((parts,)),
        ],
        compiler_params=PARAMS,
        name="transport",
    )(seam_codes, solved, velocity_x, velocity_y, wet_levels, fields, below, above)


def solution(mesh):
    placed = (
        P(None, None, "face", "ens"),
        P("face", "ens"),
        P(None, "face", "ens"),
        P(None, "face", "ens"),
        P(None, "face", "ens"),
        P(),
        P("face", None),
        P("face", None),
        P("face"),
    )
    return jax.shard_map(
        shards,
        mesh=mesh,
        in_specs=placed,
        out_specs=(P(None, None, "face", "ens"), P("face", "ens")),
        check_vma=False,
    )
```

```python
import functools
import jax
import jax.numpy as jnp
from jax import lax
from jax.experimental import pallas as pl
from jax.experimental.pallas import tpu as pltpu
from jax.sharding import PartitionSpec as P

ITERS = 4
LANES = 128
SUBLANES = 8
diffusion = 0.1
advection = 0.5

MIDDLE = 4.1
LOSS = 1000.0

SMEM = pl.BlockSpec(memory_space=pltpu.SMEM)
VMEM = pl.BlockSpec(memory_space=pltpu.VMEM)
HBM = pl.BlockSpec(memory_space=pltpu.HBM)
PARAMS = pltpu.CompilerParams(vmem_limit_bytes=32 * 2**20)


def in_hbm(x):
    return pltpu.with_memory_space_constraint(x, pltpu.HBM)


def with_halo(x, sides, width):
    for axis, dim in sides:
        count, length = (lax.axis_size(axis), x.shape[dim])
        up = [(i, (i + 1) % count) for i in range(count)]
        down = [(j, i) for i, j in up]
        last = lax.slice_in_dim(x, length - width, length, axis=dim)
        initial = lax.slice_in_dim(x, 0, width, axis=dim)
        before = lax.ppermute(last, axis, up)
        after = lax.ppermute(initial, axis, down)
        x = jnp.concatenate([before, x, after], axis=dim)
    return x


def raised(block_rows, turned):
    upper_row = block_rows[..., -1:, :]
    upper_row = jnp.where(turned, jnp.flip(upper_row, -1), upper_row)
    return jnp.concatenate([block_rows[..., :-1, :], upper_row], axis=-2)


def settled(block_rows, padded, turned):
    lower_rim = padded[..., :1, :]
    upper_rim = padded[..., -1:, :]
    upper_rim = jnp.where(turned, jnp.flip(upper_rim, -1), upper_rim)
    southern = jnp.concatenate([lower_rim, block_rows[..., :-1, :]], axis=-2)
    northern = jnp.concatenate([block_rows[..., 1:, :], upper_rim], axis=-2)
    return (southern, northern)


def surface_apply(values_in, damping, turned):
    padded = with_halo(raised(values_in, turned), (("face", 0),), 1)
    southern, northern = settled(values_in, padded, turned)
    return (4.0 + damping) * values_in - (
        southern + northern + jnp.roll(values_in, 1, -1) + jnp.roll(values_in, -1, -1)
    )


def stepwise_surface(eta_adjoint, surface_damping, turned):
    surface = jnp.zeros_like(eta_adjoint)
    residual = eta_adjoint
    direction = eta_adjoint
    norm_now = lax.psum(jnp.sum(residual * residual), "face")
    for step in range(ITERS):
        applied = surface_apply(direction, surface_damping, turned)
        step_size = norm_now / lax.psum(jnp.sum(direction * applied), "face")
        surface = surface + step_size * direction
        residual = residual - step_size * applied
        norm_next = lax.psum(jnp.sum(residual * residual), "face")
        direction = residual + norm_next / norm_now * direction
        norm_now = norm_next
    return surface


def flip_lanes(rows):
    width = rows.shape[1]
    back = LANES - 1 - lax.broadcasted_iota(jnp.int32, (SUBLANES, LANES), 1)
    tiles = []
    for start in range(width - LANES, -1, -LANES):
        tiles.append(
            jnp.take_along_axis(
                rows[:, start : start + LANES], back, axis=1, mode="promise_in_bounds"
            )
        )
    return jnp.concatenate(tiles, axis=1)


def chunks_of(levels, size):
    return [(k, min(size, levels - k)) for k in range(0, levels, size)]


def flip_some(rows):
    height, width = rows.shape
    if height < SUBLANES:
        rows = jnp.concatenate([rows, jnp.zeros((SUBLANES - height, width), rows.dtype)], axis=0)
    return flip_lanes(rows)[:height]


def outer_kernel(seam, eta, damping, up, down, mark):
    half = SUBLANES // 2
    down[:half, :] = eta[:half, :]
    down[half:, :] = damping[:half, :]
    up[:half, :] = eta[half:, :]
    up[half:, :] = damping[half:, :]

    @pl.when(seam[0] == 1)
    def _():
        up[...] = flip_lanes(up[...])


def basis_kernel(seam, eta, damping, below, above, basis, sums):
    half = SUBLANES // 2
    rows = 2 * SUBLANES
    beyond = above[...]
    beyond = jnp.where(seam[0] == 1, flip_lanes(beyond), beyond)
    width = beyond.shape[1]
    v = jnp.concatenate([below[:half, :], eta[...], beyond[:half, :]], axis=0)
    d = jnp.concatenate([below[half:, :], damping[...], beyond[half:, :]], axis=0)
    d = (d + (4.0 - MIDDLE)) * (1.0 / MIDDLE)
    vectors = [v]
    for j in range(ITERS):
        now = vectors[-1]
        near = (
            pltpu.roll(now, 1, 0)
            + pltpu.roll(now, rows - 1, 0)
            + pltpu.roll(now, 1, 1)
            + pltpu.roll(now, width - 1, 1)
        )
        image = d * now - near * (1.0 / MIDDLE)
        vectors.append(image if j == 0 else 2.0 * image - vectors[-2])
    for j in range(ITERS):
        basis[j] = vectors[j]
    row = lax.broadcasted_iota(jnp.int32, (rows, LANES), 0)
    own = (row >= half) & (row < half + SUBLANES)
    parts = []
    for j in range(2 * ITERS):
        product = vectors[j // 2] * vectors[j // 2 + j % 2]
        total = product[:, :LANES]
        for start in range(LANES, width, LANES):
            total = total + product[:, start : start + LANES]
        parts.append(jnp.sum(jnp.where(own, total, 0.0), axis=0, keepdims=True))
    tile = jnp.concatenate(parts, axis=0)
    for i in range(sums.shape[0]):
        sums[i] = tile


def coefficients(moments):
    def dot(a, b):
        total = None
        for i, x in enumerate(a):
            for j, y in enumerate(b):
                term = x * y * (moments[i + j] + moments[abs(i - j)])
                total = term if total is None else total + term
        return 0.5 * total

    def image(p):
        q = [MIDDLE * x for x in p] + [jnp.zeros_like(p[0])]
        for i, x in enumerate(p):
            if i == 0:
                q[1] = q[1] + MIDDLE * x
            else:
                q[i + 1] = q[i + 1] + (0.5 * MIDDLE) * x
                q[i - 1] = q[i - 1] + (0.5 * MIDDLE) * x
        return q

    def size(p):
        return functools.reduce(lambda a, b: a + b, [jnp.abs(x) for x in p])

    def plus(a, b):
        return [x + y for x, y in zip(a, b)] + list(a[len(b) :]) + list(b[len(a) :])

    norm_first = moments[0]
    p = [jnp.ones_like(norm_first)]
    r = p
    norm_now = norm_first
    s = []
    sound = norm_first > 0.0
    for step in range(ITERS):
        q = image(p)
        curve = dot(p, q)
        sound = sound & (curve * LOSS >= size(p) * size(q) * norm_first)
        rate = norm_now / curve
        s = plus(s, [rate * x for x in p])
        if step < ITERS - 1:
            r = plus(r, [-rate * x for x in q])
            norm_next = dot(r, r)
            sound = sound & (norm_next * LOSS >= size(r) * size(r) * norm_first)
            ratio = norm_next / norm_now
            p = plus(r, [ratio * x for x in p])
            norm_now = norm_next
    return s, sound


def outer_lines(seam, fields, edges, up, down):
    turned = seam[0] == 1
    for k in range(0, up.shape[0], SUBLANES):
        at = slice(k, k + SUBLANES)
        top = edges[0, at, :] + fields[SUBLANES - 1 : SUBLANES, :] * edges[1, at, :]
        up[at, :] = jnp.where(turned, flip_lanes(top), top)
        down[at, :] = edges[2, at, :] + fields[:1, :] * edges[3, at, :]


def surface_kernel(seam, sums, basis, edges, surface, up, down, sound):
    half = SUBLANES // 2
    parts = [sums[i] for i in range(sums.shape[0])]
    while len(parts) > 1:
        pairs = [a + b for a, b in zip(parts[::2], parts[1::2])]
        parts = pairs + parts[len(parts) - len(parts) % 2 :]
    total = jnp.sum(parts[0], axis=1, keepdims=True)
    raw = [total[j : j + 1, :] for j in range(2 * ITERS)]
    moments = raw[:2]
    for j in range(2, 2 * ITERS):
        moments.append(2.0 * raw[j] - raw[j % 2])
    s, good = coefficients(moments)
    value = s[0] * basis[0]
    for j in range(1, ITERS):
        value = value + s[j] * basis[j]
    surface[...] = value[half : half + SUBLANES, :]
    sound[0] = jnp.where(good, 1, 0)[0, 0]
    outer_lines(seam, surface, edges, up, down)


CHUNK = 10


def column_kernel(
    seam, thickness_from, tracer, mixing, velocity_y, wet, after, solved, up, down, edges,
    thickness, depth_at, tracer_at, mixing_at, velocity_at, solved_at, ratio_at,
    sems, out_sems,
):
    levels = tracer.shape[1]
    chunks = chunks_of(levels, CHUNK)
    few = [
        pltpu.make_async_copy(thickness_from, thickness, sems.at[2, 1]),
        pltpu.make_async_copy(wet, depth_at, sems.at[2, 2]),
    ]
    loads = []
    for i, (k, n) in enumerate(chunks):
        m = min(n, levels - 1 - k)
        loads.append((
            pltpu.make_async_copy(
                mixing.at[pl.ds(k, m)], mixing_at.at[pl.ds(k, m)], sems.at[1, i]
            ),
            pltpu.make_async_copy(
                tracer.at[:, pl.ds(k, n)], tracer_at.at[:, pl.ds(k, n)], sems.at[0, i]
            ),
        ))
    velocity_load = pltpu.make_async_copy(velocity_y, velocity_at, sems.at[2, 0])
    for pair in [few] + loads:
        pair[0].start()
        pair[1].start()
    velocity_load.start()

    few[0].wait()
    few[1].wait()
    depth = depth_at[...]
    zero = jnp.zeros(depth.shape, jnp.float32)

    def forward(k, carry):
        c_before, g_before, y0, y1, y2 = carry
        th = thickness[k]
        c = jnp.where(k + 1 < depth, mixing_at[jnp.minimum(k, levels - 2)], 0.0)
        inverse = 1.0 / (th + c + c_before * (1.0 - g_before))
        g = c * inverse
        y0 = (tracer_at[0, k] + c_before * y0) * inverse
        y1 = (tracer_at[1, k] + c_before * y1) * inverse
        y2 = (jnp.where(k < depth, th, 0.0) + c_before * y2) * inverse
        ratio_at[k] = g
        solved_at[0, k] = y0
        solved_at[1, k] = y1
        solved_at[2, k] = y2
        return c, g, y0, y1, y2

    carry = (zero,) * 5
    for i, (k, n) in enumerate(chunks):
        loads[i][0].wait()
        loads[i][1].wait()
        carry = lax.fori_loop(k, k + n, forward, carry, unroll=5)

    stores = []
    carry = (zero,) * 3
    for i, (k, n) in reversed(list(enumerate(chunks))):

        def backward(j, carry, last=k + n - 1):
            level = last - j
            th = thickness[level]
            g = ratio_at[level]
            after = []
            for t in range(3):
                u = solved_at[t, level] + g * carry[t]
                solved_at[t, level] = th * u
                after.append(u)
            return tuple(after)

        carry = lax.fori_loop(0, n, backward, carry, unroll=5)
        stores.append(
            pltpu.make_async_copy(
                solved_at.at[:, pl.ds(k, n)], solved.at[:, pl.ds(k, n)], out_sems.at[i]
            )
        )
        stores[-1].start()

    velocity_load.wait()
    turned = seam[0] == 1
    for k, n in chunks_of(levels, SUBLANES):
        at = slice(k, k + n)
        to_up = diffusion - advection * velocity_at[pl.ds(k, n), SUBLANES - 1, :]
        to_down = diffusion + advection * velocity_at[pl.ds(k, n), 0, :]
        top = solved_at[1, pl.ds(k, n), SUBLANES - 1, :] * to_up
        up[at, :] = jnp.where(turned, flip_some(top), top)
        down[at, :] = solved_at[1, pl.ds(k, n), 0, :] * to_down
        for t in range(2):
            edges[t, at, :] = solved_at[2 * t, pl.ds(k, n), SUBLANES - 1, :] * to_up
            edges[2 + t, at, :] = solved_at[2 * t, pl.ds(k, n), 0, :] * to_down
    for store in stores:
        store.wait()


def inside_kernel(solved, velocity_x, velocity_y, wet, fields, result, surface):
    levels = velocity_x.shape[0]
    width = wet.shape[1]
    depth = wet[...]
    s = fields[...]
    surface[...] = s
    row = lax.broadcasted_iota(jnp.int32, depth.shape, 0)
    is_south = row == 0
    is_north = row == SUBLANES - 1

    def level(k, _):
        flow_x = advection * velocity_x[k]
        flow_y = advection * velocity_y[k]
        to_west = diffusion + flow_x
        to_east = diffusion - flow_x
        to_south = jnp.where(is_south, 0.0, diffusion + flow_y)
        to_north = jnp.where(is_north, 0.0, diffusion - flow_y)
        is_wet = k < depth
        for t in range(2):
            x = solved[t, k]
            if t == 0:
                x = x + s * solved[2, k]
            eastern = pltpu.roll(x * to_west, width - 1, 1)
            western = pltpu.roll(x * to_east, 1, 1)
            northern = pltpu.roll(x * to_south, SUBLANES - 1, 0)
            southern = pltpu.roll(x * to_north, 1, 0)
            value = (1.0 - 4.0 * diffusion) * x + ((eastern + western) + (northern + southern))
            result[t, k] = jnp.where(is_wet, value, 0.0)
        return 0

    lax.fori_loop(0, levels, level, 0, unroll=5)


def rim_kernel(seam, inside, wet, south0, north0, south1, north1, result, result_at, out_sems):
    levels = inside.shape[1]
    width = wet.shape[1]
    turned = seam[0] == 1
    depth_south = wet[:1, :]
    depth_north = wet[SUBLANES - 1 :, :]
    stores = []
    for i, (k, n) in enumerate(chunks_of(levels, SUBLANES)):
        at = pl.ds(k, n)
        index = k + lax.broadcasted_iota(jnp.int32, (n, width), 0)
        result_at[:, at] = inside[:, at]
        for t, (south_from, north_from) in enumerate(((south0, north0), (south1, north1))):
            south = south_from[k : k + n, :]
            north = north_from[k : k + n, :]
            north = jnp.where(turned, flip_some(north), north)
            result_at[t, at, 0, :] += jnp.where(index < depth_south, south, 0.0)
            result_at[t, at, SUBLANES - 1, :] += jnp.where(index < depth_north, north, 0.0)
        stores.append(pltpu.make_async_copy(result_at.at[:, at], result.at[:, at], out_sems.at[i]))
        stores[-1].start()
    for store in stores:
        store.wait()


def shards(
    tracer_adjoint,
    eta_adjoint,
    velocity_x,
    velocity_y,
    mixing,
    thickness,
    surface_damping,
    wet_levels,
    seam_codes,
):
    tracers, levels, rows, width = tracer_adjoint.shape
    f32 = jnp.float32
    count = lax.axis_size("face")
    upward = [(i, (i + 1) % count) for i in range(count)]
    downward = [(j, i) for i, j in upward]
    tile = jax.ShapeDtypeStruct((rows, width), f32)
    ext = jax.ShapeDtypeStruct((ITERS, 2 * rows, width), f32)
    lines = -(-levels // SUBLANES) * SUBLANES
    line = jax.ShapeDtypeStruct((lines, width), f32)

    up, down, mark = pl.pallas_call(
        outer_kernel,
        out_shape=(tile, tile, pltpu.HBM((rows, LANES), f32)),
        in_specs=[SMEM, VMEM, VMEM],
        out_specs=(VMEM, VMEM, HBM),
        name="outer_rows",
    )(seam_codes, eta_adjoint, surface_damping)
    below = lax.ppermute(up, "face", upward)
    above = lax.ppermute(down, "face", downward)

    cube = pltpu.VMEM((levels, rows, width), f32)
    parts = len(chunks_of(levels, CHUNK))
    solved, up1, down1, edges = pl.pallas_call(
        column_kernel,
        out_shape=(
            pltpu.HBM((3, levels, rows, width), f32),
            line,
            line,
            jax.ShapeDtypeStruct((4, lines, width), f32),
        ),
        in_specs=[SMEM] + [HBM] * 6,
        out_specs=(HBM, VMEM, VMEM, VMEM),
        scratch_shapes=[
            pltpu.SMEM((levels,), f32),
            pltpu.VMEM((rows, width), jnp.int32),
            pltpu.VMEM((tracers, levels, rows, width), f32),
            cube,
            cube,
            pltpu.VMEM((3, levels, rows, width), f32),
            cube,
            pltpu.SemaphoreType.DMA((3, max(parts, 3))),
            pltpu.SemaphoreType.DMA((parts,)),
        ],
        compiler_params=PARAMS,
        cost_estimate=pl.CostEstimate(flops=40000000, bytes_accessed=13000000, transcendentals=0),
        name="columns",
    )(
        seam_codes,
        *map(in_hbm, (thickness, tracer_adjoint, mixing, velocity_y, wet_levels, mark)),
    )

    basis, sums = pl.pallas_call(
        basis_kernel,
        out_shape=(ext, jax.ShapeDtypeStruct((count, SUBLANES, LANES), f32)),
        in_specs=[SMEM] + [VMEM] * 4,
        out_specs=(VMEM, VMEM),
        compiler_params=PARAMS,
        name="surface_basis",
    )(seam_codes, eta_adjoint, surface_damping, below, above)
    sums, up1, down1 = lax.optimization_barrier((sums, up1, down1))
    sums = lax.all_to_all(sums, "face", 0, 0)
    south1 = lax.ppermute(up1, "face", upward)
    north1 = lax.ppermute(down1, "face", downward)
    sums, south1, north1 = lax.optimization_barrier((sums, south1, north1))

    fields, up0, down0, sound = pl.pallas_call(
        surface_kernel,
        out_shape=(tile, line, line, jax.ShapeDtypeStruct((1,), jnp.int32)),
        in_specs=[SMEM, VMEM, VMEM, VMEM],
        out_specs=(VMEM, VMEM, VMEM, SMEM),
        compiler_params=PARAMS,
        name="surface",
    )(seam_codes, sums, basis, edges)

    def by_moments(fields, up0, down0):
        return fields, up0, down0

    def by_steps(fields, up0, down0):
        turned = seam_codes[0] == 1
        surface = stepwise_surface(eta_adjoint, surface_damping, turned)
        up0, down0 = pl.pallas_call(
            outer_lines,
            out_shape=(line, line),
            in_specs=[SMEM, VMEM, VMEM],
            out_specs=(VMEM, VMEM),
            compiler_params=PARAMS,
            name="outer_lines",
        )(seam_codes, surface, edges)
        return surface, up0, down0

    fields, up0, down0 = lax.cond(sound[0] == 1, by_moments, by_steps, fields, up0, down0)
    south0 = lax.ppermute(up0, "face", upward)
    north0 = lax.ppermute(down0, "face", downward)

    parts = len(chunks_of(levels, SUBLANES))
    inside, surface = pl.pallas_call(
        inside_kernel,
        out_shape=(jax.ShapeDtypeStruct((tracers, levels, rows, width), f32), tile),
        in_specs=[VMEM] * 5,
        out_specs=(VMEM, VMEM),
        compiler_params=PARAMS,
        cost_estimate=pl.CostEstimate(flops=20000000, bytes_accessed=13000000, transcendentals=0),
        name="inside",
    )(solved, velocity_x, velocity_y, wet_levels, fields)

    result = pl.pallas_call(
        rim_kernel,
        out_shape=jax.ShapeDtypeStruct((tracers, levels, rows, width), f32),
        in_specs=[SMEM] + [VMEM] * 6,
        out_specs=HBM,
        scratch_shapes=[
            pltpu.VMEM((tracers, levels, rows, width), f32),
            pltpu.SemaphoreType.DMA((parts,)),
        ],
        compiler_params=PARAMS,
        name="rims",
    )(seam_codes, inside, wet_levels, south0, north0, south1, north1)
    return result, surface


def solution(mesh):
    placed = (
        P(None, None, "face", "ens"),
        P("face", "ens"),
        P(None, "face", "ens"),
        P(None, "face", "ens"),
        P(None, "face", "ens"),
        P(),
        P("face", None),
        P("face", None),
        P("face"),
    )
    return jax.shard_map(
        shards,
        mesh=mesh,
        in_specs=placed,
        out_specs=(P(None, None, "face", "ens"), P("face", "ens")),
        check_vma=False,
    )
```

```python
import functools
import jax
import jax.numpy as jnp
from jax import lax
from jax.experimental import pallas as pl
from jax.experimental.pallas import tpu as pltpu
from jax.sharding import PartitionSpec as P

ITERS = 4
LANES = 128
SUBLANES = 8
diffusion = 0.1
advection = 0.5

MIDDLE = 4.1
LOSS = 1000.0

SMEM = pl.BlockSpec(memory_space=pltpu.SMEM)
VMEM = pl.BlockSpec(memory_space=pltpu.VMEM)
HBM = pl.BlockSpec(memory_space=pltpu.HBM)
PARAMS = pltpu.CompilerParams(vmem_limit_bytes=32 * 2**20)


def in_hbm(x):
    return pltpu.with_memory_space_constraint(x, pltpu.HBM)


def with_halo(x, sides, width):
    for axis, dim in sides:
        count, length = (lax.axis_size(axis), x.shape[dim])
        up = [(i, (i + 1) % count) for i in range(count)]
        down = [(j, i) for i, j in up]
        last = lax.slice_in_dim(x, length - width, length, axis=dim)
        initial = lax.slice_in_dim(x, 0, width, axis=dim)
        before = lax.ppermute(last, axis, up)
        after = lax.ppermute(initial, axis, down)
        x = jnp.concatenate([before, x, after], axis=dim)
    return x


def raised(block_rows, turned):
    upper_row = block_rows[..., -1:, :]
    upper_row = jnp.where(turned, jnp.flip(upper_row, -1), upper_row)
    return jnp.concatenate([block_rows[..., :-1, :], upper_row], axis=-2)


def settled(block_rows, padded, turned):
    lower_rim = padded[..., :1, :]
    upper_rim = padded[..., -1:, :]
    upper_rim = jnp.where(turned, jnp.flip(upper_rim, -1), upper_rim)
    southern = jnp.concatenate([lower_rim, block_rows[..., :-1, :]], axis=-2)
    northern = jnp.concatenate([block_rows[..., 1:, :], upper_rim], axis=-2)
    return (southern, northern)


def surface_apply(values_in, damping, turned):
    padded = with_halo(raised(values_in, turned), (("face", 0),), 1)
    southern, northern = settled(values_in, padded, turned)
    return (4.0 + damping) * values_in - (
        southern + northern + jnp.roll(values_in, 1, -1) + jnp.roll(values_in, -1, -1)
    )


def stepwise_surface(eta_adjoint, surface_damping, turned):
    surface = jnp.zeros_like(eta_adjoint)
    residual = eta_adjoint
    direction = eta_adjoint
    norm_now = lax.psum(jnp.sum(residual * residual), "face")
    for step in range(ITERS):
        applied = surface_apply(direction, surface_damping, turned)
        step_size = norm_now / lax.psum(jnp.sum(direction * applied), "face")
        surface = surface + step_size * direction
        residual = residual - step_size * applied
        norm_next = lax.psum(jnp.sum(residual * residual), "face")
        direction = residual + norm_next / norm_now * direction
        norm_now = norm_next
    return surface


def flip_lanes(rows):
    width = rows.shape[1]
    back = LANES - 1 - lax.broadcasted_iota(jnp.int32, (SUBLANES, LANES), 1)
    tiles = []
    for start in range(width - LANES, -1, -LANES):
        tiles.append(
            jnp.take_along_axis(
                rows[:, start : start + LANES], back, axis=1, mode="promise_in_bounds"
            )
        )
    return jnp.concatenate(tiles, axis=1)


def chunks_of(levels, size):
    return [(k, min(size, levels - k)) for k in range(0, levels, size)]


def flip_some(rows):
    height, width = rows.shape
    if height < SUBLANES:
        rows = jnp.concatenate([rows, jnp.zeros((SUBLANES - height, width), rows.dtype)], axis=0)
    return flip_lanes(rows)[:height]


def outer_kernel(seam, eta, damping, up, down, mark):
    half = SUBLANES // 2
    down[:half, :] = eta[:half, :]
    down[half:, :] = damping[:half, :]
    up[:half, :] = eta[half:, :]
    up[half:, :] = damping[half:, :]

    @pl.when(seam[0] == 1)
    def _():
        up[...] = flip_lanes(up[...])


def basis_kernel(seam, eta, damping, below, above, basis, sums):
    half = SUBLANES // 2
    rows = 2 * SUBLANES
    beyond = above[...]
    beyond = jnp.where(seam[0] == 1, flip_lanes(beyond), beyond)
    width = beyond.shape[1]
    v = jnp.concatenate([below[:half, :], eta[...], beyond[:half, :]], axis=0)
    d = jnp.concatenate([below[half:, :], damping[...], beyond[half:, :]], axis=0)
    d = (d + (4.0 - MIDDLE)) * (1.0 / MIDDLE)
    vectors = [v]
    for j in range(ITERS):
        now = vectors[-1]
        near = (
            pltpu.roll(now, 1, 0)
            + pltpu.roll(now, rows - 1, 0)
            + pltpu.roll(now, 1, 1)
            + pltpu.roll(now, width - 1, 1)
        )
        image = d * now - near * (1.0 / MIDDLE)
        vectors.append(image if j == 0 else 2.0 * image - vectors[-2])
    for j in range(ITERS):
        basis[j] = vectors[j]
    row = lax.broadcasted_iota(jnp.int32, (rows, LANES), 0)
    own = (row >= half) & (row < half + SUBLANES)
    parts = []
    for j in range(2 * ITERS):
        product = vectors[j // 2] * vectors[j // 2 + j % 2]
        total = product[:, :LANES]
        for start in range(LANES, width, LANES):
            total = total + product[:, start : start + LANES]
        parts.append(jnp.sum(jnp.where(own, total, 0.0), axis=0, keepdims=True))
    tile = jnp.concatenate(parts, axis=0)
    for i in range(sums.shape[0]):
        sums[i] = tile


def coefficients(moments):
    def dot(a, b):
        total = None
        for i, x in enumerate(a):
            for j, y in enumerate(b):
                term = x * y * (moments[i + j] + moments[abs(i - j)])
                total = term if total is None else total + term
        return 0.5 * total

    def image(p):
        q = [MIDDLE * x for x in p] + [jnp.zeros_like(p[0])]
        for i, x in enumerate(p):
            if i == 0:
                q[1] = q[1] + MIDDLE * x
            else:
                q[i + 1] = q[i + 1] + (0.5 * MIDDLE) * x
                q[i - 1] = q[i - 1] + (0.5 * MIDDLE) * x
        return q

    def size(p):
        return functools.reduce(lambda a, b: a + b, [jnp.abs(x) for x in p])

    def plus(a, b):
        return [x + y for x, y in zip(a, b)] + list(a[len(b) :]) + list(b[len(a) :])

    norm_first = moments[0]
    p = [jnp.ones_like(norm_first)]
    r = p
    norm_now = norm_first
    s = []
    sound = norm_first > 0.0
    for step in range(ITERS):
        q = image(p)
        curve = dot(p, q)
        sound = sound & (curve * LOSS >= size(p) * size(q) * norm_first)
        rate = norm_now / curve
        s = plus(s, [rate * x for x in p])
        if step < ITERS - 1:
            r = plus(r, [-rate * x for x in q])
            norm_next = dot(r, r)
            sound = sound & (norm_next * LOSS >= size(r) * size(r) * norm_first)
            ratio = norm_next / norm_now
            p = plus(r, [ratio * x for x in p])
            norm_now = norm_next
    return s, sound


def outer_lines(seam, fields, edges, up, down):
    turned = seam[0] == 1
    for k in range(0, up.shape[0], SUBLANES):
        at = slice(k, k + SUBLANES)
        top = edges[0, at, :] + fields[SUBLANES - 1 : SUBLANES, :] * edges[1, at, :]
        up[at, :] = jnp.where(turned, flip_lanes(top), top)
        down[at, :] = edges[2, at, :] + fields[:1, :] * edges[3, at, :]


def surface_kernel(seam, sums, basis, edges, surface, up, down, sound):
    half = SUBLANES // 2
    parts = [sums[i] for i in range(sums.shape[0])]
    while len(parts) > 1:
        pairs = [a + b for a, b in zip(parts[::2], parts[1::2])]
        parts = pairs + parts[len(parts) - len(parts) % 2 :]
    total = jnp.sum(parts[0], axis=1, keepdims=True)
    raw = [total[j : j + 1, :] for j in range(2 * ITERS)]
    moments = raw[:2]
    for j in range(2, 2 * ITERS):
        moments.append(2.0 * raw[j] - raw[j % 2])
    s, good = coefficients(moments)
    value = s[0] * basis[0]
    for j in range(1, ITERS):
        value = value + s[j] * basis[j]
    surface[...] = value[half : half + SUBLANES, :]
    sound[0] = jnp.where(good, 1, 0)[0, 0]
    outer_lines(seam, surface, edges, up, down)


CHUNK = 10


def column_kernel(
    seam, thickness_from, tracer, mixing, velocity_y, wet, after, solved, up, down, edges,
    thickness, depth_at, tracer_at, mixing_at, velocity_at, ratio_at, sems,
):
    levels = tracer.shape[1]
    chunks = chunks_of(levels, CHUNK)
    few = [
        pltpu.make_async_copy(thickness_from, thickness, sems.at[2, 1]),
        pltpu.make_async_copy(wet, depth_at, sems.at[2, 2]),
    ]
    loads = []
    for i, (k, n) in enumerate(chunks):
        m = min(n, levels - 1 - k)
        loads.append((
            pltpu.make_async_copy(
                mixing.at[pl.ds(k, m)], mixing_at.at[pl.ds(k, m)], sems.at[1, i]
            ),
            pltpu.make_async_copy(
                tracer.at[:, pl.ds(k, n)], tracer_at.at[:, pl.ds(k, n)], sems.at[0, i]
            ),
        ))
    velocity_load = pltpu.make_async_copy(velocity_y, velocity_at, sems.at[2, 0])
    for pair in [few] + loads:
        pair[0].start()
        pair[1].start()
    velocity_load.start()

    few[0].wait()
    few[1].wait()
    depth = depth_at[...]
    zero = jnp.zeros(depth.shape, jnp.float32)

    def forward(k, carry):
        c_before, g_before, y0, y1, y2 = carry
        th = thickness[k]
        c = jnp.where(k + 1 < depth, mixing_at[jnp.minimum(k, levels - 2)], 0.0)
        inverse = 1.0 / (th + c + c_before * (1.0 - g_before))
        g = c * inverse
        y0 = (tracer_at[0, k] + c_before * y0) * inverse
        y1 = (tracer_at[1, k] + c_before * y1) * inverse
        y2 = (jnp.where(k < depth, th, 0.0) + c_before * y2) * inverse
        ratio_at[k] = g
        solved[0, k] = y0
        solved[1, k] = y1
        solved[2, k] = y2
        return c, g, y0, y1, y2

    carry = (zero,) * 5
    for i, (k, n) in enumerate(chunks):
        loads[i][0].wait()
        loads[i][1].wait()
        carry = lax.fori_loop(k, k + n, forward, carry, unroll=5)

    carry = (zero,) * 3
    for i, (k, n) in reversed(list(enumerate(chunks))):

        def backward(j, carry, last=k + n - 1):
            level = last - j
            th = thickness[level]
            g = ratio_at[level]
            after = []
            for t in range(3):
                u = solved[t, level] + g * carry[t]
                solved[t, level] = th * u
                after.append(u)
            return tuple(after)

        carry = lax.fori_loop(0, n, backward, carry, unroll=5)

    velocity_load.wait()
    turned = seam[0] == 1
    for k, n in chunks_of(levels, SUBLANES):
        at = slice(k, k + n)
        to_up = diffusion - advection * velocity_at[pl.ds(k, n), SUBLANES - 1, :]
        to_down = diffusion + advection * velocity_at[pl.ds(k, n), 0, :]
        top = solved[1, pl.ds(k, n), SUBLANES - 1, :] * to_up
        up[at, :] = jnp.where(turned, flip_some(top), top)
        down[at, :] = solved[1, pl.ds(k, n), 0, :] * to_down
        for t in range(2):
            edges[t, at, :] = solved[2 * t, pl.ds(k, n), SUBLANES - 1, :] * to_up
            edges[2 + t, at, :] = solved[2 * t, pl.ds(k, n), 0, :] * to_down


def inside_kernel(solved, velocity_x, velocity_y, wet, surface, result):
    levels = velocity_x.shape[0]
    width = wet.shape[1]
    depth = wet[...]
    s = surface[...]
    row = lax.broadcasted_iota(jnp.int32, depth.shape, 0)
    is_south = row == 0
    is_north = row == SUBLANES - 1

    def level(k, _):
        flow_x = advection * velocity_x[k]
        flow_y = advection * velocity_y[k]
        to_west = diffusion + flow_x
        to_east = diffusion - flow_x
        to_south = jnp.where(is_south, 0.0, diffusion + flow_y)
        to_north = jnp.where(is_north, 0.0, diffusion - flow_y)
        is_wet = k < depth
        for t in range(2):
            x = solved[t, k]
            if t == 0:
                x = x + s * solved[2, k]
            eastern = pltpu.roll(x * to_west, width - 1, 1)
            western = pltpu.roll(x * to_east, 1, 1)
            northern = pltpu.roll(x * to_south, SUBLANES - 1, 0)
            southern = pltpu.roll(x * to_north, 1, 0)
            value = (1.0 - 4.0 * diffusion) * x + ((eastern + western) + (northern + southern))
            result[t, k] = jnp.where(is_wet, value, 0.0)
        return 0

    lax.fori_loop(0, levels, level, 0, unroll=5)


def rim_kernel(seam, inside, wet, south0, north0, south1, north1, result, result_at, out_sems):
    levels = inside.shape[1]
    width = wet.shape[1]
    turned = seam[0] == 1
    depth_south = wet[:1, :]
    depth_north = wet[SUBLANES - 1 :, :]
    stores = []
    for i, (k, n) in enumerate(chunks_of(levels, SUBLANES)):
        at = pl.ds(k, n)
        index = k + lax.broadcasted_iota(jnp.int32, (n, width), 0)
        result_at[:, at] = inside[:, at]
        for t, (south_from, north_from) in enumerate(((south0, north0), (south1, north1))):
            south = south_from[k : k + n, :]
            north = north_from[k : k + n, :]
            north = jnp.where(turned, flip_some(north), north)
            result_at[t, at, 0, :] += jnp.where(index < depth_south, south, 0.0)
            result_at[t, at, SUBLANES - 1, :] += jnp.where(index < depth_north, north, 0.0)
        stores.append(pltpu.make_async_copy(result_at.at[:, at], result.at[:, at], out_sems.at[i]))
        stores[-1].start()
    for store in stores:
        store.wait()


def shards(
    tracer_adjoint,
    eta_adjoint,
    velocity_x,
    velocity_y,
    mixing,
    thickness,
    surface_damping,
    wet_levels,
    seam_codes,
):
    tracers, levels, rows, width = tracer_adjoint.shape
    f32 = jnp.float32
    count = lax.axis_size("face")
    upward = [(i, (i + 1) % count) for i in range(count)]
    downward = [(j, i) for i, j in upward]
    tile = jax.ShapeDtypeStruct((rows, width), f32)
    ext = pltpu.HBM((ITERS, 2 * rows, width), f32)
    lines = -(-levels // SUBLANES) * SUBLANES
    line = jax.ShapeDtypeStruct((lines, width), f32)

    up, down, mark = pl.pallas_call(
        outer_kernel,
        out_shape=(tile, tile, pltpu.HBM((rows, LANES), f32)),
        in_specs=[SMEM, VMEM, VMEM],
        out_specs=(VMEM, VMEM, HBM),
        name="outer_rows",
    )(seam_codes, eta_adjoint, surface_damping)
    below = lax.ppermute(up, "face", upward)
    above = lax.ppermute(down, "face", downward)

    cube = pltpu.VMEM((levels, rows, width), f32)
    parts = len(chunks_of(levels, CHUNK))
    solved, up1, down1, edges = pl.pallas_call(
        column_kernel,
        out_shape=(
            jax.ShapeDtypeStruct((3, levels, rows, width), f32),
            line,
            line,
            jax.ShapeDtypeStruct((4, lines, width), f32),
        ),
        in_specs=[SMEM] + [HBM] * 6,
        out_specs=(VMEM, VMEM, VMEM, VMEM),
        scratch_shapes=[
            pltpu.SMEM((levels,), f32),
            pltpu.VMEM((rows, width), jnp.int32),
            pltpu.VMEM((tracers, levels, rows, width), f32),
            cube,
            cube,
            cube,
            pltpu.SemaphoreType.DMA((3, max(parts, 3))),
        ],
        compiler_params=PARAMS,
        cost_estimate=pl.CostEstimate(flops=40000000, bytes_accessed=13000000, transcendentals=0),
        name="columns",
    )(
        seam_codes,
        *map(in_hbm, (thickness, tracer_adjoint, mixing, velocity_y, wet_levels, mark)),
    )

    basis, sums = pl.pallas_call(
        basis_kernel,
        out_shape=(ext, jax.ShapeDtypeStruct((count, SUBLANES, LANES), f32)),
        in_specs=[SMEM] + [VMEM] * 4,
        out_specs=(VMEM, VMEM),
        compiler_params=PARAMS,
        name="surface_basis",
    )(seam_codes, eta_adjoint, surface_damping, below, above)
    sums, up1, down1 = lax.optimization_barrier((sums, up1, down1))
    sums = lax.all_to_all(sums, "face", 0, 0)
    south1 = lax.ppermute(up1, "face", upward)
    north1 = lax.ppermute(down1, "face", downward)
    sums, south1, north1 = lax.optimization_barrier((sums, south1, north1))

    surface, up0, down0, sound = pl.pallas_call(
        surface_kernel,
        out_shape=(tile, line, line, jax.ShapeDtypeStruct((1,), jnp.int32)),
        in_specs=[SMEM, VMEM, VMEM, VMEM],
        out_specs=(VMEM, VMEM, VMEM, SMEM),
        compiler_params=PARAMS,
        name="surface",
    )(seam_codes, sums, basis, edges)

    parts = len(chunks_of(levels, SUBLANES))

    def inside_of(surface):
        return pl.pallas_call(
            inside_kernel,
            out_shape=jax.ShapeDtypeStruct((tracers, levels, rows, width), f32),
            in_specs=[VMEM] * 5,
            out_specs=VMEM,
            compiler_params=PARAMS,
            cost_estimate=pl.CostEstimate(
                flops=20000000, bytes_accessed=13000000, transcendentals=0
            ),
            name="inside",
        )(solved, velocity_x, velocity_y, wet_levels, surface)

    def with_rims(inside, south0, north0, south1, north1):
        return pl.pallas_call(
            rim_kernel,
            out_shape=pltpu.HBM((tracers, levels, rows, width), f32),
            in_specs=[SMEM] + [VMEM] * 6,
            out_specs=HBM,
            scratch_shapes=[
                pltpu.VMEM((tracers, levels, rows, width), f32),
                pltpu.SemaphoreType.DMA((parts,)),
            ],
            compiler_params=PARAMS,
            name="rims",
        )(seam_codes, inside, wet_levels, south0, north0, south1, north1)

    south0 = lax.ppermute(up0, "face", upward)
    north0 = lax.ppermute(down0, "face", downward)
    inside = inside_of(surface)

    def by_moments(surface, inside, south0, north0):
        return with_rims(inside, south0, north0, south1, north1), surface

    def by_steps(surface, inside, south0, north0):
        surface = stepwise_surface(eta_adjoint, surface_damping, seam_codes[0] == 1)
        up0, down0 = pl.pallas_call(
            outer_lines,
            out_shape=(line, line),
            in_specs=[SMEM, VMEM, VMEM],
            out_specs=(VMEM, VMEM),
            compiler_params=PARAMS,
            name="outer_lines",
        )(seam_codes, surface, edges)
        south0 = lax.ppermute(up0, "face", upward)
        north0 = lax.ppermute(down0, "face", downward)
        return with_rims(inside_of(surface), south0, north0, south1, north1), surface

    return lax.cond(sound[0] == 1, by_moments, by_steps, surface, inside, south0, north0)


def solution(mesh):
    placed = (
        P(None, None, "face", "ens"),
        P("face", "ens"),
        P(None, "face", "ens"),
        P(None, "face", "ens"),
        P(None, "face", "ens"),
        P(),
        P("face", None),
        P("face", None),
        P("face"),
    )
    return jax.shard_map(
        shards,
        mesh=mesh,
        in_specs=placed,
        out_specs=(P(None, None, "face", "ens"), P("face", "ens")),
        check_vma=False,
    )
```

```python
import functools
import jax
import jax.numpy as jnp
from jax import lax
from jax.experimental import pallas as pl
from jax.experimental.pallas import tpu as pltpu
from jax.sharding import PartitionSpec as P

ITERS = 4
LANES = 128
SUBLANES = 8
diffusion = 0.1
advection = 0.5

MIDDLE = 4.1
LOSS = 1000.0

SMEM = pl.BlockSpec(memory_space=pltpu.SMEM)
VMEM = pl.BlockSpec(memory_space=pltpu.VMEM)
HBM = pl.BlockSpec(memory_space=pltpu.HBM)
PARAMS = pltpu.CompilerParams(vmem_limit_bytes=24 * 2**20)


def in_hbm(x):
    return pltpu.with_memory_space_constraint(x, pltpu.HBM)


def with_halo(x, sides, width):
    for axis, dim in sides:
        count, length = (lax.axis_size(axis), x.shape[dim])
        up = [(i, (i + 1) % count) for i in range(count)]
        down = [(j, i) for i, j in up]
        last = lax.slice_in_dim(x, length - width, length, axis=dim)
        initial = lax.slice_in_dim(x, 0, width, axis=dim)
        before = lax.ppermute(last, axis, up)
        after = lax.ppermute(initial, axis, down)
        x = jnp.concatenate([before, x, after], axis=dim)
    return x


def raised(block_rows, turned):
    upper_row = block_rows[..., -1:, :]
    upper_row = jnp.where(turned, jnp.flip(upper_row, -1), upper_row)
    return jnp.concatenate([block_rows[..., :-1, :], upper_row], axis=-2)


def settled(block_rows, padded, turned):
    lower_rim = padded[..., :1, :]
    upper_rim = padded[..., -1:, :]
    upper_rim = jnp.where(turned, jnp.flip(upper_rim, -1), upper_rim)
    southern = jnp.concatenate([lower_rim, block_rows[..., :-1, :]], axis=-2)
    northern = jnp.concatenate([block_rows[..., 1:, :], upper_rim], axis=-2)
    return (southern, northern)


def surface_apply(values_in, damping, turned):
    padded = with_halo(raised(values_in, turned), (("face", 0),), 1)
    southern, northern = settled(values_in, padded, turned)
    return (4.0 + damping) * values_in - (
        southern + northern + jnp.roll(values_in, 1, -1) + jnp.roll(values_in, -1, -1)
    )


def stepwise_surface(eta_adjoint, surface_damping, turned):
    surface = jnp.zeros_like(eta_adjoint)
    residual = eta_adjoint
    direction = eta_adjoint
    norm_now = lax.psum(jnp.sum(residual * residual), "face")
    for step in range(ITERS):
        applied = surface_apply(direction, surface_damping, turned)
        step_size = norm_now / lax.psum(jnp.sum(direction * applied), "face")
        surface = surface + step_size * direction
        residual = residual - step_size * applied
        norm_next = lax.psum(jnp.sum(residual * residual), "face")
        direction = residual + norm_next / norm_now * direction
        norm_now = norm_next
    return surface


def flip_lanes(rows):
    width = rows.shape[1]
    back = LANES - 1 - lax.broadcasted_iota(jnp.int32, (SUBLANES, LANES), 1)
    tiles = []
    for start in range(width - LANES, -1, -LANES):
        tiles.append(
            jnp.take_along_axis(
                rows[:, start : start + LANES], back, axis=1, mode="promise_in_bounds"
            )
        )
    return jnp.concatenate(tiles, axis=1)


def chunks_of(levels, size):
    return [(k, min(size, levels - k)) for k in range(0, levels, size)]


def flip_some(rows):
    height, width = rows.shape
    if height < SUBLANES:
        rows = jnp.concatenate([rows, jnp.zeros((SUBLANES - height, width), rows.dtype)], axis=0)
    return flip_lanes(rows)[:height]


def outer_kernel(seam, eta, damping, up, down):
    half = SUBLANES // 2
    down[:half, :] = eta[:half, :]
    down[half:, :] = damping[:half, :]
    up[:half, :] = eta[half:, :]
    up[half:, :] = damping[half:, :]

    @pl.when(seam[0] == 1)
    def _():
        up[...] = flip_lanes(up[...])


def basis_kernel(seam, eta, damping, below, above, basis, sums, mark):
    half = SUBLANES // 2
    rows = 2 * SUBLANES
    beyond = above[...]
    beyond = jnp.where(seam[0] == 1, flip_lanes(beyond), beyond)
    width = beyond.shape[1]
    v = jnp.concatenate([below[:half, :], eta[...], beyond[:half, :]], axis=0)
    d = jnp.concatenate([below[half:, :], damping[...], beyond[half:, :]], axis=0)
    d = (d + (4.0 - MIDDLE)) * (1.0 / MIDDLE)
    vectors = [v]
    for j in range(ITERS):
        now = vectors[-1]
        near = (
            pltpu.roll(now, 1, 0)
            + pltpu.roll(now, rows - 1, 0)
            + pltpu.roll(now, 1, 1)
            + pltpu.roll(now, width - 1, 1)
        )
        image = d * now - near * (1.0 / MIDDLE)
        vectors.append(image if j == 0 else 2.0 * image - vectors[-2])
    for j in range(ITERS):
        basis[j] = vectors[j]
    row = lax.broadcasted_iota(jnp.int32, (rows, LANES), 0)
    own = (row >= half) & (row < half + SUBLANES)
    parts = []
    for j in range(2 * ITERS):
        product = vectors[j // 2] * vectors[j // 2 + j % 2]
        total = product[:, :LANES]
        for start in range(LANES, width, LANES):
            total = total + product[:, start : start + LANES]
        parts.append(jnp.sum(jnp.where(own, total, 0.0), axis=0, keepdims=True))
    tile = jnp.concatenate(parts, axis=0)
    for i in range(sums.shape[0]):
        sums[i] = tile


def coefficients(moments):
    def dot(a, b):
        total = None
        for i, x in enumerate(a):
            for j, y in enumerate(b):
                term = x * y * (moments[i + j] + moments[abs(i - j)])
                total = term if total is None else total + term
        return 0.5 * total

    def image(p):
        q = [MIDDLE * x for x in p] + [jnp.zeros_like(p[0])]
        for i, x in enumerate(p):
            if i == 0:
                q[1] = q[1] + MIDDLE * x
            else:
                q[i + 1] = q[i + 1] + (0.5 * MIDDLE) * x
                q[i - 1] = q[i - 1] + (0.5 * MIDDLE) * x
        return q

    def size(p):
        return functools.reduce(lambda a, b: a + b, [jnp.abs(x) for x in p])

    def plus(a, b):
        return [x + y for x, y in zip(a, b)] + list(a[len(b) :]) + list(b[len(a) :])

    norm_first = moments[0]
    p = [jnp.ones_like(norm_first)]
    r = p
    norm_now = norm_first
    s = []
    sound = norm_first > 0.0
    for step in range(ITERS):
        q = image(p)
        curve = dot(p, q)
        sound = sound & (curve * LOSS >= size(p) * size(q) * norm_first)
        rate = norm_now / curve
        s = plus(s, [rate * x for x in p])
        if step < ITERS - 1:
            r = plus(r, [-rate * x for x in q])
            norm_next = dot(r, r)
            sound = sound & (norm_next * LOSS >= size(r) * size(r) * norm_first)
            ratio = norm_next / norm_now
            p = plus(r, [ratio * x for x in p])
            norm_now = norm_next
    return s, sound


def outer_lines(seam, fields, edges, up, down):
    turned = seam[0] == 1
    for k in range(0, up.shape[0], SUBLANES):
        at = slice(k, k + SUBLANES)
        top = edges[0, at, :] + fields[SUBLANES - 1 : SUBLANES, :] * edges[1, at, :]
        up[at, :] = jnp.where(turned, flip_lanes(top), top)
        down[at, :] = edges[2, at, :] + fields[:1, :] * edges[3, at, :]


def surface_kernel(
    seam, sums, basis_from, edges_from, surface, up, down, sound, basis, edges, sems
):
    half = SUBLANES // 2
    loads = (
        pltpu.make_async_copy(basis_from, basis, sems.at[0]),
        pltpu.make_async_copy(edges_from, edges, sems.at[1]),
    )
    for load in loads:
        load.start()
    parts = [sums[i] for i in range(sums.shape[0])]
    while len(parts) > 1:
        pairs = [a + b for a, b in zip(parts[::2], parts[1::2])]
        parts = pairs + parts[len(parts) - len(parts) % 2 :]
    total = jnp.sum(parts[0], axis=1, keepdims=True)
    raw = [total[j : j + 1, :] for j in range(2 * ITERS)]
    moments = raw[:2]
    for j in range(2, 2 * ITERS):
        moments.append(2.0 * raw[j] - raw[j % 2])
    s, good = coefficients(moments)
    for load in loads:
        load.wait()
    value = s[0] * basis[0]
    for j in range(1, ITERS):
        value = value + s[j] * basis[j]
    surface[...] = value[half : half + SUBLANES, :]
    sound[0] = jnp.where(good, 1, 0)[0, 0]
    outer_lines(seam, surface, edges, up, down)


CHUNK = 10


def column_kernel(
    seam, thickness_from, tracer, mixing, velocity_y, wet, after, solved, up, down, edges,
    thickness, depth_at, tracer_at, mixing_at, velocity_at, ratio_at, sems,
):
    levels = tracer.shape[1]
    chunks = chunks_of(levels, CHUNK)
    few = [
        pltpu.make_async_copy(thickness_from, thickness, sems.at[2, 1]),
        pltpu.make_async_copy(wet, depth_at, sems.at[2, 2]),
    ]
    loads = []
    for i, (k, n) in enumerate(chunks):
        m = min(n, levels - 1 - k)
        loads.append((
            pltpu.make_async_copy(
                mixing.at[pl.ds(k, m)], mixing_at.at[pl.ds(k, m)], sems.at[1, i]
            ),
            pltpu.make_async_copy(
                tracer.at[:, pl.ds(k, n)], tracer_at.at[:, pl.ds(k, n)], sems.at[0, i]
            ),
        ))
    velocity_load = pltpu.make_async_copy(velocity_y, velocity_at, sems.at[2, 0])
    for pair in [few] + loads:
        pair[0].start()
        pair[1].start()
    velocity_load.start()

    few[0].wait()
    few[1].wait()
    depth = depth_at[...]
    zero = jnp.zeros(depth.shape, jnp.float32)

    def forward(k, carry):
        c_before, g_before, y0, y1, y2 = carry
        th = thickness[k]
        c = jnp.where(k + 1 < depth, mixing_at[jnp.minimum(k, levels - 2)], 0.0)
        inverse = 1.0 / (th + c + c_before * (1.0 - g_before))
        g = c * inverse
        y0 = (tracer_at[0, k] + c_before * y0) * inverse
        y1 = (tracer_at[1, k] + c_before * y1) * inverse
        y2 = (jnp.where(k < depth, th, 0.0) + c_before * y2) * inverse
        ratio_at[k] = g
        solved[0, k] = y0
        solved[1, k] = y1
        solved[2, k] = y2
        return c, g, y0, y1, y2

    carry = (zero,) * 5
    for i, (k, n) in enumerate(chunks):
        loads[i][0].wait()
        loads[i][1].wait()
        carry = lax.fori_loop(k, k + n, forward, carry, unroll=5)

    carry = (zero,) * 3
    for i, (k, n) in reversed(list(enumerate(chunks))):

        def backward(j, carry, last=k + n - 1):
            level = last - j
            th = thickness[level]
            g = ratio_at[level]
            after = []
            for t in range(3):
                u = solved[t, level] + g * carry[t]
                solved[t, level] = th * u
                after.append(u)
            return tuple(after)

        carry = lax.fori_loop(0, n, backward, carry, unroll=5)

    velocity_load.wait()
    turned = seam[0] == 1
    for k, n in chunks_of(levels, SUBLANES):
        at = slice(k, k + n)
        to_up = diffusion - advection * velocity_at[pl.ds(k, n), SUBLANES - 1, :]
        to_down = diffusion + advection * velocity_at[pl.ds(k, n), 0, :]
        top = solved[1, pl.ds(k, n), SUBLANES - 1, :] * to_up
        up[at, :] = jnp.where(turned, flip_some(top), top)
        down[at, :] = solved[1, pl.ds(k, n), 0, :] * to_down
        for t in range(2):
            edges[t, at, :] = solved[2 * t, pl.ds(k, n), SUBLANES - 1, :] * to_up
            edges[2 + t, at, :] = solved[2 * t, pl.ds(k, n), 0, :] * to_down


def inside_kernel(solved, velocity_x, velocity_y, wet, surface, result):
    levels = velocity_x.shape[0]
    width = wet.shape[1]
    depth = wet[...]
    s = surface[...]
    row = lax.broadcasted_iota(jnp.int32, depth.shape, 0)
    is_south = row == 0
    is_north = row == SUBLANES - 1

    def level(k, _):
        flow_x = advection * velocity_x[k]
        flow_y = advection * velocity_y[k]
        to_west = diffusion + flow_x
        to_east = diffusion - flow_x
        to_south = jnp.where(is_south, 0.0, diffusion + flow_y)
        to_north = jnp.where(is_north, 0.0, diffusion - flow_y)
        is_wet = k < depth
        for t in range(2):
            x = solved[t, k]
            if t == 0:
                x = x + s * solved[2, k]
            eastern = pltpu.roll(x * to_west, width - 1, 1)
            western = pltpu.roll(x * to_east, 1, 1)
            northern = pltpu.roll(x * to_south, SUBLANES - 1, 0)
            southern = pltpu.roll(x * to_north, 1, 0)
            value = (1.0 - 4.0 * diffusion) * x + ((eastern + western) + (northern + southern))
            result[t, k] = jnp.where(is_wet, value, 0.0)
        return 0

    lax.fori_loop(0, levels, level, 0, unroll=5)


def rim_kernel(
    seam, inside, wet, south0, north0, south1, north1, result, result_at, lines_at, sems, out_sems
):
    loads = []
    for i, line in enumerate((south1, north1, south0, north0)):
        loads.append(pltpu.make_async_copy(line, lines_at.at[i], sems.at[i]))
        loads[-1].start()
    for load in loads:
        load.wait()
    levels = inside.shape[1]
    width = wet.shape[1]
    turned = seam[0] == 1
    depth_south = wet[:1, :]
    depth_north = wet[SUBLANES - 1 :, :]
    stores = []
    for i, (k, n) in enumerate(chunks_of(levels, SUBLANES)):
        at = pl.ds(k, n)
        index = k + lax.broadcasted_iota(jnp.int32, (n, width), 0)
        result_at[:, at] = inside[:, at]
        for t in range(2):
            south = lines_at[2 - 2 * t, k : k + n, :]
            north = lines_at[3 - 2 * t, k : k + n, :]
            north = jnp.where(turned, flip_some(north), north)
            result_at[t, at, 0, :] += jnp.where(index < depth_south, south, 0.0)
            result_at[t, at, SUBLANES - 1, :] += jnp.where(index < depth_north, north, 0.0)
        stores.append(pltpu.make_async_copy(result_at.at[:, at], result.at[:, at], out_sems.at[i]))
        stores[-1].start()
    for store in stores:
        store.wait()


def shards(
    tracer_adjoint,
    eta_adjoint,
    velocity_x,
    velocity_y,
    mixing,
    thickness,
    surface_damping,
    wet_levels,
    seam_codes,
):
    tracers, levels, rows, width = tracer_adjoint.shape
    f32 = jnp.float32
    count = lax.axis_size("face")
    upward = [(i, (i + 1) % count) for i in range(count)]
    downward = [(j, i) for i, j in upward]
    tile = jax.ShapeDtypeStruct((rows, width), f32)
    ext = pltpu.HBM((ITERS, 2 * rows, width), f32)
    lines = -(-levels // SUBLANES) * SUBLANES
    line = jax.ShapeDtypeStruct((lines, width), f32)

    up, down = pl.pallas_call(
        outer_kernel,
        out_shape=(tile, tile),
        in_specs=[SMEM, VMEM, VMEM],
        out_specs=(VMEM, VMEM),
        name="outer_rows",
    )(seam_codes, eta_adjoint, surface_damping)
    below = lax.ppermute(up, "face", upward)
    above = lax.ppermute(down, "face", downward)

    cube = pltpu.VMEM((levels, rows, width), f32)
    chunks = len(chunks_of(levels, CHUNK))
    parts = len(chunks_of(levels, SUBLANES))
    inputs = [in_hbm(x) for x in (thickness, tracer_adjoint, mixing, velocity_y, wet_levels)]

    def columns_after(mark, place):
        return pl.pallas_call(
            column_kernel,
            out_shape=(
                place((3, levels, rows, width), f32),
                line,
                line,
                pltpu.HBM((4, lines, width), f32),
            ),
            in_specs=[SMEM] + [HBM] * 6,
            out_specs=(VMEM, VMEM, VMEM, VMEM),
            scratch_shapes=[
                pltpu.SMEM((levels,), f32),
                pltpu.VMEM((rows, width), jnp.int32),
                pltpu.VMEM((tracers, levels, rows, width), f32),
                cube,
                cube,
                cube,
                pltpu.SemaphoreType.DMA((3, max(chunks, 3))),
            ],
            compiler_params=PARAMS,
            cost_estimate=pl.CostEstimate(
                flops=40000000, bytes_accessed=13000000, transcendentals=0
            ),
            name="columns",
        )(seam_codes, *inputs, mark)

    def inside_of(solved, surface, place):
        return pl.pallas_call(
            inside_kernel,
            out_shape=place((tracers, levels, rows, width), f32),
            in_specs=[VMEM] * 5,
            out_specs=VMEM,
            compiler_params=PARAMS,
            cost_estimate=pl.CostEstimate(flops=1000, bytes_accessed=1000, transcendentals=0),
            name="inside",
        )(solved, velocity_x, velocity_y, wet_levels, surface)

    def with_rims(inside, *beyond):
        return pl.pallas_call(
            rim_kernel,
            out_shape=pltpu.HBM((tracers, levels, rows, width), f32),
            in_specs=[SMEM, VMEM, VMEM] + [HBM] * 4,
            out_specs=HBM,
            scratch_shapes=[
                pltpu.VMEM((tracers, levels, rows, width), f32),
                pltpu.VMEM((4, lines, width), f32),
                pltpu.SemaphoreType.DMA((4,)),
                pltpu.SemaphoreType.DMA((parts,)),
            ],
            compiler_params=PARAMS,
            name="rims",
        )(seam_codes, inside, wet_levels, *map(in_hbm, beyond))

    def across(up, down):
        return lax.ppermute(up, "face", upward), lax.ppermute(down, "face", downward)

    basis, sums, mark = pl.pallas_call(
        basis_kernel,
        out_shape=(
            ext,
            pltpu.HBM((count, SUBLANES, LANES), f32),
            pltpu.HBM((SUBLANES, LANES), f32),
        ),
        in_specs=[SMEM] + [VMEM] * 4,
        out_specs=(VMEM, VMEM, HBM),
        compiler_params=PARAMS,
        name="surface_basis",
    )(seam_codes, eta_adjoint, surface_damping, below, above)
    sums = lax.all_to_all(sums, "face", 0, 0)

    solved, up1, down1, edges = columns_after(in_hbm(mark), pltpu.VMEM)
    south1, north1 = across(up1, down1)
    sums, south1, north1 = lax.optimization_barrier((sums, south1, north1))

    surface, up0, down0, sound = pl.pallas_call(
        surface_kernel,
        out_shape=(tile, line, line, jax.ShapeDtypeStruct((1,), jnp.int32)),
        in_specs=[SMEM, VMEM, HBM, HBM],
        out_specs=(VMEM, VMEM, VMEM, SMEM),
        scratch_shapes=[
            pltpu.VMEM((ITERS, 2 * rows, width), f32),
            pltpu.VMEM((4, lines, width), f32),
            pltpu.SemaphoreType.DMA((2,)),
        ],
        compiler_params=PARAMS,
        name="surface",
    )(seam_codes, sums, in_hbm(basis), in_hbm(edges))
    south0, north0 = across(up0, down0)
    inside = inside_of(solved, surface, pltpu.VMEM)

    def by_moments(surface, inside, south0, north0, south1, north1):
        return with_rims(inside, south0, north0, south1, north1), surface

    def by_steps(surface, inside, south0, north0, south1, north1):
        surface = stepwise_surface(eta_adjoint, surface_damping, seam_codes[0] == 1)
        solved, up1, down1, edges = columns_after(in_hbm(mark), jax.ShapeDtypeStruct)
        up0, down0 = pl.pallas_call(
            outer_lines,
            out_shape=(line, line),
            in_specs=[SMEM, VMEM, VMEM],
            out_specs=(VMEM, VMEM),
            compiler_params=PARAMS,
            name="outer_lines",
        )(seam_codes, surface, edges)
        inside = inside_of(solved, surface, jax.ShapeDtypeStruct)
        return with_rims(inside, *across(up0, down0), *across(up1, down1)), surface

    return lax.cond(
        sound[0] == 1, by_moments, by_steps, surface, inside, south0, north0, south1, north1
    )


def solution(mesh):
    placed = (
        P(None, None, "face", "ens"),
        P("face", "ens"),
        P(None, "face", "ens"),
        P(None, "face", "ens"),
        P(None, "face", "ens"),
        P(),
        P("face", None),
        P("face", None),
        P("face"),
    )
    return jax.shard_map(
        shards,
        mesh=mesh,
        in_specs=placed,
        out_specs=(P(None, None, "face", "ens"), P("face", "ens")),
        check_vma=False,
    )
```

```python
import functools
import jax
import jax.numpy as jnp
from jax import lax
from jax.experimental import pallas as pl
from jax.experimental.pallas import tpu as pltpu
from jax.sharding import PartitionSpec as P

ITERS = 4
LANES = 128
SUBLANES = 8
diffusion = 0.1
advection = 0.5

MIDDLE = 4.1
LOSS = 1000.0

SMEM = pl.BlockSpec(memory_space=pltpu.SMEM)
VMEM = pl.BlockSpec(memory_space=pltpu.VMEM)
HBM = pl.BlockSpec(memory_space=pltpu.HBM)
PARAMS = pltpu.CompilerParams(vmem_limit_bytes=24 * 2**20)


def in_hbm(x):
    return pltpu.with_memory_space_constraint(x, pltpu.HBM)


def with_halo(x, sides, width):
    for axis, dim in sides:
        count, length = (lax.axis_size(axis), x.shape[dim])
        up = [(i, (i + 1) % count) for i in range(count)]
        down = [(j, i) for i, j in up]
        last = lax.slice_in_dim(x, length - width, length, axis=dim)
        initial = lax.slice_in_dim(x, 0, width, axis=dim)
        before = lax.ppermute(last, axis, up)
        after = lax.ppermute(initial, axis, down)
        x = jnp.concatenate([before, x, after], axis=dim)
    return x


def raised(block_rows, turned):
    upper_row = block_rows[..., -1:, :]
    upper_row = jnp.where(turned, jnp.flip(upper_row, -1), upper_row)
    return jnp.concatenate([block_rows[..., :-1, :], upper_row], axis=-2)


def settled(block_rows, padded, turned):
    lower_rim = padded[..., :1, :]
    upper_rim = padded[..., -1:, :]
    upper_rim = jnp.where(turned, jnp.flip(upper_rim, -1), upper_rim)
    southern = jnp.concatenate([lower_rim, block_rows[..., :-1, :]], axis=-2)
    northern = jnp.concatenate([block_rows[..., 1:, :], upper_rim], axis=-2)
    return (southern, northern)


def surface_apply(values_in, damping, turned):
    padded = with_halo(raised(values_in, turned), (("face", 0),), 1)
    southern, northern = settled(values_in, padded, turned)
    return (4.0 + damping) * values_in - (
        southern + northern + jnp.roll(values_in, 1, -1) + jnp.roll(values_in, -1, -1)
    )


def stepwise_surface(eta_adjoint, surface_damping, turned):
    surface = jnp.zeros_like(eta_adjoint)
    residual = eta_adjoint
    direction = eta_adjoint
    norm_now = lax.psum(jnp.sum(residual * residual), "face")
    for step in range(ITERS):
        applied = surface_apply(direction, surface_damping, turned)
        step_size = norm_now / lax.psum(jnp.sum(direction * applied), "face")
        surface = surface + step_size * direction
        residual = residual - step_size * applied
        norm_next = lax.psum(jnp.sum(residual * residual), "face")
        direction = residual + norm_next / norm_now * direction
        norm_now = norm_next
    return surface


def flip_lanes(rows):
    width = rows.shape[1]
    back = LANES - 1 - lax.broadcasted_iota(jnp.int32, (SUBLANES, LANES), 1)
    tiles = []
    for start in range(width - LANES, -1, -LANES):
        tiles.append(
            jnp.take_along_axis(
                rows[:, start : start + LANES], back, axis=1, mode="promise_in_bounds"
            )
        )
    return jnp.concatenate(tiles, axis=1)


def chunks_of(levels, size):
    return [(k, min(size, levels - k)) for k in range(0, levels, size)]


def flip_some(rows):
    height, width = rows.shape
    if height < SUBLANES:
        rows = jnp.concatenate([rows, jnp.zeros((SUBLANES - height, width), rows.dtype)], axis=0)
    return flip_lanes(rows)[:height]


def outer_kernel(seam, eta, damping, up, down, own, mark):
    half = SUBLANES // 2
    own[:SUBLANES, :] = eta[...]
    own[SUBLANES:, :] = damping[...]
    down[:half, :] = eta[:half, :]
    down[half:, :] = damping[:half, :]
    up[:half, :] = eta[half:, :]
    up[half:, :] = damping[half:, :]

    @pl.when(seam[0] == 1)
    def _():
        up[...] = flip_lanes(up[...])


def basis_kernel(seam, own_rows, below, above, basis, sums):
    half = SUBLANES // 2
    rows = 2 * SUBLANES
    beyond = above[...]
    beyond = jnp.where(seam[0] == 1, flip_lanes(beyond), beyond)
    width = beyond.shape[1]
    v = jnp.concatenate([below[:half, :], own_rows[:SUBLANES, :], beyond[:half, :]], axis=0)
    d = jnp.concatenate([below[half:, :], own_rows[SUBLANES:, :], beyond[half:, :]], axis=0)
    d = (d + (4.0 - MIDDLE)) * (1.0 / MIDDLE)
    vectors = [v]
    for j in range(ITERS):
        now = vectors[-1]
        near = (
            pltpu.roll(now, 1, 0)
            + pltpu.roll(now, rows - 1, 0)
            + pltpu.roll(now, 1, 1)
            + pltpu.roll(now, width - 1, 1)
        )
        image = d * now - near * (1.0 / MIDDLE)
        vectors.append(image if j == 0 else 2.0 * image - vectors[-2])
    for j in range(ITERS):
        basis[j] = vectors[j]
    row = lax.broadcasted_iota(jnp.int32, (rows, LANES), 0)
    own = (row >= half) & (row < half + SUBLANES)
    parts = []
    for j in range(2 * ITERS):
        product = vectors[j // 2] * vectors[j // 2 + j % 2]
        total = product[:, :LANES]
        for start in range(LANES, width, LANES):
            total = total + product[:, start : start + LANES]
        parts.append(jnp.sum(jnp.where(own, total, 0.0), axis=0, keepdims=True))
    tile = jnp.concatenate(parts, axis=0)
    for i in range(sums.shape[0]):
        sums[i] = tile


def coefficients(moments):
    def dot(a, b):
        total = None
        for i, x in enumerate(a):
            for j, y in enumerate(b):
                term = x * y * (moments[i + j] + moments[abs(i - j)])
                total = term if total is None else total + term
        return 0.5 * total

    def image(p):
        q = [MIDDLE * x for x in p] + [jnp.zeros_like(p[0])]
        for i, x in enumerate(p):
            if i == 0:
                q[1] = q[1] + MIDDLE * x
            else:
                q[i + 1] = q[i + 1] + (0.5 * MIDDLE) * x
                q[i - 1] = q[i - 1] + (0.5 * MIDDLE) * x
        return q

    def size(p):
        return functools.reduce(lambda a, b: a + b, [jnp.abs(x) for x in p])

    def plus(a, b):
        return [x + y for x, y in zip(a, b)] + list(a[len(b) :]) + list(b[len(a) :])

    norm_first = moments[0]
    p = [jnp.ones_like(norm_first)]
    r = p
    norm_now = norm_first
    s = []
    sound = norm_first > 0.0
    for step in range(ITERS):
        q = image(p)
        curve = dot(p, q)
        sound = sound & (curve * LOSS >= size(p) * size(q) * norm_first)
        rate = norm_now / curve
        s = plus(s, [rate * x for x in p])
        if step < ITERS - 1:
            r = plus(r, [-rate * x for x in q])
            norm_next = dot(r, r)
            sound = sound & (norm_next * LOSS >= size(r) * size(r) * norm_first)
            ratio = norm_next / norm_now
            p = plus(r, [ratio * x for x in p])
            norm_now = norm_next
    return s, sound


def outer_lines(seam, fields, edges, up, down):
    turned = seam[0] == 1
    for k in range(0, up.shape[0], SUBLANES):
        at = slice(k, k + SUBLANES)
        top = edges[0, at, :] + fields[SUBLANES - 1 : SUBLANES, :] * edges[1, at, :]
        up[at, :] = jnp.where(turned, flip_lanes(top), top)
        down[at, :] = edges[2, at, :] + fields[:1, :] * edges[3, at, :]


def surface_kernel(seam, sums, basis, edges, surface, up, down, sound):
    half = SUBLANES // 2
    parts = [sums[i] for i in range(sums.shape[0])]
    while len(parts) > 1:
        pairs = [a + b for a, b in zip(parts[::2], parts[1::2])]
        parts = pairs + parts[len(parts) - len(parts) % 2 :]
    total = jnp.sum(parts[0], axis=1, keepdims=True)
    raw = [total[j : j + 1, :] for j in range(2 * ITERS)]
    moments = raw[:2]
    for j in range(2, 2 * ITERS):
        moments.append(2.0 * raw[j] - raw[j % 2])
    s, good = coefficients(moments)
    value = s[0] * basis[0]
    for j in range(1, ITERS):
        value = value + s[j] * basis[j]
    surface[...] = value[half : half + SUBLANES, :]
    sound[0] = jnp.where(good, 1, 0)[0, 0]
    outer_lines(seam, surface, edges, up, down)


CHUNK = 10


def column_kernel(
    seam, thickness_from, tracer, mixing, velocity_y, wet, after, solved, up, down, edges,
    thickness, depth_at, tracer_at, mixing_at, velocity_at, ratio_at, sems,
):
    levels = tracer.shape[1]
    chunks = chunks_of(levels, CHUNK)
    few = [
        pltpu.make_async_copy(thickness_from, thickness, sems.at[2, 1]),
        pltpu.make_async_copy(wet, depth_at, sems.at[2, 2]),
    ]
    loads = []
    for i, (k, n) in enumerate(chunks):
        m = min(n, levels - 1 - k)
        loads.append((
            pltpu.make_async_copy(
                mixing.at[pl.ds(k, m)], mixing_at.at[pl.ds(k, m)], sems.at[1, i]
            ),
            pltpu.make_async_copy(
                tracer.at[:, pl.ds(k, n)], tracer_at.at[:, pl.ds(k, n)], sems.at[0, i]
            ),
        ))
    velocity_load = pltpu.make_async_copy(velocity_y, velocity_at, sems.at[2, 0])
    for pair in [few] + loads:
        pair[0].start()
        pair[1].start()
    velocity_load.start()

    few[0].wait()
    few[1].wait()
    depth = depth_at[...]
    zero = jnp.zeros(depth.shape, jnp.float32)

    def forward(k, carry):
        c_before, g_before, y0, y1, y2 = carry
        th = thickness[k]
        c = jnp.where(k + 1 < depth, mixing_at[jnp.minimum(k, levels - 2)], 0.0)
        inverse = 1.0 / (th + c + c_before * (1.0 - g_before))
        g = c * inverse
        y0 = (tracer_at[0, k] + c_before * y0) * inverse
        y1 = (tracer_at[1, k] + c_before * y1) * inverse
        y2 = (jnp.where(k < depth, th, 0.0) + c_before * y2) * inverse
        ratio_at[k] = g
        solved[0, k] = y0
        solved[1, k] = y1
        solved[2, k] = y2
        return c, g, y0, y1, y2

    carry = (zero,) * 5
    for i, (k, n) in enumerate(chunks):
        loads[i][0].wait()
        loads[i][1].wait()
        carry = lax.fori_loop(k, k + n, forward, carry, unroll=5)

    carry = (zero,) * 3
    for i, (k, n) in reversed(list(enumerate(chunks))):

        def backward(j, carry, last=k + n - 1):
            level = last - j
            th = thickness[level]
            g = ratio_at[level]
            after = []
            for t in range(3):
                u = solved[t, level] + g * carry[t]
                solved[t, level] = th * u
                after.append(u)
            return tuple(after)

        carry = lax.fori_loop(0, n, backward, carry, unroll=5)

    velocity_load.wait()
    turned = seam[0] == 1
    for k, n in chunks_of(levels, SUBLANES):
        at = slice(k, k + n)
        to_up = diffusion - advection * velocity_at[pl.ds(k, n), SUBLANES - 1, :]
        to_down = diffusion + advection * velocity_at[pl.ds(k, n), 0, :]
        top = solved[1, pl.ds(k, n), SUBLANES - 1, :] * to_up
        up[at, :] = jnp.where(turned, flip_some(top), top)
        down[at, :] = solved[1, pl.ds(k, n), 0, :] * to_down
        for t in range(2):
            edges[t, at, :] = solved[2 * t, pl.ds(k, n), SUBLANES - 1, :] * to_up
            edges[2 + t, at, :] = solved[2 * t, pl.ds(k, n), 0, :] * to_down


def inside_kernel(solved, velocity_x, velocity_y, wet, surface, result):
    levels = velocity_x.shape[0]
    width = wet.shape[1]
    depth = wet[...]
    s = surface[...]
    row = lax.broadcasted_iota(jnp.int32, depth.shape, 0)
    is_south = row == 0
    is_north = row == SUBLANES - 1

    def level(k, _):
        flow_x = advection * velocity_x[k]
        flow_y = advection * velocity_y[k]
        to_west = diffusion + flow_x
        to_east = diffusion - flow_x
        to_south = jnp.where(is_south, 0.0, diffusion + flow_y)
        to_north = jnp.where(is_north, 0.0, diffusion - flow_y)
        is_wet = k < depth
        for t in range(2):
            x = solved[t, k]
            if t == 0:
                x = x + s * solved[2, k]
            eastern = pltpu.roll(x * to_west, width - 1, 1)
            western = pltpu.roll(x * to_east, 1, 1)
            northern = pltpu.roll(x * to_south, SUBLANES - 1, 0)
            southern = pltpu.roll(x * to_north, 1, 0)
            value = (1.0 - 4.0 * diffusion) * x + ((eastern + western) + (northern + southern))
            result[t, k] = jnp.where(is_wet, value, 0.0)
        return 0

    lax.fori_loop(0, levels, level, 0, unroll=5)


def rim_kernel(seam, inside, wet, south0, north0, south1, north1, result, result_at, out_sems):
    levels = inside.shape[1]
    width = wet.shape[1]
    turned = seam[0] == 1
    depth_south = wet[:1, :]
    depth_north = wet[SUBLANES - 1 :, :]
    stores = []
    for i, (k, n) in enumerate(chunks_of(levels, SUBLANES)):
        at = pl.ds(k, n)
        index = k + lax.broadcasted_iota(jnp.int32, (n, width), 0)
        result_at[:, at] = inside[:, at]
        for t, (south_from, north_from) in enumerate(((south0, north0), (south1, north1))):
            south = south_from[k : k + n, :]
            north = north_from[k : k + n, :]
            north = jnp.where(turned, flip_some(north), north)
            result_at[t, at, 0, :] += jnp.where(index < depth_south, south, 0.0)
            result_at[t, at, SUBLANES - 1, :] += jnp.where(index < depth_north, north, 0.0)
        stores.append(pltpu.make_async_copy(result_at.at[:, at], result.at[:, at], out_sems.at[i]))
        stores[-1].start()
    for store in stores:
        store.wait()


def shards(
    tracer_adjoint,
    eta_adjoint,
    velocity_x,
    velocity_y,
    mixing,
    thickness,
    surface_damping,
    wet_levels,
    seam_codes,
):
    tracers, levels, rows, width = tracer_adjoint.shape
    f32 = jnp.float32
    count = lax.axis_size("face")
    upward = [(i, (i + 1) % count) for i in range(count)]
    downward = [(j, i) for i, j in upward]
    tile = jax.ShapeDtypeStruct((rows, width), f32)
    ext = pltpu.VMEM((ITERS, 2 * rows, width), f32)
    lines = -(-levels // SUBLANES) * SUBLANES
    line = jax.ShapeDtypeStruct((lines, width), f32)

    up, down, own, mark = pl.pallas_call(
        outer_kernel,
        out_shape=(
            tile,
            tile,
            pltpu.VMEM((2 * rows, width), f32),
            pltpu.HBM((SUBLANES, LANES), f32),
        ),
        in_specs=[SMEM, VMEM, VMEM],
        out_specs=(VMEM, VMEM, VMEM, HBM),
        name="outer_rows",
    )(seam_codes, eta_adjoint, surface_damping)
    below = lax.ppermute(up, "face", upward)
    above = lax.ppermute(down, "face", downward)

    cube = pltpu.VMEM((levels, rows, width), f32)
    chunks = len(chunks_of(levels, CHUNK))
    parts = len(chunks_of(levels, SUBLANES))
    inputs = [in_hbm(x) for x in (thickness, tracer_adjoint, mixing, velocity_y, wet_levels)]

    def columns_after(mark, place):
        return pl.pallas_call(
            column_kernel,
            out_shape=(
                place((3, levels, rows, width), f32),
                line,
                line,
                place((4, lines, width), f32),
            ),
            in_specs=[SMEM] + [HBM] * 6,
            out_specs=(VMEM, VMEM, VMEM, VMEM),
            scratch_shapes=[
                pltpu.SMEM((levels,), f32),
                pltpu.VMEM((rows, width), jnp.int32),
                pltpu.VMEM((tracers, levels, rows, width), f32),
                cube,
                cube,
                cube,
                pltpu.SemaphoreType.DMA((3, max(chunks, 3))),
            ],
            compiler_params=PARAMS,
            cost_estimate=pl.CostEstimate(
                flops=40000000, bytes_accessed=13000000, transcendentals=0
            ),
            name="columns",
        )(seam_codes, *inputs, mark)

    def inside_of(solved, surface, place):
        return pl.pallas_call(
            inside_kernel,
            out_shape=place((tracers, levels, rows, width), f32),
            in_specs=[VMEM] * 5,
            out_specs=VMEM,
            compiler_params=PARAMS,
            cost_estimate=pl.CostEstimate(flops=1000, bytes_accessed=1000, transcendentals=0),
            name="inside",
        )(solved, velocity_x, velocity_y, wet_levels, surface)

    def with_rims(inside, *beyond):
        return pl.pallas_call(
            rim_kernel,
            out_shape=pltpu.HBM((tracers, levels, rows, width), f32),
            in_specs=[SMEM] + [VMEM] * 6,
            out_specs=HBM,
            scratch_shapes=[
                pltpu.VMEM((tracers, levels, rows, width), f32),
                pltpu.SemaphoreType.DMA((parts,)),
            ],
            compiler_params=PARAMS,
            name="rims",
        )(seam_codes, inside, wet_levels, *beyond)

    def across(up, down):
        return lax.ppermute(up, "face", upward), lax.ppermute(down, "face", downward)

    basis, sums = pl.pallas_call(
        basis_kernel,
        out_shape=(
            ext,
            jax.ShapeDtypeStruct((count, SUBLANES, LANES), f32),
        ),
        in_specs=[SMEM] + [VMEM] * 3,
        out_specs=(VMEM, VMEM),
        compiler_params=PARAMS,
        name="surface_basis",
    )(seam_codes, own, below, above)
    sums = lax.all_to_all(sums, "face", 0, 0)

    solved, up1, down1, edges = columns_after(in_hbm(mark), pltpu.VMEM)
    south1, north1 = across(up1, down1)
    sums, south1, north1 = lax.optimization_barrier((sums, south1, north1))

    surface, up0, down0, sound = pl.pallas_call(
        surface_kernel,
        out_shape=(tile, line, line, jax.ShapeDtypeStruct((1,), jnp.int32)),
        in_specs=[SMEM, VMEM, VMEM, VMEM],
        out_specs=(VMEM, VMEM, VMEM, SMEM),
        compiler_params=PARAMS,
        name="surface",
    )(seam_codes, sums, basis, edges)
    south0, north0 = across(up0, down0)
    inside = inside_of(solved, surface, pltpu.VMEM)

    def by_moments(surface, inside, south0, north0, south1, north1):
        return with_rims(inside, south0, north0, south1, north1), surface

    def by_steps(surface, inside, south0, north0, south1, north1):
        surface = stepwise_surface(eta_adjoint, surface_damping, seam_codes[0] == 1)
        solved, up1, down1, edges = columns_after(in_hbm(mark), jax.ShapeDtypeStruct)
        up0, down0 = pl.pallas_call(
            outer_lines,
            out_shape=(line, line),
            in_specs=[SMEM, VMEM, VMEM],
            out_specs=(VMEM, VMEM),
            compiler_params=PARAMS,
            name="outer_lines",
        )(seam_codes, surface, edges)
        inside = inside_of(solved, surface, jax.ShapeDtypeStruct)
        return with_rims(inside, *across(up0, down0), *across(up1, down1)), surface

    return lax.cond(
        sound[0] == 1, by_moments, by_steps, surface, inside, south0, north0, south1, north1
    )


def solution(mesh):
    placed = (
        P(None, None, "face", "ens"),
        P("face", "ens"),
        P(None, "face", "ens"),
        P(None, "face", "ens"),
        P(None, "face", "ens"),
        P(),
        P("face", None),
        P("face", None),
        P("face"),
    )
    return jax.shard_map(
        shards,
        mesh=mesh,
        in_specs=placed,
        out_specs=(P(None, None, "face", "ens"), P("face", "ens")),
        check_vma=False,
    )
```

```python
import functools
import jax
import jax.numpy as jnp
from jax import lax
from jax.experimental import pallas as pl
from jax.experimental.pallas import tpu as pltpu
from jax.sharding import PartitionSpec as P

ITERS = 4
LANES = 128
SUBLANES = 8
diffusion = 0.1
advection = 0.5

MIDDLE = 4.1
LOSS = 1000.0

SMEM = pl.BlockSpec(memory_space=pltpu.SMEM)
VMEM = pl.BlockSpec(memory_space=pltpu.VMEM)
HBM = pl.BlockSpec(memory_space=pltpu.HBM)
PARAMS = pltpu.CompilerParams(vmem_limit_bytes=24 * 2**20)


def in_hbm(x):
    return pltpu.with_memory_space_constraint(x, pltpu.HBM)


def with_halo(x, sides, width):
    for axis, dim in sides:
        count, length = (lax.axis_size(axis), x.shape[dim])
        up = [(i, (i + 1) % count) for i in range(count)]
        down = [(j, i) for i, j in up]
        last = lax.slice_in_dim(x, length - width, length, axis=dim)
        initial = lax.slice_in_dim(x, 0, width, axis=dim)
        before = lax.ppermute(last, axis, up)
        after = lax.ppermute(initial, axis, down)
        x = jnp.concatenate([before, x, after], axis=dim)
    return x


def raised(block_rows, turned):
    upper_row = block_rows[..., -1:, :]
    upper_row = jnp.where(turned, jnp.flip(upper_row, -1), upper_row)
    return jnp.concatenate([block_rows[..., :-1, :], upper_row], axis=-2)


def settled(block_rows, padded, turned):
    lower_rim = padded[..., :1, :]
    upper_rim = padded[..., -1:, :]
    upper_rim = jnp.where(turned, jnp.flip(upper_rim, -1), upper_rim)
    southern = jnp.concatenate([lower_rim, block_rows[..., :-1, :]], axis=-2)
    northern = jnp.concatenate([block_rows[..., 1:, :], upper_rim], axis=-2)
    return (southern, northern)


def surface_apply(values_in, damping, turned):
    padded = with_halo(raised(values_in, turned), (("face", 0),), 1)
    southern, northern = settled(values_in, padded, turned)
    return (4.0 + damping) * values_in - (
        southern + northern + jnp.roll(values_in, 1, -1) + jnp.roll(values_in, -1, -1)
    )


def stepwise_surface(eta_adjoint, surface_damping, turned):
    surface = jnp.zeros_like(eta_adjoint)
    residual = eta_adjoint
    direction = eta_adjoint
    norm_now = lax.psum(jnp.sum(residual * residual), "face")
    for step in range(ITERS):
        applied = surface_apply(direction, surface_damping, turned)
        step_size = norm_now / lax.psum(jnp.sum(direction * applied), "face")
        surface = surface + step_size * direction
        residual = residual - step_size * applied
        norm_next = lax.psum(jnp.sum(residual * residual), "face")
        direction = residual + norm_next / norm_now * direction
        norm_now = norm_next
    return surface


def flip_lanes(rows):
    width = rows.shape[1]
    back = LANES - 1 - lax.broadcasted_iota(jnp.int32, (SUBLANES, LANES), 1)
    tiles = []
    for start in range(width - LANES, -1, -LANES):
        tiles.append(
            jnp.take_along_axis(
                rows[:, start : start + LANES], back, axis=1, mode="promise_in_bounds"
            )
        )
    return jnp.concatenate(tiles, axis=1)


def chunks_of(levels, size):
    return [(k, min(size, levels - k)) for k in range(0, levels, size)]


def flip_some(rows):
    height, width = rows.shape
    if height < SUBLANES:
        rows = jnp.concatenate([rows, jnp.zeros((SUBLANES - height, width), rows.dtype)], axis=0)
    return flip_lanes(rows)[:height]


def outer_kernel(seam, eta, damping, up, down, own, mark):
    half = SUBLANES // 2
    own[:SUBLANES, :] = eta[...]
    own[SUBLANES:, :] = damping[...]
    down[:half, :] = eta[:half, :]
    down[half:, :] = damping[:half, :]
    up[:half, :] = eta[half:, :]
    up[half:, :] = damping[half:, :]

    @pl.when(seam[0] == 1)
    def _():
        up[...] = flip_lanes(up[...])


def basis_kernel(seam, own_rows, below, above, basis, sums):
    half = SUBLANES // 2
    rows = 2 * SUBLANES
    beyond = above[...]
    beyond = jnp.where(seam[0] == 1, flip_lanes(beyond), beyond)
    width = beyond.shape[1]
    v = jnp.concatenate([below[:half, :], own_rows[:SUBLANES, :], beyond[:half, :]], axis=0)
    d = jnp.concatenate([below[half:, :], own_rows[SUBLANES:, :], beyond[half:, :]], axis=0)
    d = (d + (4.0 - MIDDLE)) * (1.0 / MIDDLE)
    vectors = [v]
    for j in range(ITERS):
        now = vectors[-1]
        near = (
            pltpu.roll(now, 1, 0)
            + pltpu.roll(now, rows - 1, 0)
            + pltpu.roll(now, 1, 1)
            + pltpu.roll(now, width - 1, 1)
        )
        image = d * now - near * (1.0 / MIDDLE)
        vectors.append(image if j == 0 else 2.0 * image - vectors[-2])
    for j in range(ITERS):
        basis[j] = vectors[j]
    row = lax.broadcasted_iota(jnp.int32, (rows, LANES), 0)
    own = (row >= half) & (row < half + SUBLANES)
    parts = []
    for j in range(2 * ITERS):
        product = vectors[j // 2] * vectors[j // 2 + j % 2]
        total = product[:, :LANES]
        for start in range(LANES, width, LANES):
            total = total + product[:, start : start + LANES]
        parts.append(jnp.sum(jnp.where(own, total, 0.0), axis=0, keepdims=True))
    tile = jnp.concatenate(parts, axis=0)
    for i in range(sums.shape[0]):
        sums[i] = tile


def coefficients(moments):
    def dot(a, b):
        total = None
        for i, x in enumerate(a):
            for j, y in enumerate(b):
                term = x * y * (moments[i + j] + moments[abs(i - j)])
                total = term if total is None else total + term
        return 0.5 * total

    def image(p):
        q = [MIDDLE * x for x in p] + [jnp.zeros_like(p[0])]
        for i, x in enumerate(p):
            if i == 0:
                q[1] = q[1] + MIDDLE * x
            else:
                q[i + 1] = q[i + 1] + (0.5 * MIDDLE) * x
                q[i - 1] = q[i - 1] + (0.5 * MIDDLE) * x
        return q

    def size(p):
        return functools.reduce(lambda a, b: a + b, [jnp.abs(x) for x in p])

    def plus(a, b):
        return [x + y for x, y in zip(a, b)] + list(a[len(b) :]) + list(b[len(a) :])

    norm_first = moments[0]
    p = [jnp.ones_like(norm_first)]
    r = p
    norm_now = norm_first
    s = []
    sound = norm_first > 0.0
    for step in range(ITERS):
        q = image(p)
        curve = dot(p, q)
        sound = sound & (curve * LOSS >= size(p) * size(q) * norm_first)
        rate = norm_now / curve
        s = plus(s, [rate * x for x in p])
        if step < ITERS - 1:
            r = plus(r, [-rate * x for x in q])
            norm_next = dot(r, r)
            sound = sound & (norm_next * LOSS >= size(r) * size(r) * norm_first)
            ratio = norm_next / norm_now
            p = plus(r, [ratio * x for x in p])
            norm_now = norm_next
    return s, sound


def outer_lines(seam, fields, edges, up, down):
    turned = seam[0] == 1
    for k in range(0, up.shape[0], SUBLANES):
        at = slice(k, k + SUBLANES)
        top = edges[0, at, :] + fields[SUBLANES - 1 : SUBLANES, :] * edges[1, at, :]
        up[at, :] = jnp.where(turned, flip_lanes(top), top)
        down[at, :] = edges[2, at, :] + fields[:1, :] * edges[3, at, :]


def surface_kernel(seam, sums, basis, edges, surface, up, down, sound):
    half = SUBLANES // 2
    parts = [sums[i] for i in range(sums.shape[0])]
    while len(parts) > 1:
        pairs = [a + b for a, b in zip(parts[::2], parts[1::2])]
        parts = pairs + parts[len(parts) - len(parts) % 2 :]
    total = jnp.sum(parts[0], axis=1, keepdims=True)
    raw = [total[j : j + 1, :] for j in range(2 * ITERS)]
    moments = raw[:2]
    for j in range(2, 2 * ITERS):
        moments.append(2.0 * raw[j] - raw[j % 2])
    s, good = coefficients(moments)
    value = s[0] * basis[0]
    for j in range(1, ITERS):
        value = value + s[j] * basis[j]
    surface[...] = value[half : half + SUBLANES, :]
    sound[0] = jnp.where(good, 1, 0)[0, 0]
    outer_lines(seam, surface, edges, up, down)


CHUNK = 10


def column_kernel(
    seam, thickness_from, tracer, mixing, velocity_y, wet, after, solved, up, down, edges,
    thickness, depth_at, tracer_at, mixing_at, velocity_at, ratio_at, sems,
):
    levels = tracer.shape[1]
    chunks = chunks_of(levels, CHUNK)
    few = [
        pltpu.make_async_copy(thickness_from, thickness, sems.at[2, 1]),
        pltpu.make_async_copy(wet, depth_at, sems.at[2, 2]),
    ]
    loads = []
    for i, (k, n) in enumerate(chunks):
        m = min(n, levels - 1 - k)
        loads.append((
            pltpu.make_async_copy(
                mixing.at[pl.ds(k, m)], mixing_at.at[pl.ds(k, m)], sems.at[1, i]
            ),
            pltpu.make_async_copy(
                tracer.at[:, pl.ds(k, n)], tracer_at.at[:, pl.ds(k, n)], sems.at[0, i]
            ),
        ))
    velocity_load = pltpu.make_async_copy(velocity_y, velocity_at, sems.at[2, 0])
    for pair in [few] + loads:
        pair[0].start()
        pair[1].start()
    velocity_load.start()

    few[0].wait()
    few[1].wait()
    depth = depth_at[...]
    zero = jnp.zeros(depth.shape, jnp.float32)

    def forward(k, carry):
        c_before, g_before, y0, y1, y2 = carry
        th = thickness[k]
        c = jnp.where(k + 1 < depth, mixing_at[jnp.minimum(k, levels - 2)], 0.0)
        inverse = 1.0 / (th + c + c_before * (1.0 - g_before))
        g = c * inverse
        y0 = (tracer_at[0, k] + c_before * y0) * inverse
        y1 = (tracer_at[1, k] + c_before * y1) * inverse
        y2 = (jnp.where(k < depth, th, 0.0) + c_before * y2) * inverse
        ratio_at[k] = g
        solved[0, k] = y0
        solved[1, k] = y1
        solved[2, k] = y2
        return c, g, y0, y1, y2

    carry = (zero,) * 5
    for i, (k, n) in enumerate(chunks):
        loads[i][0].wait()
        loads[i][1].wait()
        carry = lax.fori_loop(k, k + n, forward, carry, unroll=5)

    carry = (zero,) * 3
    for i, (k, n) in reversed(list(enumerate(chunks))):

        def backward(j, carry, last=k + n - 1):
            level = last - j
            th = thickness[level]
            g = ratio_at[level]
            after = []
            for t in range(3):
                u = solved[t, level] + g * carry[t]
                solved[t, level] = th * u
                after.append(u)
            return tuple(after)

        carry = lax.fori_loop(0, n, backward, carry, unroll=5)

    velocity_load.wait()
    turned = seam[0] == 1
    for k, n in chunks_of(levels, SUBLANES):
        at = slice(k, k + n)
        to_up = diffusion - advection * velocity_at[pl.ds(k, n), SUBLANES - 1, :]
        to_down = diffusion + advection * velocity_at[pl.ds(k, n), 0, :]
        top = solved[1, pl.ds(k, n), SUBLANES - 1, :] * to_up
        up[at, :] = jnp.where(turned, flip_some(top), top)
        down[at, :] = solved[1, pl.ds(k, n), 0, :] * to_down
        for t in range(2):
            edges[t, at, :] = solved[2 * t, pl.ds(k, n), SUBLANES - 1, :] * to_up
            edges[2 + t, at, :] = solved[2 * t, pl.ds(k, n), 0, :] * to_down


def inside_kernel(solved, velocity_x, velocity_y, wet, surface, result):
    levels = velocity_x.shape[0]
    width = wet.shape[1]
    depth = wet[...]
    s = surface[...]
    row = lax.broadcasted_iota(jnp.int32, depth.shape, 0)
    is_south = row == 0
    is_north = row == SUBLANES - 1

    def level(k, _):
        flow_x = advection * velocity_x[k]
        flow_y = advection * velocity_y[k]
        to_west = diffusion + flow_x
        to_east = diffusion - flow_x
        to_south = jnp.where(is_south, 0.0, diffusion + flow_y)
        to_north = jnp.where(is_north, 0.0, diffusion - flow_y)
        is_wet = k < depth
        for t in range(2):
            x = solved[t, k]
            if t == 0:
                x = x + s * solved[2, k]
            eastern = pltpu.roll(x * to_west, width - 1, 1)
            western = pltpu.roll(x * to_east, 1, 1)
            northern = pltpu.roll(x * to_south, SUBLANES - 1, 0)
            southern = pltpu.roll(x * to_north, 1, 0)
            value = (1.0 - 4.0 * diffusion) * x + ((eastern + western) + (northern + southern))
            result[t, k] = jnp.where(is_wet, value, 0.0)
        return 0

    lax.fori_loop(0, levels, level, 0, unroll=5)


def rim_kernel(seam, inside, wet, south0, north0, south1, north1, result, result_at, out_sems):
    levels = inside.shape[1]
    width = wet.shape[1]
    turned = seam[0] == 1
    depth_south = wet[:1, :]
    depth_north = wet[SUBLANES - 1 :, :]
    stores = []
    for i, (k, n) in enumerate(chunks_of(levels, SUBLANES)):
        at = pl.ds(k, n)
        index = k + lax.broadcasted_iota(jnp.int32, (n, width), 0)
        result_at[:, at] = inside[:, at]
        for t, (south_from, north_from) in enumerate(((south0, north0), (south1, north1))):
            south = south_from[k : k + n, :]
            north = north_from[k : k + n, :]
            north = jnp.where(turned, flip_some(north), north)
            result_at[t, at, 0, :] += jnp.where(index < depth_south, south, 0.0)
            result_at[t, at, SUBLANES - 1, :] += jnp.where(index < depth_north, north, 0.0)
        stores.append(pltpu.make_async_copy(result_at.at[:, at], result.at[:, at], out_sems.at[i]))
        stores[-1].start()
    for store in stores:
        store.wait()


def shards(
    tracer_adjoint,
    eta_adjoint,
    velocity_x,
    velocity_y,
    mixing,
    thickness,
    surface_damping,
    wet_levels,
    seam_codes,
):
    tracers, levels, rows, width = tracer_adjoint.shape
    f32 = jnp.float32
    count = lax.axis_size("face")
    upward = [(i, (i + 1) % count) for i in range(count)]
    downward = [(j, i) for i, j in upward]
    tile = jax.ShapeDtypeStruct((rows, width), f32)
    ext = pltpu.VMEM((ITERS, 2 * rows, width), f32)
    lines = -(-levels // SUBLANES) * SUBLANES
    line = jax.ShapeDtypeStruct((lines, width), f32)

    up, down, own, mark = pl.pallas_call(
        outer_kernel,
        out_shape=(
            tile,
            tile,
            pltpu.VMEM((2 * rows, width), f32),
            pltpu.HBM((SUBLANES, LANES), f32),
        ),
        in_specs=[SMEM, VMEM, VMEM],
        out_specs=(VMEM, VMEM, VMEM, HBM),
        name="outer_rows",
    )(seam_codes, eta_adjoint, surface_damping)
    below = lax.ppermute(up, "face", upward)
    above = lax.ppermute(down, "face", downward)

    cube = pltpu.VMEM((levels, rows, width), f32)
    chunks = len(chunks_of(levels, CHUNK))
    parts = len(chunks_of(levels, SUBLANES))
    inputs = [in_hbm(x) for x in (thickness, tracer_adjoint, mixing, velocity_y, wet_levels)]

    def columns_after(mark, place):
        return pl.pallas_call(
            column_kernel,
            out_shape=(
                place((3, levels, rows, width), f32),
                line,
                line,
                place((4, lines, width), f32),
            ),
            in_specs=[SMEM] + [HBM] * 6,
            out_specs=(VMEM, VMEM, VMEM, VMEM),
            scratch_shapes=[
                pltpu.SMEM((levels,), f32),
                pltpu.VMEM((rows, width), jnp.int32),
                pltpu.VMEM((tracers, levels, rows, width), f32),
                cube,
                cube,
                cube,
                pltpu.SemaphoreType.DMA((3, max(chunks, 3))),
            ],
            compiler_params=PARAMS,
            cost_estimate=pl.CostEstimate(
                flops=40000000, bytes_accessed=13000000, transcendentals=0
            ),
            name="columns",
        )(seam_codes, *inputs, mark)

    def inside_of(solved, surface, place):
        return pl.pallas_call(
            inside_kernel,
            out_shape=place((tracers, levels, rows, width), f32),
            in_specs=[VMEM] * 5,
            out_specs=VMEM,
            compiler_params=PARAMS,
            cost_estimate=pl.CostEstimate(flops=1000, bytes_accessed=1000, transcendentals=0),
            name="inside",
        )(solved, velocity_x, velocity_y, wet_levels, surface)

    def with_rims(inside, *beyond):
        return pl.pallas_call(
            rim_kernel,
            out_shape=pltpu.HBM((tracers, levels, rows, width), f32),
            in_specs=[SMEM] + [VMEM] * 6,
            out_specs=HBM,
            scratch_shapes=[
                pltpu.VMEM((tracers, levels, rows, width), f32),
                pltpu.SemaphoreType.DMA((parts,)),
            ],
            compiler_params=PARAMS,
            name="rims",
        )(seam_codes, inside, wet_levels, *beyond)

    def across(up, down):
        return lax.ppermute(up, "face", upward), lax.ppermute(down, "face", downward)

    basis, sums = pl.pallas_call(
        basis_kernel,
        out_shape=(
            ext,
            jax.ShapeDtypeStruct((count, SUBLANES, LANES), f32),
        ),
        in_specs=[SMEM] + [VMEM] * 3,
        out_specs=(VMEM, VMEM),
        compiler_params=PARAMS,
        name="surface_basis",
    )(seam_codes, own, below, above)
    solved, up1, down1, edges = columns_after(in_hbm(mark), pltpu.VMEM)
    sums, up1, down1 = lax.optimization_barrier((sums, up1, down1))
    sums = lax.all_to_all(sums, "face", 0, 0)
    south1, north1 = across(up1, down1)
    sums, south1, north1 = lax.optimization_barrier((sums, south1, north1))

    surface, up0, down0, sound = pl.pallas_call(
        surface_kernel,
        out_shape=(tile, line, line, jax.ShapeDtypeStruct((1,), jnp.int32)),
        in_specs=[SMEM, VMEM, VMEM, VMEM],
        out_specs=(VMEM, VMEM, VMEM, SMEM),
        compiler_params=PARAMS,
        name="surface",
    )(seam_codes, sums, basis, edges)
    south0, north0 = across(up0, down0)
    inside = inside_of(solved, surface, pltpu.VMEM)

    def by_moments(surface, inside, south0, north0, south1, north1):
        return with_rims(inside, south0, north0, south1, north1), surface

    def by_steps(surface, inside, south0, north0, south1, north1):
        surface = stepwise_surface(eta_adjoint, surface_damping, seam_codes[0] == 1)
        solved, up1, down1, edges = columns_after(in_hbm(mark), jax.ShapeDtypeStruct)
        up0, down0 = pl.pallas_call(
            outer_lines,
            out_shape=(line, line),
            in_specs=[SMEM, VMEM, VMEM],
            out_specs=(VMEM, VMEM),
            compiler_params=PARAMS,
            name="outer_lines",
        )(seam_codes, surface, edges)
        inside = inside_of(solved, surface, jax.ShapeDtypeStruct)
        return with_rims(inside, *across(up0, down0), *across(up1, down1)), surface

    return lax.cond(
        sound[0] == 1, by_moments, by_steps, surface, inside, south0, north0, south1, north1
    )


def solution(mesh):
    placed = (
        P(None, None, "face", "ens"),
        P("face", "ens"),
        P(None, "face", "ens"),
        P(None, "face", "ens"),
        P(None, "face", "ens"),
        P(),
        P("face", None),
        P("face", None),
        P("face"),
    )
    return jax.shard_map(
        shards,
        mesh=mesh,
        in_specs=placed,
        out_specs=(P(None, None, "face", "ens"), P("face", "ens")),
        check_vma=False,
    )
```

```python
import functools
import jax
import jax.numpy as jnp
from jax import lax
from jax.experimental import pallas as pl
from jax.experimental.pallas import tpu as pltpu
from jax.sharding import PartitionSpec as P

ITERS = 4
LANES = 128
SUBLANES = 8
diffusion = 0.1
advection = 0.5

MIDDLE = 4.1
LOSS = 1000.0

SMEM = pl.BlockSpec(memory_space=pltpu.SMEM)
VMEM = pl.BlockSpec(memory_space=pltpu.VMEM)
HBM = pl.BlockSpec(memory_space=pltpu.HBM)
PARAMS = pltpu.CompilerParams(vmem_limit_bytes=24 * 2**20)


def in_hbm(x):
    return pltpu.with_memory_space_constraint(x, pltpu.HBM)


def with_halo(x, sides, width):
    for axis, dim in sides:
        count, length = (lax.axis_size(axis), x.shape[dim])
        up = [(i, (i + 1) % count) for i in range(count)]
        down = [(j, i) for i, j in up]
        last = lax.slice_in_dim(x, length - width, length, axis=dim)
        initial = lax.slice_in_dim(x, 0, width, axis=dim)
        before = lax.ppermute(last, axis, up)
        after = lax.ppermute(initial, axis, down)
        x = jnp.concatenate([before, x, after], axis=dim)
    return x


def raised(block_rows, turned):
    upper_row = block_rows[..., -1:, :]
    upper_row = jnp.where(turned, jnp.flip(upper_row, -1), upper_row)
    return jnp.concatenate([block_rows[..., :-1, :], upper_row], axis=-2)


def settled(block_rows, padded, turned):
    lower_rim = padded[..., :1, :]
    upper_rim = padded[..., -1:, :]
    upper_rim = jnp.where(turned, jnp.flip(upper_rim, -1), upper_rim)
    southern = jnp.concatenate([lower_rim, block_rows[..., :-1, :]], axis=-2)
    northern = jnp.concatenate([block_rows[..., 1:, :], upper_rim], axis=-2)
    return (southern, northern)


def surface_apply(values_in, damping, turned):
    padded = with_halo(raised(values_in, turned), (("face", 0),), 1)
    southern, northern = settled(values_in, padded, turned)
    return (4.0 + damping) * values_in - (
        southern + northern + jnp.roll(values_in, 1, -1) + jnp.roll(values_in, -1, -1)
    )


def stepwise_surface(eta_adjoint, surface_damping, turned):
    surface = jnp.zeros_like(eta_adjoint)
    residual = eta_adjoint
    direction = eta_adjoint
    norm_now = lax.psum(jnp.sum(residual * residual), "face")
    for step in range(ITERS):
        applied = surface_apply(direction, surface_damping, turned)
        step_size = norm_now / lax.psum(jnp.sum(direction * applied), "face")
        surface = surface + step_size * direction
        residual = residual - step_size * applied
        norm_next = lax.psum(jnp.sum(residual * residual), "face")
        direction = residual + norm_next / norm_now * direction
        norm_now = norm_next
    return surface


def flip_lanes(rows):
    width = rows.shape[1]
    back = LANES - 1 - lax.broadcasted_iota(jnp.int32, (SUBLANES, LANES), 1)
    tiles = []
    for start in range(width - LANES, -1, -LANES):
        tiles.append(
            jnp.take_along_axis(
                rows[:, start : start + LANES], back, axis=1, mode="promise_in_bounds"
            )
        )
    return jnp.concatenate(tiles, axis=1)


def chunks_of(levels, size):
    return [(k, min(size, levels - k)) for k in range(0, levels, size)]


def flip_some(rows):
    height, width = rows.shape
    if height < SUBLANES:
        rows = jnp.concatenate([rows, jnp.zeros((SUBLANES - height, width), rows.dtype)], axis=0)
    return flip_lanes(rows)[:height]


def outer_kernel(seam, eta, damping, up, down, own, mark):
    half = SUBLANES // 2
    own[:SUBLANES, :] = eta[...]
    own[SUBLANES:, :] = damping[...]
    down[:half, :] = eta[:half, :]
    down[half:, :] = damping[:half, :]
    up[:half, :] = eta[half:, :]
    up[half:, :] = damping[half:, :]

    @pl.when(seam[0] == 1)
    def _():
        up[...] = flip_lanes(up[...])


def basis_kernel(seam, own_rows, below, above, basis, sums):
    half = SUBLANES // 2
    rows = 2 * SUBLANES
    beyond = above[...]
    beyond = jnp.where(seam[0] == 1, flip_lanes(beyond), beyond)
    width = beyond.shape[1]
    v = jnp.concatenate([below[:half, :], own_rows[:SUBLANES, :], beyond[:half, :]], axis=0)
    d = jnp.concatenate([below[half:, :], own_rows[SUBLANES:, :], beyond[half:, :]], axis=0)
    d = (d + (4.0 - MIDDLE)) * (1.0 / MIDDLE)
    vectors = [v]
    for j in range(ITERS):
        now = vectors[-1]
        near = (
            pltpu.roll(now, 1, 0)
            + pltpu.roll(now, rows - 1, 0)
            + pltpu.roll(now, 1, 1)
            + pltpu.roll(now, width - 1, 1)
        )
        image = d * now - near * (1.0 / MIDDLE)
        vectors.append(image if j == 0 else 2.0 * image - vectors[-2])
    for j in range(ITERS):
        basis[j] = vectors[j]
    row = lax.broadcasted_iota(jnp.int32, (rows, LANES), 0)
    own = (row >= half) & (row < half + SUBLANES)
    parts = []
    for j in range(2 * ITERS):
        product = vectors[j // 2] * vectors[j // 2 + j % 2]
        total = product[:, :LANES]
        for start in range(LANES, width, LANES):
            total = total + product[:, start : start + LANES]
        parts.append(jnp.sum(jnp.where(own, total, 0.0), axis=0, keepdims=True))
    tile = jnp.concatenate(parts, axis=0)
    for i in range(sums.shape[0]):
        sums[i] = tile


def coefficients(moments):
    def dot(a, b):
        total = None
        for i, x in enumerate(a):
            for j, y in enumerate(b):
                term = x * y * (moments[i + j] + moments[abs(i - j)])
                total = term if total is None else total + term
        return 0.5 * total

    def image(p):
        q = [MIDDLE * x for x in p] + [jnp.zeros_like(p[0])]
        for i, x in enumerate(p):
            if i == 0:
                q[1] = q[1] + MIDDLE * x
            else:
                q[i + 1] = q[i + 1] + (0.5 * MIDDLE) * x
                q[i - 1] = q[i - 1] + (0.5 * MIDDLE) * x
        return q

    def size(p):
        return functools.reduce(lambda a, b: a + b, [jnp.abs(x) for x in p])

    def plus(a, b):
        return [x + y for x, y in zip(a, b)] + list(a[len(b) :]) + list(b[len(a) :])

    norm_first = moments[0]
    p = [jnp.ones_like(norm_first)]
    r = p
    norm_now = norm_first
    s = []
    sound = norm_first > 0.0
    for step in range(ITERS):
        q = image(p)
        curve = dot(p, q)
        sound = sound & (curve * LOSS >= size(p) * size(q) * norm_first)
        rate = norm_now / curve
        s = plus(s, [rate * x for x in p])
        if step < ITERS - 1:
            r = plus(r, [-rate * x for x in q])
            norm_next = dot(r, r)
            sound = sound & (norm_next * LOSS >= size(r) * size(r) * norm_first)
            ratio = norm_next / norm_now
            p = plus(r, [ratio * x for x in p])
            norm_now = norm_next
    return s, sound


def outer_lines(seam, fields, edges, up, down):
    turned = seam[0] == 1
    for k in range(0, up.shape[1], SUBLANES):
        at = slice(k, k + SUBLANES)
        top = edges[0, at, :] + fields[SUBLANES - 1 : SUBLANES, :] * edges[1, at, :]
        up[0, at, :] = jnp.where(turned, flip_lanes(top), top)
        down[0, at, :] = edges[2, at, :] + fields[:1, :] * edges[3, at, :]
        up[1, at, :] = edges[4, at, :]
        down[1, at, :] = edges[5, at, :]


def surface_kernel(seam, sums, basis, edges, surface, up, down, sound):
    half = SUBLANES // 2
    parts = [sums[i] for i in range(sums.shape[0])]
    while len(parts) > 1:
        pairs = [a + b for a, b in zip(parts[::2], parts[1::2])]
        parts = pairs + parts[len(parts) - len(parts) % 2 :]
    total = jnp.sum(parts[0], axis=1, keepdims=True)
    raw = [total[j : j + 1, :] for j in range(2 * ITERS)]
    moments = raw[:2]
    for j in range(2, 2 * ITERS):
        moments.append(2.0 * raw[j] - raw[j % 2])
    s, good = coefficients(moments)
    value = s[0] * basis[0]
    for j in range(1, ITERS):
        value = value + s[j] * basis[j]
    surface[...] = value[half : half + SUBLANES, :]
    sound[0] = jnp.where(good, 1, 0)[0, 0]
    outer_lines(seam, surface, edges, up, down)


CHUNK = 10


def column_kernel(
    seam, thickness_from, tracer, mixing, velocity_y, wet, after, solved, edges,
    thickness, depth_at, tracer_at, mixing_at, velocity_at, ratio_at, sems,
):
    levels = tracer.shape[1]
    chunks = chunks_of(levels, CHUNK)
    few = [
        pltpu.make_async_copy(thickness_from, thickness, sems.at[2, 1]),
        pltpu.make_async_copy(wet, depth_at, sems.at[2, 2]),
    ]
    loads = []
    for i, (k, n) in enumerate(chunks):
        m = min(n, levels - 1 - k)
        loads.append((
            pltpu.make_async_copy(
                mixing.at[pl.ds(k, m)], mixing_at.at[pl.ds(k, m)], sems.at[1, i]
            ),
            pltpu.make_async_copy(
                tracer.at[:, pl.ds(k, n)], tracer_at.at[:, pl.ds(k, n)], sems.at[0, i]
            ),
        ))
    velocity_load = pltpu.make_async_copy(velocity_y, velocity_at, sems.at[2, 0])
    for pair in [few] + loads:
        pair[0].start()
        pair[1].start()
    velocity_load.start()

    few[0].wait()
    few[1].wait()
    depth = depth_at[...]
    zero = jnp.zeros(depth.shape, jnp.float32)

    def forward(k, carry):
        c_before, g_before, y0, y1, y2 = carry
        th = thickness[k]
        c = jnp.where(k + 1 < depth, mixing_at[jnp.minimum(k, levels - 2)], 0.0)
        inverse = 1.0 / (th + c + c_before * (1.0 - g_before))
        g = c * inverse
        y0 = (tracer_at[0, k] + c_before * y0) * inverse
        y1 = (tracer_at[1, k] + c_before * y1) * inverse
        y2 = (jnp.where(k < depth, th, 0.0) + c_before * y2) * inverse
        ratio_at[k] = g
        solved[0, k] = y0
        solved[1, k] = y1
        solved[2, k] = y2
        return c, g, y0, y1, y2

    carry = (zero,) * 5
    for i, (k, n) in enumerate(chunks):
        loads[i][0].wait()
        loads[i][1].wait()
        carry = lax.fori_loop(k, k + n, forward, carry, unroll=5)

    carry = (zero,) * 3
    for i, (k, n) in reversed(list(enumerate(chunks))):

        def backward(j, carry, last=k + n - 1):
            level = last - j
            th = thickness[level]
            g = ratio_at[level]
            after = []
            for t in range(3):
                u = solved[t, level] + g * carry[t]
                solved[t, level] = th * u
                after.append(u)
            return tuple(after)

        carry = lax.fori_loop(0, n, backward, carry, unroll=5)

    velocity_load.wait()
    turned = seam[0] == 1
    for k, n in chunks_of(levels, SUBLANES):
        at = slice(k, k + n)
        to_up = diffusion - advection * velocity_at[pl.ds(k, n), SUBLANES - 1, :]
        to_down = diffusion + advection * velocity_at[pl.ds(k, n), 0, :]
        top = solved[1, pl.ds(k, n), SUBLANES - 1, :] * to_up
        edges[4, at, :] = jnp.where(turned, flip_some(top), top)
        edges[5, at, :] = solved[1, pl.ds(k, n), 0, :] * to_down
        for t in range(2):
            edges[t, at, :] = solved[2 * t, pl.ds(k, n), SUBLANES - 1, :] * to_up
            edges[2 + t, at, :] = solved[2 * t, pl.ds(k, n), 0, :] * to_down


def inside_kernel(solved, velocity_x, velocity_y, wet, surface, result):
    levels = velocity_x.shape[0]
    width = wet.shape[1]
    depth = wet[...]
    s = surface[...]
    row = lax.broadcasted_iota(jnp.int32, depth.shape, 0)
    is_south = row == 0
    is_north = row == SUBLANES - 1

    def level(k, _):
        flow_x = advection * velocity_x[k]
        flow_y = advection * velocity_y[k]
        to_west = diffusion + flow_x
        to_east = diffusion - flow_x
        to_south = jnp.where(is_south, 0.0, diffusion + flow_y)
        to_north = jnp.where(is_north, 0.0, diffusion - flow_y)
        is_wet = k < depth
        for t in range(2):
            x = solved[t, k]
            if t == 0:
                x = x + s * solved[2, k]
            eastern = pltpu.roll(x * to_west, width - 1, 1)
            western = pltpu.roll(x * to_east, 1, 1)
            northern = pltpu.roll(x * to_south, SUBLANES - 1, 0)
            southern = pltpu.roll(x * to_north, 1, 0)
            value = (1.0 - 4.0 * diffusion) * x + ((eastern + western) + (northern + southern))
            result[t, k] = jnp.where(is_wet, value, 0.0)
        return 0

    lax.fori_loop(0, levels, level, 0, unroll=5)


def rim_kernel(seam, inside, wet, below, above, result, result_at, out_sems):
    levels = inside.shape[1]
    width = wet.shape[1]
    turned = seam[0] == 1
    depth_south = wet[:1, :]
    depth_north = wet[SUBLANES - 1 :, :]
    stores = []
    for i, (k, n) in enumerate(chunks_of(levels, SUBLANES)):
        at = pl.ds(k, n)
        index = k + lax.broadcasted_iota(jnp.int32, (n, width), 0)
        result_at[:, at] = inside[:, at]
        for t in range(2):
            south = below[t, k : k + n, :]
            north = above[t, k : k + n, :]
            north = jnp.where(turned, flip_some(north), north)
            result_at[t, at, 0, :] += jnp.where(index < depth_south, south, 0.0)
            result_at[t, at, SUBLANES - 1, :] += jnp.where(index < depth_north, north, 0.0)
        stores.append(pltpu.make_async_copy(result_at.at[:, at], result.at[:, at], out_sems.at[i]))
        stores[-1].start()
    for store in stores:
        store.wait()


def shards(
    tracer_adjoint,
    eta_adjoint,
    velocity_x,
    velocity_y,
    mixing,
    thickness,
    surface_damping,
    wet_levels,
    seam_codes,
):
    tracers, levels, rows, width = tracer_adjoint.shape
    f32 = jnp.float32
    count = lax.axis_size("face")
    upward = [(i, (i + 1) % count) for i in range(count)]
    downward = [(j, i) for i, j in upward]
    tile = jax.ShapeDtypeStruct((rows, width), f32)
    ext = pltpu.VMEM((ITERS, 2 * rows, width), f32)
    lines = -(-levels // SUBLANES) * SUBLANES
    line = jax.ShapeDtypeStruct((tracers, lines, width), f32)

    up, down, own, mark = pl.pallas_call(
        outer_kernel,
        out_shape=(
            tile,
            tile,
            pltpu.VMEM((2 * rows, width), f32),
            pltpu.HBM((SUBLANES, LANES), f32),
        ),
        in_specs=[SMEM, VMEM, VMEM],
        out_specs=(VMEM, VMEM, VMEM, HBM),
        name="outer_rows",
    )(seam_codes, eta_adjoint, surface_damping)
    below = lax.ppermute(up, "face", upward)
    above = lax.ppermute(down, "face", downward)

    cube = pltpu.VMEM((levels, rows, width), f32)
    chunks = len(chunks_of(levels, CHUNK))
    parts = len(chunks_of(levels, SUBLANES))
    inputs = [in_hbm(x) for x in (thickness, tracer_adjoint, mixing, velocity_y, wet_levels)]

    def columns_after(mark, place):
        return pl.pallas_call(
            column_kernel,
            out_shape=(
                place((3, levels, rows, width), f32),
                place((6, lines, width), f32),
            ),
            in_specs=[SMEM] + [HBM] * 6,
            out_specs=(VMEM, VMEM),
            scratch_shapes=[
                pltpu.SMEM((levels,), f32),
                pltpu.VMEM((rows, width), jnp.int32),
                pltpu.VMEM((tracers, levels, rows, width), f32),
                cube,
                cube,
                cube,
                pltpu.SemaphoreType.DMA((3, max(chunks, 3))),
            ],
            compiler_params=PARAMS,
            cost_estimate=pl.CostEstimate(
                flops=40000000, bytes_accessed=13000000, transcendentals=0
            ),
            name="columns",
        )(seam_codes, *inputs, mark)

    def inside_of(solved, surface, place):
        return pl.pallas_call(
            inside_kernel,
            out_shape=place((tracers, levels, rows, width), f32),
            in_specs=[VMEM] * 5,
            out_specs=VMEM,
            compiler_params=PARAMS,
            cost_estimate=pl.CostEstimate(flops=1000, bytes_accessed=1000, transcendentals=0),
            name="inside",
        )(solved, velocity_x, velocity_y, wet_levels, surface)

    def with_rims(inside, *beyond):
        return pl.pallas_call(
            rim_kernel,
            out_shape=pltpu.HBM((tracers, levels, rows, width), f32),
            in_specs=[SMEM] + [VMEM] * 4,
            out_specs=HBM,
            scratch_shapes=[
                pltpu.VMEM((tracers, levels, rows, width), f32),
                pltpu.SemaphoreType.DMA((parts,)),
            ],
            compiler_params=PARAMS,
            name="rims",
        )(seam_codes, inside, wet_levels, *beyond)

    def across(up, down):
        return lax.ppermute(up, "face", upward), lax.ppermute(down, "face", downward)

    basis, sums = pl.pallas_call(
        basis_kernel,
        out_shape=(
            ext,
            jax.ShapeDtypeStruct((count, SUBLANES, LANES), f32),
        ),
        in_specs=[SMEM] + [VMEM] * 3,
        out_specs=(VMEM, VMEM),
        compiler_params=PARAMS,
        name="surface_basis",
    )(seam_codes, own, below, above)
    solved, edges = columns_after(in_hbm(mark), pltpu.VMEM)
    sums = lax.all_to_all(sums, "face", 0, 0)
    surface, up, down, sound = pl.pallas_call(
        surface_kernel,
        out_shape=(tile, line, line, jax.ShapeDtypeStruct((1,), jnp.int32)),
        in_specs=[SMEM, VMEM, VMEM, VMEM],
        out_specs=(VMEM, VMEM, VMEM, SMEM),
        compiler_params=PARAMS,
        name="surface",
    )(seam_codes, sums, basis, edges)
    below, above = across(up, down)
    inside = inside_of(solved, surface, pltpu.VMEM)

    def by_moments(surface, inside, below, above):
        return with_rims(inside, below, above), surface

    def by_steps(surface, inside, below, above):
        surface = stepwise_surface(eta_adjoint, surface_damping, seam_codes[0] == 1)
        solved, edges = columns_after(in_hbm(mark), jax.ShapeDtypeStruct)
        up, down = pl.pallas_call(
            outer_lines,
            out_shape=(line, line),
            in_specs=[SMEM, VMEM, VMEM],
            out_specs=(VMEM, VMEM),
            compiler_params=PARAMS,
            name="outer_lines",
        )(seam_codes, surface, edges)
        inside = inside_of(solved, surface, jax.ShapeDtypeStruct)
        return with_rims(inside, *across(up, down)), surface

    return lax.cond(sound[0] == 1, by_moments, by_steps, surface, inside, below, above)


def solution(mesh):
    placed = (
        P(None, None, "face", "ens"),
        P("face", "ens"),
        P(None, "face", "ens"),
        P(None, "face", "ens"),
        P(None, "face", "ens"),
        P(),
        P("face", None),
        P("face", None),
        P("face"),
    )
    return jax.shard_map(
        shards,
        mesh=mesh,
        in_specs=placed,
        out_specs=(P(None, None, "face", "ens"), P("face", "ens")),
        check_vma=False,
    )
```

```python
import functools
import jax
import jax.numpy as jnp
from jax import lax
from jax.experimental import pallas as pl
from jax.experimental.pallas import tpu as pltpu
from jax.sharding import PartitionSpec as P

ITERS = 4
LANES = 128
SUBLANES = 8
diffusion = 0.1
advection = 0.5

MIDDLE = 4.1
LOSS = 1000.0

SMEM = pl.BlockSpec(memory_space=pltpu.SMEM)
VMEM = pl.BlockSpec(memory_space=pltpu.VMEM)
HBM = pl.BlockSpec(memory_space=pltpu.HBM)
PARAMS = pltpu.CompilerParams(vmem_limit_bytes=24 * 2**20)


def in_hbm(x):
    return pltpu.with_memory_space_constraint(x, pltpu.HBM)


def with_halo(x, sides, width):
    for axis, dim in sides:
        count, length = (lax.axis_size(axis), x.shape[dim])
        up = [(i, (i + 1) % count) for i in range(count)]
        down = [(j, i) for i, j in up]
        last = lax.slice_in_dim(x, length - width, length, axis=dim)
        initial = lax.slice_in_dim(x, 0, width, axis=dim)
        before = lax.ppermute(last, axis, up)
        after = lax.ppermute(initial, axis, down)
        x = jnp.concatenate([before, x, after], axis=dim)
    return x


def raised(block_rows, turned):
    upper_row = block_rows[..., -1:, :]
    upper_row = jnp.where(turned, jnp.flip(upper_row, -1), upper_row)
    return jnp.concatenate([block_rows[..., :-1, :], upper_row], axis=-2)


def settled(block_rows, padded, turned):
    lower_rim = padded[..., :1, :]
    upper_rim = padded[..., -1:, :]
    upper_rim = jnp.where(turned, jnp.flip(upper_rim, -1), upper_rim)
    southern = jnp.concatenate([lower_rim, block_rows[..., :-1, :]], axis=-2)
    northern = jnp.concatenate([block_rows[..., 1:, :], upper_rim], axis=-2)
    return (southern, northern)


def surface_apply(values_in, damping, turned):
    padded = with_halo(raised(values_in, turned), (("face", 0),), 1)
    southern, northern = settled(values_in, padded, turned)
    return (4.0 + damping) * values_in - (
        southern + northern + jnp.roll(values_in, 1, -1) + jnp.roll(values_in, -1, -1)
    )


def stepwise_surface(eta_adjoint, surface_damping, turned):
    surface = jnp.zeros_like(eta_adjoint)
    residual = eta_adjoint
    direction = eta_adjoint
    norm_now = lax.psum(jnp.sum(residual * residual), "face")
    for step in range(ITERS):
        applied = surface_apply(direction, surface_damping, turned)
        step_size = norm_now / lax.psum(jnp.sum(direction * applied), "face")
        surface = surface + step_size * direction
        residual = residual - step_size * applied
        norm_next = lax.psum(jnp.sum(residual * residual), "face")
        direction = residual + norm_next / norm_now * direction
        norm_now = norm_next
    return surface


def flip_lanes(rows):
    width = rows.shape[1]
    back = LANES - 1 - lax.broadcasted_iota(jnp.int32, (SUBLANES, LANES), 1)
    tiles = []
    for start in range(width - LANES, -1, -LANES):
        tiles.append(
            jnp.take_along_axis(
                rows[:, start : start + LANES], back, axis=1, mode="promise_in_bounds"
            )
        )
    return jnp.concatenate(tiles, axis=1)


def chunks_of(levels, size):
    return [(k, min(size, levels - k)) for k in range(0, levels, size)]


def flip_some(rows):
    height, width = rows.shape
    if height < SUBLANES:
        rows = jnp.concatenate([rows, jnp.zeros((SUBLANES - height, width), rows.dtype)], axis=0)
    return flip_lanes(rows)[:height]


def outer_kernel(seam, eta, damping, up, down, own, mark):
    half = SUBLANES // 2
    own[:SUBLANES, :] = eta[...]
    own[SUBLANES:, :] = damping[...]
    down[:half, :] = eta[:half, :]
    down[half:, :] = damping[:half, :]
    up[:half, :] = eta[half:, :]
    up[half:, :] = damping[half:, :]

    @pl.when(seam[0] == 1)
    def _():
        up[...] = flip_lanes(up[...])


def basis_kernel(seam, own_rows, below, above, basis, sums):
    half = SUBLANES // 2
    rows = 2 * SUBLANES
    beyond = above[...]
    beyond = jnp.where(seam[0] == 1, flip_lanes(beyond), beyond)
    width = beyond.shape[1]
    v = jnp.concatenate([below[:half, :], own_rows[:SUBLANES, :], beyond[:half, :]], axis=0)
    d = jnp.concatenate([below[half:, :], own_rows[SUBLANES:, :], beyond[half:, :]], axis=0)
    d = (d + (4.0 - MIDDLE)) * (1.0 / MIDDLE)
    vectors = [v]
    for j in range(ITERS):
        now = vectors[-1]
        near = (
            pltpu.roll(now, 1, 0)
            + pltpu.roll(now, rows - 1, 0)
            + pltpu.roll(now, 1, 1)
            + pltpu.roll(now, width - 1, 1)
        )
        image = d * now - near * (1.0 / MIDDLE)
        vectors.append(image if j == 0 else 2.0 * image - vectors[-2])
    for j in range(ITERS):
        basis[j] = vectors[j]
    row = lax.broadcasted_iota(jnp.int32, (rows, LANES), 0)
    own = (row >= half) & (row < half + SUBLANES)
    parts = []
    for j in range(2 * ITERS):
        product = vectors[j // 2] * vectors[j // 2 + j % 2]
        total = product[:, :LANES]
        for start in range(LANES, width, LANES):
            total = total + product[:, start : start + LANES]
        parts.append(jnp.sum(jnp.where(own, total, 0.0), axis=0, keepdims=True))
    tile = jnp.sum(jnp.concatenate(parts, axis=0), axis=1, keepdims=True)
    shape = (2 * ITERS, LANES)
    place = lax.broadcasted_iota(jnp.int32, shape, 0)
    own_lane = place == lax.broadcasted_iota(jnp.int32, shape, 1)
    tile = jnp.sum(jnp.where(own_lane, tile, 0.0), axis=0, keepdims=True)
    for i in range(sums.shape[0]):
        sums[i] = tile


def coefficients(moments):
    def dot(a, b):
        total = None
        for i, x in enumerate(a):
            for j, y in enumerate(b):
                term = x * y * (moments[i + j] + moments[abs(i - j)])
                total = term if total is None else total + term
        return 0.5 * total

    def image(p):
        q = [MIDDLE * x for x in p] + [jnp.zeros_like(p[0])]
        for i, x in enumerate(p):
            if i == 0:
                q[1] = q[1] + MIDDLE * x
            else:
                q[i + 1] = q[i + 1] + (0.5 * MIDDLE) * x
                q[i - 1] = q[i - 1] + (0.5 * MIDDLE) * x
        return q

    def size(p):
        return functools.reduce(lambda a, b: a + b, [jnp.abs(x) for x in p])

    def plus(a, b):
        return [x + y for x, y in zip(a, b)] + list(a[len(b) :]) + list(b[len(a) :])

    norm_first = moments[0]
    p = [jnp.ones_like(norm_first)]
    r = p
    norm_now = norm_first
    s = []
    sound = norm_first > 0.0
    for step in range(ITERS):
        q = image(p)
        curve = dot(p, q)
        sound = sound & (curve * LOSS >= size(p) * size(q) * norm_first)
        rate = norm_now / curve
        s = plus(s, [rate * x for x in p])
        if step < ITERS - 1:
            r = plus(r, [-rate * x for x in q])
            norm_next = dot(r, r)
            sound = sound & (norm_next * LOSS >= size(r) * size(r) * norm_first)
            ratio = norm_next / norm_now
            p = plus(r, [ratio * x for x in p])
            norm_now = norm_next
    return s, sound


def outer_lines(seam, fields, edges, up, down):
    turned = seam[0] == 1
    for k in range(0, up.shape[0], SUBLANES):
        at = slice(k, k + SUBLANES)
        top = edges[0, at, :] + fields[SUBLANES - 1 : SUBLANES, :] * edges[1, at, :]
        up[at, :] = jnp.where(turned, flip_lanes(top), top)
        down[at, :] = edges[2, at, :] + fields[:1, :] * edges[3, at, :]


def surface_kernel(seam, sums, basis, edges, surface, up, down, sound):
    half = SUBLANES // 2
    parts = [sums[i] for i in range(sums.shape[0])]
    while len(parts) > 1:
        pairs = [a + b for a, b in zip(parts[::2], parts[1::2])]
        parts = pairs + parts[len(parts) - len(parts) % 2 :]
    raw = [parts[0][:, j : j + 1] for j in range(2 * ITERS)]
    moments = raw[:2]
    for j in range(2, 2 * ITERS):
        moments.append(2.0 * raw[j] - raw[j % 2])
    s, good = coefficients(moments)
    value = s[0] * basis[0]
    for j in range(1, ITERS):
        value = value + s[j] * basis[j]
    surface[...] = value[half : half + SUBLANES, :]
    sound[0] = jnp.where(good, 1, 0)[0, 0]
    outer_lines(seam, surface, edges, up, down)


CHUNK = 10


def column_kernel(
    seam, thickness_from, tracer, mixing, velocity_y, wet, after, solved, up, down, edges,
    thickness, depth_at, tracer_at, mixing_at, velocity_at, ratio_at, sems,
):
    levels = tracer.shape[1]
    chunks = chunks_of(levels, CHUNK)
    few = [
        pltpu.make_async_copy(thickness_from, thickness, sems.at[2, 1]),
        pltpu.make_async_copy(wet, depth_at, sems.at[2, 2]),
    ]
    loads = []
    for i, (k, n) in enumerate(chunks):
        m = min(n, levels - 1 - k)
        loads.append((
            pltpu.make_async_copy(
                mixing.at[pl.ds(k, m)], mixing_at.at[pl.ds(k, m)], sems.at[1, i]
            ),
            pltpu.make_async_copy(
                tracer.at[:, pl.ds(k, n)], tracer_at.at[:, pl.ds(k, n)], sems.at[0, i]
            ),
        ))
    velocity_load = pltpu.make_async_copy(velocity_y, velocity_at, sems.at[2, 0])
    for pair in [few] + loads:
        pair[0].start()
        pair[1].start()
    velocity_load.start()

    few[0].wait()
    few[1].wait()
    depth = depth_at[...]
    zero = jnp.zeros(depth.shape, jnp.float32)

    def forward(k, carry):
        c_before, g_before, y0, y1, y2 = carry
        th = thickness[k]
        c = jnp.where(k + 1 < depth, mixing_at[jnp.minimum(k, levels - 2)], 0.0)
        inverse = 1.0 / (th + c + c_before * (1.0 - g_before))
        g = c * inverse
        y0 = (tracer_at[0, k] + c_before * y0) * inverse
        y1 = (tracer_at[1, k] + c_before * y1) * inverse
        y2 = (jnp.where(k < depth, th, 0.0) + c_before * y2) * inverse
        ratio_at[k] = g
        solved[0, k] = y0
        solved[1, k] = y1
        solved[2, k] = y2
        return c, g, y0, y1, y2

    carry = (zero,) * 5
    for i, (k, n) in enumerate(chunks):
        loads[i][0].wait()
        loads[i][1].wait()
        carry = lax.fori_loop(k, k + n, forward, carry, unroll=5)

    carry = (zero,) * 3
    for i, (k, n) in reversed(list(enumerate(chunks))):

        def backward(j, carry, last=k + n - 1):
            level = last - j
            th = thickness[level]
            g = ratio_at[level]
            after = []
            for t in range(3):
                u = solved[t, level] + g * carry[t]
                solved[t, level] = th * u
                after.append(u)
            return tuple(after)

        carry = lax.fori_loop(0, n, backward, carry, unroll=5)

    velocity_load.wait()
    turned = seam[0] == 1
    for k, n in chunks_of(levels, SUBLANES):
        at = slice(k, k + n)
        to_up = diffusion - advection * velocity_at[pl.ds(k, n), SUBLANES - 1, :]
        to_down = diffusion + advection * velocity_at[pl.ds(k, n), 0, :]
        top = solved[1, pl.ds(k, n), SUBLANES - 1, :] * to_up
        up[at, :] = jnp.where(turned, flip_some(top), top)
        down[at, :] = solved[1, pl.ds(k, n), 0, :] * to_down
        for t in range(2):
            edges[t, at, :] = solved[2 * t, pl.ds(k, n), SUBLANES - 1, :] * to_up
            edges[2 + t, at, :] = solved[2 * t, pl.ds(k, n), 0, :] * to_down


def inside_kernel(solved, velocity_x, velocity_y, wet, surface, result):
    levels = velocity_x.shape[0]
    width = wet.shape[1]
    depth = wet[...]
    s = surface[...]
    row = lax.broadcasted_iota(jnp.int32, depth.shape, 0)
    is_south = row == 0
    is_north = row == SUBLANES - 1

    def level(k, _):
        flow_x = advection * velocity_x[k]
        flow_y = advection * velocity_y[k]
        to_west = diffusion + flow_x
        to_east = diffusion - flow_x
        to_south = jnp.where(is_south, 0.0, diffusion + flow_y)
        to_north = jnp.where(is_north, 0.0, diffusion - flow_y)
        is_wet = k < depth
        for t in range(2):
            x = solved[t, k]
            if t == 0:
                x = x + s * solved[2, k]
            eastern = pltpu.roll(x * to_west, width - 1, 1)
            western = pltpu.roll(x * to_east, 1, 1)
            northern = pltpu.roll(x * to_south, SUBLANES - 1, 0)
            southern = pltpu.roll(x * to_north, 1, 0)
            value = (1.0 - 4.0 * diffusion) * x + ((eastern + western) + (northern + southern))
            result[t, k] = jnp.where(is_wet, value, 0.0)
        return 0

    lax.fori_loop(0, levels, level, 0, unroll=5)


def rim_kernel(seam, inside, wet, south0, north0, south1, north1, result, result_at, out_sems):
    levels = inside.shape[1]
    width = wet.shape[1]
    turned = seam[0] == 1
    depth_south = wet[:1, :]
    depth_north = wet[SUBLANES - 1 :, :]
    stores = []
    for i, (k, n) in enumerate(chunks_of(levels, SUBLANES)):
        at = pl.ds(k, n)
        index = k + lax.broadcasted_iota(jnp.int32, (n, width), 0)
        result_at[:, at] = inside[:, at]
        for t, (south_from, north_from) in enumerate(((south0, north0), (south1, north1))):
            south = south_from[k : k + n, :]
            north = north_from[k : k + n, :]
            north = jnp.where(turned, flip_some(north), north)
            result_at[t, at, 0, :] += jnp.where(index < depth_south, south, 0.0)
            result_at[t, at, SUBLANES - 1, :] += jnp.where(index < depth_north, north, 0.0)
        stores.append(pltpu.make_async_copy(result_at.at[:, at], result.at[:, at], out_sems.at[i]))
        stores[-1].start()
    for store in stores:
        store.wait()


def shards(
    tracer_adjoint,
    eta_adjoint,
    velocity_x,
    velocity_y,
    mixing,
    thickness,
    surface_damping,
    wet_levels,
    seam_codes,
):
    tracers, levels, rows, width = tracer_adjoint.shape
    f32 = jnp.float32
    count = lax.axis_size("face")
    upward = [(i, (i + 1) % count) for i in range(count)]
    downward = [(j, i) for i, j in upward]
    tile = jax.ShapeDtypeStruct((rows, width), f32)
    ext = pltpu.VMEM((ITERS, 2 * rows, width), f32)
    lines = -(-levels // SUBLANES) * SUBLANES
    line = jax.ShapeDtypeStruct((lines, width), f32)

    up, down, own, mark = pl.pallas_call(
        outer_kernel,
        out_shape=(
            tile,
            tile,
            pltpu.VMEM((2 * rows, width), f32),
            pltpu.HBM((SUBLANES, LANES), f32),
        ),
        in_specs=[SMEM, VMEM, VMEM],
        out_specs=(VMEM, VMEM, VMEM, HBM),
        name="outer_rows",
    )(seam_codes, eta_adjoint, surface_damping)
    below = lax.ppermute(up, "face", upward)
    above = lax.ppermute(down, "face", downward)

    cube = pltpu.VMEM((levels, rows, width), f32)
    chunks = len(chunks_of(levels, CHUNK))
    parts = len(chunks_of(levels, SUBLANES))
    inputs = [in_hbm(x) for x in (thickness, tracer_adjoint, mixing, velocity_y, wet_levels)]

    def columns_after(mark, place):
        return pl.pallas_call(
            column_kernel,
            out_shape=(
                place((3, levels, rows, width), f32),
                line,
                line,
                place((4, lines, width), f32),
            ),
            in_specs=[SMEM] + [HBM] * 6,
            out_specs=(VMEM, VMEM, VMEM, VMEM),
            scratch_shapes=[
                pltpu.SMEM((levels,), f32),
                pltpu.VMEM((rows, width), jnp.int32),
                pltpu.VMEM((tracers, levels, rows, width), f32),
                cube,
                cube,
                cube,
                pltpu.SemaphoreType.DMA((3, max(chunks, 3))),
            ],
            compiler_params=PARAMS,
            cost_estimate=pl.CostEstimate(
                flops=40000000, bytes_accessed=13000000, transcendentals=0
            ),
            name="columns",
        )(seam_codes, *inputs, mark)

    def inside_of(solved, surface, place):
        return pl.pallas_call(
            inside_kernel,
            out_shape=place((tracers, levels, rows, width), f32),
            in_specs=[VMEM] * 5,
            out_specs=VMEM,
            compiler_params=PARAMS,
            cost_estimate=pl.CostEstimate(flops=1000, bytes_accessed=1000, transcendentals=0),
            name="inside",
        )(solved, velocity_x, velocity_y, wet_levels, surface)

    def with_rims(inside, *beyond):
        return pl.pallas_call(
            rim_kernel,
            out_shape=pltpu.HBM((tracers, levels, rows, width), f32),
            in_specs=[SMEM] + [VMEM] * 6,
            out_specs=HBM,
            scratch_shapes=[
                pltpu.VMEM((tracers, levels, rows, width), f32),
                pltpu.SemaphoreType.DMA((parts,)),
            ],
            compiler_params=PARAMS,
            name="rims",
        )(seam_codes, inside, wet_levels, *beyond)

    def across(up, down):
        return lax.ppermute(up, "face", upward), lax.ppermute(down, "face", downward)

    basis, sums = pl.pallas_call(
        basis_kernel,
        out_shape=(
            ext,
            jax.ShapeDtypeStruct((count, 1, LANES), f32),
        ),
        in_specs=[SMEM] + [VMEM] * 3,
        out_specs=(VMEM, VMEM),
        compiler_params=PARAMS,
        name="surface_basis",
    )(seam_codes, own, below, above)
    solved, up1, down1, edges = columns_after(in_hbm(mark), pltpu.VMEM)
    sums, up1, down1 = lax.optimization_barrier((sums, up1, down1))
    sums = lax.all_to_all(sums, "face", 0, 0)
    south1, north1 = across(up1, down1)
    sums, south1, north1 = lax.optimization_barrier((sums, south1, north1))

    surface, up0, down0, sound = pl.pallas_call(
        surface_kernel,
        out_shape=(tile, line, line, jax.ShapeDtypeStruct((1,), jnp.int32)),
        in_specs=[SMEM, VMEM, VMEM, VMEM],
        out_specs=(VMEM, VMEM, VMEM, SMEM),
        compiler_params=PARAMS,
        name="surface",
    )(seam_codes, sums, basis, edges)
    south0, north0 = across(up0, down0)
    inside = inside_of(solved, surface, pltpu.VMEM)

    def by_moments(surface, inside, south0, north0, south1, north1):
        return with_rims(inside, south0, north0, south1, north1), surface

    def by_steps(surface, inside, south0, north0, south1, north1):
        surface = stepwise_surface(eta_adjoint, surface_damping, seam_codes[0] == 1)
        solved, up1, down1, edges = columns_after(in_hbm(mark), jax.ShapeDtypeStruct)
        up0, down0 = pl.pallas_call(
            outer_lines,
            out_shape=(line, line),
            in_specs=[SMEM, VMEM, VMEM],
            out_specs=(VMEM, VMEM),
            compiler_params=PARAMS,
            name="outer_lines",
        )(seam_codes, surface, edges)
        inside = inside_of(solved, surface, jax.ShapeDtypeStruct)
        return with_rims(inside, *across(up0, down0), *across(up1, down1)), surface

    return lax.cond(
        sound[0] == 1, by_moments, by_steps, surface, inside, south0, north0, south1, north1
    )


def solution(mesh):
    placed = (
        P(None, None, "face", "ens"),
        P("face", "ens"),
        P(None, "face", "ens"),
        P(None, "face", "ens"),
        P(None, "face", "ens"),
        P(),
        P("face", None),
        P("face", None),
        P("face"),
    )
    return jax.shard_map(
        shards,
        mesh=mesh,
        in_specs=placed,
        out_specs=(P(None, None, "face", "ens"), P("face", "ens")),
        check_vma=False,
    )
```
